128 devices in a mesh: slab: 32 (over z_lo, y, x), col: 4 (over z_hi, core).
Axes of the slice: x: 4, y: 4, z: 4 (z_hi: 2, z_lo: 2; z = z_hi * 2 + z_lo), core: 2. Of those that a mesh axis runs over, the one named last changes fastest.
Arguments:
- hamiltonian_blocks: bfloat16 [512, 9, 128, 128], P('slab'), may hold values from -0.0625 to 0.0625
- block_columns: int32 [512, 9], P('slab'), may hold values from 0 to 511, as said below
- probe: bfloat16 [65536, 2048], P('slab', 'col'), may hold values from -6 to 6
- previous: float32 [65536, 2048], P('slab', 'col'), may hold values from -6 to 6
- current: float32 [65536, 2048], P('slab', 'col'), may hold values from -6 to 6
- orbital_weight: float32 [65536], P('slab'), may hold values from 0.1 to 10
Outputs:
- last_previous: float32 [65536, 2048], P('slab', 'col')
- last_current: float32 [65536, 2048], P('slab', 'col')
- moments: float32 [3, 2048], P(None, 'col')
The draws below stay inside these ranges and needn't reach their ends.
Inputs may be any that keep to these rules, and one draw needn't show every extreme that they name: `block_columns`: the 9 entries of a row are distinct block columns within 5 of the row's own block row, counted cyclically modulo 512; they include the row itself and the block rows 5 before and 5 after it.
All inputs are finite; a program needn't handle non-finite values.
Results may differ from the reference program's by a relative error of at most 0.0024.
Values may be sent and summed in bfloat16 or wider, within the bound.
No kernel may reach another device: no remote copies, remote signals or barrier semaphores. Data moves between devices by JAX's collectives and lax.ppermute only.
A program may use at most 192 MiB of HBM per device.

```python
import math
import jax
import jax.numpy as jnp
from jax import lax

BLK = 128
BAND = 5
NB = 9
TERMS = 3
NBR = 512
NORB = 65536
COLS = 2048


def draw_block_columns(key, part):
    count = 2 * BAND - 2
    scores = jax.random.randint(key, (NBR, count), 0, 1 << 20) * count + jnp.arange(count)[None, :]
    picked = jnp.argsort(scores, axis=1)[:, :NB - 3]
    offsets = jnp.where(picked < BAND - 1, picked - (BAND - 1), picked - BAND + 2)
    fixed_part = jnp.broadcast_to(jnp.array([0, -BAND, BAND], jnp.int32)[None, :], (NBR, 3))
    every = jnp.concatenate([fixed_part, offsets.astype(jnp.int32)], axis=1)
    rowid = jnp.arange(NBR, dtype=jnp.int32)[:, None]
    return ((rowid + every) % NBR).astype(jnp.int32)


def steps_of(own_key, extent, shards, low, largest):
    gain = 1.0
    for dim, shards_of in shards:
        draws = jax.random.uniform(jax.random.fold_in(jax.random.fold_in(own_key, 6), dim), (shards_of,), jnp.float32, low / len(shards), largest / len(shards))
        gain = gain * jnp.repeat(jnp.exp(draws), extent[dim] // shards_of).reshape((-1,) + (1,) * (len(extent) - 1 - dim))
    return gain


def centred(own_key, shape, deviation, most, pieces=(), kind=jnp.bfloat16):
    values = deviation * jax.random.normal(own_key, shape, jnp.float32)
    if pieces:
        values = values * steps_of(own_key, shape, pieces, -0.22, 0.18)
    return jnp.clip(values, -most, most).astype(kind)


def setup_inputs(seed: int = 0) -> dict:
    arg_keys = jax.random.split(jax.random.key(seed), 7)
    return {
        "hamiltonian_blocks": centred(arg_keys[0], (NBR, NB, BLK, BLK), (8 * NB * BLK) ** -0.5, 0.0625, ((0, 32),)),
        "block_columns": draw_block_columns(jax.random.fold_in(arg_keys[6], 71), 0),
        "probe": centred(arg_keys[2], (NORB, COLS), 1.0, 6.0, ((0, 32), (1, 4))),
        "previous": centred(arg_keys[3], (NORB, COLS), 1.0, 6.0, ((0, 32), (1, 4)), jnp.float32),
        "current": centred(arg_keys[4], (NORB, COLS), 1.0, 6.0, ((0, 32), (1, 4)), jnp.float32),
        "orbital_weight": jnp.clip(jnp.exp(math.log(10.0) - 4.6051702 * jax.random.uniform(arg_keys[5], (NORB,), jnp.float32) ** steps_of(arg_keys[5], (NORB,), ((0, 32),), -0.2, 0.2)), 0.1, 10.0),
    }


def reference(hamiltonian_blocks, block_columns, probe, previous, current, orbital_weight):
    total = hamiltonian_blocks.shape[0] * BLK
    weights = orbital_weight[:, None] * probe.astype(jnp.float32) / total
    results = []
    for term in range(TERMS):
        source = current.astype(jnp.bfloat16).reshape(NBR, BLK, -1)

        def one_row(pair):
            blocks, columns = pair
            picked = source[columns]
            return jnp.einsum("sij,sjc->ic", blocks.astype(jnp.float32), picked.astype(jnp.float32))

        product = lax.map(one_row, (hamiltonian_blocks, block_columns)).reshape(total, -1)
        upcoming = 2.0 * product - previous
        results.append(jnp.sum(weights * upcoming, axis=0))
        previous, current = current, upcoming
    return previous, current, jnp.stack(results)
```

```python
import functools
import jax
import jax.numpy as jnp
from jax import lax
from jax.experimental import pallas as pl
from jax.experimental.pallas import tpu as pltpu
from jax.sharding import PartitionSpec as P

BAND = 5
TERMS = 3
CHUNKS = 2
F32 = jnp.float32
BF16 = jnp.bfloat16
VMEM = pl.BlockSpec(memory_space=pltpu.VMEM)
SMEM = pl.BlockSpec(memory_space=pltpu.SMEM)
HBM = pl.BlockSpec(memory_space=pltpu.HBM)


def params(**more):
    return pltpu.CompilerParams(vmem_limit_bytes=12 * 1024 * 1024, **more)


def cost(flops, moved):
    return pl.CostEstimate(flops=flops, bytes_accessed=moved, transcendentals=0)


def edge_kernel(first, cols, rim, current, low, high, held, sems):
    rows = current.shape[0]
    copies = [
        pltpu.make_async_copy(
            current.at[pl.ds(start, rim), pl.ds(first, cols)], held.at[side], sems.at[side]
        )
        for side, start in enumerate((0, rows - rim))
    ]
    for copy in copies:
        copy.start()
    for side, out in enumerate((low, high)):
        copies[side].wait()
        out[...] = held[side].astype(BF16)


def band_kernel(places, blocks, banded):
    rows_blk, slots, width, _ = blocks.shape

    def one_pair(pair, _):
        banded[pair] = jnp.zeros(banded.shape[1:], BF16)
        for half in range(2):
            row = 2 * pair + half
            for slot in range(slots):
                at = pl.multiple_of((places[row, slot] + half) * width, width)
                banded[pair, pl.ds(half * width, width), pl.ds(at, width)] = blocks[row, slot]
        return 0

    lax.fori_loop(0, rows_blk // 2, one_pair, 0)


def fold(x):
    return jnp.sum(x.reshape(-1, 8, x.shape[-1]), axis=0)


def middle_kernel(opening, closing, first, width, rows_blk, *refs):
    refs = list(refs)
    refs.pop(0)
    banded = refs.pop(0)
    weights = refs.pop(0)
    source = [refs.pop(0)] if opening else [refs.pop(0) for _ in range(3)]
    previous = refs.pop(0)
    full_in = None
    if closing is not None:
        finished = refs.pop(0)
        if closing:
            refs.pop(0)
    upcoming, inner, partial = refs.pop(0), refs.pop(0), refs.pop(0)
    if closing is not None:
        out_hbm = refs.pop(0)
    x = refs.pop(0)
    cols = x.shape[1]
    columns = pl.ds(first, cols)
    if closing is not None:
        sem = refs.pop(0)
        copy = pltpu.make_async_copy(finished, out_hbm.at[:, columns], sem)
        copy.start()
    rim = BAND * width
    rows = rows_blk * width
    if opening:
        x[...] = source[0][:, columns].astype(BF16)
    else:
        x[0:rim] = source[0][...]
        x[rim : rows - rim] = source[1][...]
        x[rows - rim : rows] = source[2][...]
    wide = previous.shape[1] != cols
    total = jnp.zeros((8, cols), F32)
    for pair in range(rows_blk // 2):
        start = 2 * pair - BAND
        low, high = max(start, 0), min(start + 2 * BAND + 2, rows_blk)
        product = jnp.dot(
            banded[pair, :, (low - start) * width : (high - start) * width],
            x[low * width : high * width],
            preferred_element_type=F32,
        )
        here = pl.ds(2 * pair * width, 2 * width)
        before = previous[here, columns] if wide else previous[here]
        result = 2.0 * product - before
        upcoming[here] = result
        a = max(2 * pair, BAND)
        b = min(2 * pair + 2, rows_blk - BAND)
        if a < b:
            piece = result[(a - 2 * pair) * width : (b - 2 * pair) * width]
            inner[(a - BAND) * width : (b - BAND) * width] = piece.astype(BF16)
            total = total + fold(piece * weights[a * width : b * width, columns])
    partial[...] = total
    if closing is not None:
        copy.wait()


def rim_parts(rows_blk, width):
    parts = []
    for pair in range(rows_blk // 2):
        start = 2 * pair - BAND
        count = max(-start, 0)
        last = min(2 * pair + 2, BAND)
        if count and 2 * pair < BAND:
            parts.append((pair, 0, last - 2 * pair, 0, count, 0, BAND - count))
    for pair in range(rows_blk // 2):
        start = 2 * pair - BAND
        stop = start + 2 * BAND + 2
        count = max(stop - rows_blk, 0)
        a = max(2 * pair, rows_blk - BAND)
        if count and 2 * pair + 2 > rows_blk - BAND:
            parts.append((pair, a - 2 * pair, 2, rows_blk - start, 2 * BAND + 2, 1, 0))
    return parts


def rim_kernel(final, first, width, rows_blk, *refs):
    refs = list(refs)
    refs.pop(0)
    banded, weights = refs.pop(0), refs.pop(0)
    halos = [refs.pop(0), refs.pop(0)]
    begun, partial = refs.pop(0), refs.pop(0)
    earlier = []
    if final is not None:
        if final:
            refs.pop(0)
            earlier = [refs.pop(0) for _ in range(TERMS * CHUNKS - 1)]
        out_hbm, moments = refs.pop(0), refs.pop(0)
        upcoming, sems = refs.pop(0), refs.pop(0)
        edges = None
    else:
        upcoming = refs.pop(0)
        edges = [refs.pop(0), refs.pop(0)]
        moments = refs.pop(0)
    cols = begun.shape[1]
    columns = pl.ds(first, cols)
    rim = BAND * width
    rows = rows_blk * width
    total = partial[...]
    copies = []
    if final is not None:
        inside = pl.ds(rim, rows - 2 * rim)
        copies.append(pltpu.make_async_copy(begun.at[inside], out_hbm.at[inside, columns], sems.at[2]))
        copies[-1].start()
    parts = rim_parts(rows_blk, width)
    for side in range(2):
        for pair, a, b, left, right, of, halo_at in parts:
            if of != side:
                continue
            count = right - left
            product = jnp.dot(
                banded[pair, a * width : b * width, left * width : right * width],
                halos[side][halo_at * width : (halo_at + count) * width],
                preferred_element_type=F32,
            )
            top = (2 * pair + a) * width
            here = slice(top, top + (b - a) * width)
            result = begun[here] + 2.0 * product
            upcoming[here] = result
            if edges is not None:
                base = 0 if side == 0 else rows - rim
                edges[side][top - base : top - base + (b - a) * width] = result.astype(BF16)
            total = total + fold(result * weights[here, columns])
        if final is not None:
            part = pl.ds(0 if side == 0 else rows - rim, rim)
            copies.append(
                pltpu.make_async_copy(upcoming.at[part], out_hbm.at[part, columns], sems.at[side])
            )
            copies[-1].start()
    if final:
        lanes = 128
        rows_out = []
        for one in [*(ref[...] for ref in earlier), total]:
            one = jnp.sum(one, axis=0, keepdims=True)
            rows_out += [one[:, j * lanes : (j + 1) * lanes] for j in range(cols // lanes)]
        moments[...] = jnp.broadcast_to(jnp.concatenate(rows_out, axis=0)[None], moments.shape)
    else:
        moments[...] = total
    for copy in copies:
        copy.wait()


def sum_kernel(parts, out):
    lanes = parts.shape[2]
    total = jnp.sum(parts[...], axis=0)
    each = out.shape[1] // lanes
    for term in range(out.shape[0]):
        for j in range(each):
            out[term : term + 1, j * lanes : (j + 1) * lanes] = total[term * each + j][None]


def local(hamiltonian_blocks, block_columns, probe, previous, current, orbital_weight):
    rows_blk, slots, width, _ = hamiltonian_blocks.shape
    rows, all_cols = current.shape
    cols = all_cols // CHUNKS
    rim = BAND * width
    slabs = lax.axis_size("slab")
    total_blocks = rows_blk * slabs
    onward = [(i, (i + 1) % slabs) for i in range(slabs)]
    backward = [(target, source) for source, target in onward]

    def exchange(low, high):
        return lax.ppermute(high, "slab", onward), lax.ppermute(low, "slab", backward)

    shape = jax.ShapeDtypeStruct
    edge_shape = shape((rim, cols), BF16)
    full_shape = shape((rows, all_cols), F32)
    chunk_shape = shape((rows, cols), F32)
    part_shape = shape((8, cols), F32)

    halos = []
    for chunk in range(CHUNKS):
        low, high = pl.pallas_call(
            functools.partial(edge_kernel, chunk * cols, cols, rim),
            out_shape=(edge_shape, edge_shape),
            in_specs=[HBM],
            out_specs=(VMEM, VMEM),
            scratch_shapes=[pltpu.VMEM((2, rim, cols), F32), pltpu.SemaphoreType.DMA((2,))],
            compiler_params=params(),
            cost_estimate=cost(0, 6 * 2 * rim * cols),
            name="edges",
        )(current)
        halos.append(exchange(low, high))

    first_row = lax.axis_index("slab") * rows_blk
    own_row = first_row + jnp.arange(rows_blk, dtype=jnp.int32)[:, None]
    places = (block_columns - own_row + BAND + total_blocks) % total_blocks
    pairs = rows_blk // 2
    banded = pl.pallas_call(
        band_kernel,
        out_shape=shape((pairs, 2 * width, (2 * BAND + 2) * width), BF16),
        in_specs=[SMEM, VMEM],
        out_specs=VMEM,
        compiler_params=params(),
        cost_estimate=cost(0, 12 * 1024 * 1024),
        name="band",
    )(places, hamiltonian_blocks)
    weights = orbital_weight[:, None] * probe.astype(F32) / (total_blocks * width)

    flops = 2 * rows * cols * 9 * width

    def middle(token, term, chunk, source, before, finished=None, out=None):
        closing = None if finished is None else out is not None
        args = [token, banded, weights, *source, before]
        specs = [VMEM] * len(args)
        outs = [chunk_shape, shape((rows - 2 * rim, cols), BF16), part_shape]
        out_specs = [VMEM] * 3
        scratch = [pltpu.VMEM((rows, cols), BF16)]
        aliases = {}
        if finished is not None:
            args.append(finished)
            specs.append(VMEM)
            if out is not None:
                aliases = {len(args): 3}
                args.append(out)
                specs.append(HBM)
            outs.append(full_shape)
            out_specs.append(HBM)
            scratch.append(pltpu.SemaphoreType.DMA)
        return pl.pallas_call(
            functools.partial(middle_kernel, term == 0, closing, chunk * cols, width, rows_blk),
            out_shape=tuple(outs),
            in_specs=specs,
            out_specs=tuple(out_specs),
            scratch_shapes=scratch,
            input_output_aliases=aliases,
            compiler_params=params(),
            cost_estimate=cost(flops, 8 * 1024 * 1024),
            name="middle",
        )(*args)

    def rims(token, chunk, halo, begun, partial):
        args = [token, banded, weights, *halo, begun, partial]
        return pl.pallas_call(
            functools.partial(rim_kernel, None, chunk * cols, width, rows_blk),
            out_shape=(chunk_shape, edge_shape, edge_shape, part_shape),
            in_specs=[VMEM] * len(args),
            out_specs=(VMEM,) * 4,
            input_output_aliases={5: 0},
            compiler_params=params(),
            cost_estimate=cost(flops // 5, 2 * 1024 * 1024),
            name="rims",
        )(*args)

    def last_rims(token, chunk, halo, begun, partial, out, earlier):
        args = [token, banded, weights, *halo, begun, partial]
        specs = [VMEM] * len(args)
        aliases = {}
        moments = part_shape
        if out is not None:
            aliases = {len(args): 0}
            args += [out, *earlier]
            specs += [HBM] + [VMEM] * len(earlier)
            moments = shape((slabs, TERMS * all_cols // 128, 128), F32)
        return pl.pallas_call(
            functools.partial(rim_kernel, out is not None, chunk * cols, width, rows_blk),
            out_shape=(full_shape, moments),
            in_specs=specs,
            out_specs=(HBM, VMEM),
            scratch_shapes=[pltpu.VMEM((rows, cols), F32), pltpu.SemaphoreType.DMA((3,))],
            input_output_aliases=aliases,
            compiler_params=params(),
            cost_estimate=cost(flops // 5, 2 * 1024 * 1024),
            name="last_rims",
        )(*args)

    source = [(current,)] * CHUNKS
    before = [previous] * CHUNKS
    ready = [current] * CHUNKS
    begun = [None] * CHUNKS
    last_previous = last_current = None
    sums = []
    token = jnp.zeros((8, cols), F32)
    for chunk in range(CHUNKS):
        begun[chunk] = middle(token, 0, chunk, source[chunk], before[chunk])
        token = begun[chunk][2]
    for term in range(TERMS):
        for chunk in range(CHUNKS):
            start, inner, partial = begun[chunk]
            if term < TERMS - 1:
                upcoming, low, high, token = rims(token, chunk, halos[chunk], start, partial)
                halos[chunk] = exchange(low, high)
                source[chunk] = (low, inner, high)
                before[chunk], ready[chunk] = ready[chunk], upcoming
                sums.append(token)
                if term < TERMS - 2:
                    begun[chunk] = middle(token, term + 1, chunk, source[chunk], before[chunk])
                else:
                    *begun[chunk], last_previous = middle(
                        token, term + 1, chunk, source[chunk], before[chunk], ready[chunk], last_previous
                    )
                token = begun[chunk][2]
            else:
                last_current, token = last_rims(
                    token, chunk, halos[chunk], start, partial, last_current, sums
                )
                sums.append(token)
    gathered = lax.all_to_all(sums[-1], "slab", 0, 0)
    moments = pl.pallas_call(
        sum_kernel,
        out_shape=shape((TERMS, all_cols), F32),
        in_specs=[VMEM],
        out_specs=VMEM,
        compiler_params=params(),
        name="sums",
    )(gathered)
    return last_previous, last_current, moments


def solution(mesh):
    return jax.shard_map(
        local,
        mesh=mesh,
        in_specs=(
            P("slab", None, None, None),
            P("slab", None),
            P("slab", "col"),
            P("slab", "col"),
            P("slab", "col"),
            P("slab"),
        ),
        out_specs=(P("slab", "col"), P("slab", "col"), P(None, "col")),
        check_vma=False,
    )
```

```python
import functools
import jax
import jax.numpy as jnp
from jax import lax
from jax.experimental import pallas as pl
from jax.experimental.pallas import tpu as pltpu
from jax.sharding import PartitionSpec as P

BAND = 5
TERMS = 3
CHUNKS = 2
F32 = jnp.float32
BF16 = jnp.bfloat16
VMEM = pl.BlockSpec(memory_space=pltpu.VMEM)
SMEM = pl.BlockSpec(memory_space=pltpu.SMEM)
HBM = pl.BlockSpec(memory_space=pltpu.HBM)


def params(**more):
    return pltpu.CompilerParams(vmem_limit_bytes=12 * 1024 * 1024, **more)


def cost(flops, moved):
    return pl.CostEstimate(flops=flops, bytes_accessed=moved, transcendentals=0)


def edge_kernel(first, cols, rim, _, current, low, high, held, sems):
    rows = current.shape[0]
    copies = [
        pltpu.make_async_copy(
            current.at[pl.ds(start, rim), pl.ds(first, cols)], held.at[side], sems.at[side]
        )
        for side, start in enumerate((0, rows - rim))
    ]
    for copy in copies:
        copy.start()
    for side, out in enumerate((low, high)):
        copies[side].wait()
        out[...] = held[side].astype(BF16)


def band_kernel(_, places, blocks, banded, held, sems):
    rows_blk, slots, width, _ = blocks.shape

    def fetch(pair):
        two = pl.ds(2 * pair, 2)
        return pltpu.make_async_copy(blocks.at[two], held.at[two], sems.at[pair])

    for pair in range(rows_blk // 2):
        fetch(pair).start()

    def one_pair(pair, _):
        banded[pair] = jnp.zeros(banded.shape[1:], BF16)
        fetch(pair).wait()
        for half in range(2):
            row = 2 * pair + half
            for slot in range(slots):
                at = pl.multiple_of((places[row, slot] + half) * width, width)
                banded[pair, pl.ds(half * width, width), pl.ds(at, width)] = held[row, slot]
        return 0

    lax.fori_loop(0, rows_blk // 2, one_pair, 0)


def weight_kernel(scale, _, orbital, probe, weights):
    lanes = orbital.shape[1]
    for block in range(orbital.shape[0]):
        here = pl.ds(block * lanes, lanes)
        column = jnp.broadcast_to(orbital[block : block + 1, :] * scale, (lanes, lanes)).T
        for j in range(probe.shape[1] // lanes):
            there = pl.ds(j * lanes, lanes)
            weights[here, there] = column * probe[here, there].astype(F32)


def fold(x):
    return jnp.sum(x.reshape(-1, 8, x.shape[-1]), axis=0)


def middle_kernel(sources, first, cols, width, rows_blk, _, banded, weights, *refs):
    source, previous = refs[:sources], refs[sources]
    upcoming, *inner, partial, x = refs[sources + 1 + (first > 0) :]
    columns = pl.ds(first, cols)
    rim = BAND * width
    rows = rows_blk * width
    if sources == 1:
        x[...] = source[0][:, columns].astype(BF16)
    else:
        x[0:rim] = source[0][...]
        x[rim : rows - rim] = source[1][...]
        x[rows - rim : rows] = source[2][...]
    total = jnp.zeros((8, cols), F32)
    for pair in range(rows_blk // 2):
        start = 2 * pair - BAND
        low, high = max(start, 0), min(start + 2 * BAND + 2, rows_blk)
        product = jnp.dot(
            banded[pair, :, (low - start) * width : (high - start) * width],
            x[low * width : high * width],
            preferred_element_type=F32,
        )
        here = pl.ds(2 * pair * width, 2 * width)
        result = 2.0 * product - previous[here, columns]
        upcoming[here, columns] = result
        a = max(2 * pair, BAND)
        b = min(2 * pair + 2, rows_blk - BAND)
        if a < b:
            piece = result[(a - 2 * pair) * width : (b - 2 * pair) * width]
            for out in inner:
                out[(a - BAND) * width : (b - BAND) * width] = piece.astype(BF16)
            total = total + fold(piece * weights[a * width : b * width, columns])
    partial[...] = total


def rim_parts(rows_blk):
    parts = []
    for pair in range(rows_blk // 2):
        start = 2 * pair - BAND
        if 2 * pair < BAND:
            parts.append((0, pair, 0, min(2, BAND - 2 * pair), 0, -start, BAND + start))
    for pair in range(rows_blk // 2):
        start = 2 * pair - BAND
        first = max(2 * pair, rows_blk - BAND)
        if first < 2 * pair + 2:
            parts.append((1, pair, first - 2 * pair, 2, rows_blk - start, 2 * BAND + 2, 0))
    return parts


def rim_kernel(kind, first, cols, width, rows_blk, _, banded, weights, low, high, begun, partial, *refs):
    halos = (low, high)
    earlier = refs[: TERMS * CHUNKS - 1] if kind == "final" else ()
    upcoming, *edges, moments = refs[len(earlier) :]
    columns = pl.ds(first, cols)
    rim = BAND * width
    rows = rows_blk * width
    total = partial[...]
    for side, pair, a, b, left, right, at in rim_parts(rows_blk):
        product = jnp.dot(
            banded[pair, a * width : b * width, left * width : right * width],
            halos[side][at * width : (at + right - left) * width],
            preferred_element_type=F32,
        )
        top = (2 * pair + a) * width
        here = pl.ds(top, (b - a) * width)
        result = begun[here, columns] + 2.0 * product
        upcoming[here, columns] = result
        if edges:
            base = top - (0 if side == 0 else rows - rim)
            edges[side][base : base + (b - a) * width] = result.astype(BF16)
        total = total + fold(result * weights[here, columns])
    if kind == "final":
        lanes = moments.shape[2]
        parts = []
        for one in [*(ref[...] for ref in earlier), total]:
            one = jnp.sum(one, axis=0, keepdims=True)
            parts += [one[:, j * lanes : (j + 1) * lanes] for j in range(cols // lanes)]
        moments[...] = jnp.broadcast_to(jnp.concatenate(parts, axis=0)[None], moments.shape)
    else:
        moments[...] = total


def copies_of(parts, source, target, sems):
    copies = [
        pltpu.make_async_copy(source.at[part], target.at[part], sems.at[i])
        for i, part in enumerate(parts)
    ]
    for copy in copies:
        copy.start()
    return copies


def store_kernel(rim, cols, _, previous, current, out_previous, out_current, done, whole_sem, sems):
    rows, all_cols = current.shape
    held = all_cols - cols
    parts = [
        (pl.ds(0, rows), pl.ds(0, held)),
        (pl.ds(rim, rows - 2 * rim), pl.ds(held, cols)),
    ]
    copies = copies_of(parts, current, out_current, sems)
    copies += copies_of([pl.ds(0, rows)], previous, out_previous, whole_sem)
    done[...] = jnp.zeros(done.shape, F32)
    for copy in copies:
        copy.wait()


def sum_kernel(rim, cols, parts, current, _, out, out_current, sems):
    rows, all_cols = current.shape
    columns = pl.ds(all_cols - cols, cols)
    rims = [(pl.ds(0, rim), columns), (pl.ds(rows - rim, rim), columns)]
    copies = copies_of(rims, current, out_current, sems)
    lanes = parts.shape[2]
    total = jnp.sum(parts[...], axis=0)
    each = out.shape[1] // lanes
    for term in range(out.shape[0]):
        for j in range(each):
            out[term : term + 1, j * lanes : (j + 1) * lanes] = total[term * each + j][None]
    for copy in copies:
        copy.wait()


def in_hbm(x):
    return pltpu.with_memory_space_constraint(x, pltpu.HBM)


def local(hamiltonian_blocks, block_columns, probe, previous, current, orbital_weight):
    rows_blk, slots, width, _ = hamiltonian_blocks.shape
    rows, all_cols = current.shape
    cols = all_cols // CHUNKS
    rim = BAND * width
    slabs = lax.axis_size("slab")
    total_blocks = rows_blk * slabs
    onward = [(i, (i + 1) % slabs) for i in range(slabs)]
    backward = [(target, source) for source, target in onward]
    shape = jax.ShapeDtypeStruct
    edge_shape = shape((rim, cols), BF16)
    full_shape = shape((rows, all_cols), F32)
    part_shape = shape((8, cols), F32)
    flops = 2 * rows * cols * 9 * width

    def exchange(low, high):
        return lax.ppermute(high, "slab", onward), lax.ppermute(low, "slab", backward)

    def edges(token, chunk):
        return pl.pallas_call(
            functools.partial(edge_kernel, chunk * cols, cols, rim),
            out_shape=(edge_shape, edge_shape),
            in_specs=[VMEM, HBM],
            out_specs=(VMEM, VMEM),
            scratch_shapes=[pltpu.VMEM((2, rim, cols), F32), pltpu.SemaphoreType.DMA((2,))],
            compiler_params=params(),
            cost_estimate=cost(0, 6 * 2 * rim * cols),
            name="edges",
        )(token, in_hbm(current))

    def middle(token, term, chunk):
        args = [token, banded, weights, *sources[chunk], terms[term]]
        aliases = {}
        if chunk:
            aliases = {len(args): 0}
            args.append(terms[term + 2])
        outs = (full_shape, shape((rows - 2 * rim, cols), BF16), part_shape)
        if term == TERMS - 1:
            outs = (full_shape, part_shape)
        return pl.pallas_call(
            functools.partial(
                middle_kernel, len(sources[chunk]), chunk * cols, cols, width, rows_blk
            ),
            out_shape=outs,
            in_specs=[VMEM] * len(args),
            out_specs=(VMEM,) * len(outs),
            scratch_shapes=[pltpu.VMEM((rows, cols), BF16)],
            input_output_aliases=aliases,
            compiler_params=params(),
            cost_estimate=cost(flops, 8 * 1024 * 1024),
            name="middle",
        )(*args)

    def rims(token, term, chunk):
        args = [token, banded, weights, *halos[chunk], terms[term + 2], begun[chunk][-1]]
        kind = "inner"
        outs = (full_shape, edge_shape, edge_shape, part_shape)
        if term == TERMS - 1:
            kind = "last"
            outs = (full_shape, part_shape)
            if chunk == CHUNKS - 1:
                kind = "final"
                args += sums
                outs = (full_shape, shape((slabs, TERMS * all_cols // 128, 128), F32))
        return pl.pallas_call(
            functools.partial(rim_kernel, kind, chunk * cols, cols, width, rows_blk),
            out_shape=outs,
            in_specs=[VMEM] * len(args),
            out_specs=(VMEM,) * len(outs),
            input_output_aliases={5: 0},
            compiler_params=params(),
            cost_estimate=cost(flops // 5, 2 * 1024 * 1024),
            name="rims",
        )(*args)

    first_row = lax.axis_index("slab") * rows_blk
    own_row = first_row + jnp.arange(rows_blk, dtype=jnp.int32)[:, None]
    places = (block_columns - own_row + BAND + total_blocks) % total_blocks
    pairs = rows_blk // 2

    halos = [None] * CHUNKS
    opening = edges(jnp.zeros((8, 128), F32), 0)
    halos[0] = exchange(*opening)
    banded = pl.pallas_call(
        band_kernel,
        out_shape=shape((pairs, 2 * width, (2 * BAND + 2) * width), BF16),
        in_specs=[VMEM, SMEM, HBM],
        out_specs=VMEM,
        scratch_shapes=[
            pltpu.VMEM(hamiltonian_blocks.shape, BF16),
            pltpu.SemaphoreType.DMA((pairs,)),
        ],
        compiler_params=params(),
        cost_estimate=cost(0, 12 * 1024 * 1024),
        name="band",
    )(opening[0], places, in_hbm(hamiltonian_blocks))
    token = banded
    for chunk in range(1, CHUNKS):
        opening = edges(token, chunk)
        halos[chunk] = exchange(*opening)
        token = opening[0]
    weights = pl.pallas_call(
        functools.partial(weight_kernel, 1.0 / (total_blocks * width)),
        out_shape=full_shape,
        in_specs=[VMEM] * 3,
        out_specs=VMEM,
        compiler_params=params(),
        cost_estimate=cost(0, 4 * 1024 * 1024),
        name="weights",
    )(token, orbital_weight.reshape(rows_blk, width), probe)

    terms = [previous, current] + [None] * TERMS
    sources = [(current,)] * CHUNKS
    begun = [None] * CHUNKS
    sums = []
    order = [(term, chunk) for term in range(TERMS) for chunk in range(CHUNKS)]

    def begin(token, term, chunk):
        terms[term + 2], *begun[chunk] = middle(token, term, chunk)
        return begun[chunk][-1]

    token = begin(weights, *order[0])
    for step, (term, chunk) in enumerate(order):
        terms[term + 2], *sent, token = rims(token, term, chunk)
        if sent:
            halos[chunk] = exchange(*sent)
            sources[chunk] = (sent[0], begun[chunk][0], sent[1])
        sums.append(token)
        if step + 1 < len(order):
            token = begin(token, *order[step + 1])
        if step + 2 == len(order):
            last_previous, last_current, token = pl.pallas_call(
                functools.partial(store_kernel, rim, cols),
                out_shape=(full_shape, full_shape, shape((8, 128), F32)),
                in_specs=[VMEM] * 3,
                out_specs=(HBM, HBM, VMEM),
                scratch_shapes=[pltpu.SemaphoreType.DMA((1,)), pltpu.SemaphoreType.DMA((2,))],
                compiler_params=params(),
                cost_estimate=cost(0, 16 * 1024 * 1024),
                name="store",
            )(token, terms[-2], terms[-1])
    gathered = lax.all_to_all(sums[-1], "slab", 0, 0)
    moments, last_current = pl.pallas_call(
        functools.partial(sum_kernel, rim, cols),
        out_shape=(shape((TERMS, all_cols), F32), full_shape),
        in_specs=[VMEM, VMEM, HBM],
        out_specs=(VMEM, HBM),
        scratch_shapes=[pltpu.SemaphoreType.DMA((2,))],
        input_output_aliases={2: 1},
        compiler_params=params(),
        name="sums",
    )(gathered, terms[-1], last_current)
    return last_previous, last_current, moments


def solution(mesh):
    return jax.shard_map(
        local,
        mesh=mesh,
        in_specs=(
            P("slab", None, None, None),
            P("slab", None),
            P("slab", "col"),
            P("slab", "col"),
            P("slab", "col"),
            P("slab"),
        ),
        out_specs=(P("slab", "col"), P("slab", "col"), P(None, "col")),
        check_vma=False,
    )
```

```python
import functools
import jax
import jax.numpy as jnp
from jax import lax
from jax.experimental import pallas as pl
from jax.experimental.pallas import tpu as pltpu
from jax.sharding import PartitionSpec as P

BAND = 5
TERMS = 3
CHUNKS = 2
F32 = jnp.float32
BF16 = jnp.bfloat16
VMEM = pl.BlockSpec(memory_space=pltpu.VMEM)
SMEM = pl.BlockSpec(memory_space=pltpu.SMEM)
HBM = pl.BlockSpec(memory_space=pltpu.HBM)


def params(**more):
    return pltpu.CompilerParams(vmem_limit_bytes=12 * 1024 * 1024, **more)


def cost(flops, moved):
    return pl.CostEstimate(flops=flops, bytes_accessed=moved, transcendentals=0)


def put(odd, side, pairs, at, value):
    for parity in range(2):

        @pl.when(odd[0] == parity)
        def _():
            pairs[(side + parity + 1) % 2][at] = value


def pick(odd, side, pairs, at):
    evens, odds = pairs[0][at], pairs[1][at]
    taken = (odd[0] == 1) if side == 0 else (odd[0] == 0)
    return jnp.where(taken, evens, odds)


def edge_kernel(first, cols, rim, odd, _, current, evens, odds, held, sems):
    rows = current.shape[0]
    copies = [
        pltpu.make_async_copy(
            current.at[pl.ds(start, rim), pl.ds(first, cols)], held.at[side], sems.at[side]
        )
        for side, start in enumerate((0, rows - rim))
    ]
    for copy in copies:
        copy.start()
    for side in range(2):
        copies[side].wait()
        put(odd, side, (evens, odds), slice(None), held[side].astype(BF16))


def band_kernel(_, places, blocks, banded, held, sems):
    rows_blk, slots, width, _ = blocks.shape

    def fetch(pair):
        two = pl.ds(2 * pair, 2)
        return pltpu.make_async_copy(blocks.at[two], held.at[two], sems.at[pair])

    for pair in range(rows_blk // 2):
        fetch(pair).start()

    def one_pair(pair, _):
        banded[pair] = jnp.zeros(banded.shape[1:], BF16)
        fetch(pair).wait()
        for half in range(2):
            row = 2 * pair + half
            for slot in range(slots):
                at = pl.multiple_of((places[row, slot] + half) * width, width)
                banded[pair, pl.ds(half * width, width), pl.ds(at, width)] = held[row, slot]
        return 0

    lax.fori_loop(0, rows_blk // 2, one_pair, 0)


def weight_kernel(scale, _, orbital, probe, weights):
    lanes = orbital.shape[1]
    for block in range(orbital.shape[0]):
        here = pl.ds(block * lanes, lanes)
        column = jnp.broadcast_to(orbital[block : block + 1, :] * scale, (lanes, lanes)).T
        for j in range(probe.shape[1] // lanes):
            there = pl.ds(j * lanes, lanes)
            weights[here, there] = column * probe[here, there].astype(F32)


def fold(x):
    return jnp.sum(x.reshape(-1, 8, x.shape[-1]), axis=0)


def middle_kernel(sources, first, cols, width, rows_blk, odd, _, banded, weights, *refs):
    source, previous = refs[:sources], refs[sources]
    upcoming, *inner, partial, x = refs[sources + 1 + (first > 0) :]
    columns = pl.ds(first, cols)
    rim = BAND * width
    rows = rows_blk * width
    if sources == 1:
        x[...] = source[0][:, columns].astype(BF16)
    else:
        evens, inside, odds = source
        x[rim : rows - rim] = inside[...]
        for parity in range(2):

            @pl.when(odd[0] == parity)
            def _():
                x[0:rim] = (odds, evens)[parity][...]
                x[rows - rim : rows] = (evens, odds)[parity][...]

    total = jnp.zeros((8, cols), F32)
    for pair in range(rows_blk // 2):
        start = 2 * pair - BAND
        low, high = max(start, 0), min(start + 2 * BAND + 2, rows_blk)
        product = jnp.dot(
            banded[pair, :, (low - start) * width : (high - start) * width],
            x[low * width : high * width],
            preferred_element_type=F32,
        )
        here = pl.ds(2 * pair * width, 2 * width)
        result = 2.0 * product - previous[here, columns]
        upcoming[here, columns] = result
        a = max(2 * pair, BAND)
        b = min(2 * pair + 2, rows_blk - BAND)
        if a < b:
            piece = result[(a - 2 * pair) * width : (b - 2 * pair) * width]
            for out in inner:
                out[(a - BAND) * width : (b - BAND) * width] = piece.astype(BF16)
            total = total + fold(piece * weights[a * width : b * width, columns])
    partial[...] = total


def rim_parts(rows_blk):
    parts = []
    for pair in range(rows_blk // 2):
        start = 2 * pair - BAND
        if 2 * pair < BAND:
            parts.append((0, pair, 0, min(2, BAND - 2 * pair), 0, -start, BAND + start))
    for pair in range(rows_blk // 2):
        start = 2 * pair - BAND
        first = max(2 * pair, rows_blk - BAND)
        if first < 2 * pair + 2:
            parts.append((1, pair, first - 2 * pair, 2, rows_blk - start, 2 * BAND + 2, 0))
    return parts


def rim_kernel(kind, first, cols, width, rows_blk, odd, _, banded, weights, evens, odds, begun, partial, *refs):
    earlier = refs[: TERMS * CHUNKS - 1] if kind == "final" else ()
    upcoming, *edges, moments = refs[len(earlier) :]
    columns = pl.ds(first, cols)
    rim = BAND * width
    rows = rows_blk * width
    total = partial[...]
    for side, pair, a, b, left, right, at in rim_parts(rows_blk):
        product = jnp.dot(
            banded[pair, a * width : b * width, left * width : right * width],
            pick(odd, side, (evens, odds), slice(at * width, (at + right - left) * width)),
            preferred_element_type=F32,
        )
        top = (2 * pair + a) * width
        here = pl.ds(top, (b - a) * width)
        result = begun[here, columns] + 2.0 * product
        upcoming[here, columns] = result
        if edges:
            base = top - (0 if side == 0 else rows - rim)
            put(odd, side, edges, slice(base, base + (b - a) * width), result.astype(BF16))
        total = total + fold(result * weights[here, columns])
    if kind == "final":
        lanes = moments.shape[2]
        parts = []
        for one in [*(ref[...] for ref in earlier), total]:
            one = jnp.sum(one, axis=0, keepdims=True)
            parts += [one[:, j * lanes : (j + 1) * lanes] for j in range(cols // lanes)]
        moments[...] = jnp.broadcast_to(jnp.concatenate(parts, axis=0)[None], moments.shape)
    else:
        moments[...] = total


def copies_of(parts, source, target, sems):
    copies = [
        pltpu.make_async_copy(source.at[part], target.at[part], sems.at[i])
        for i, part in enumerate(parts)
    ]
    for copy in copies:
        copy.start()
    return copies


def store_kernel(rim, cols, _, previous, current, out_previous, out_current, done, whole_sem, sems):
    rows, all_cols = current.shape
    held = all_cols - cols
    parts = [
        (pl.ds(0, rows), pl.ds(0, held)),
        (pl.ds(rim, rows - 2 * rim), pl.ds(held, cols)),
    ]
    copies = copies_of(parts, current, out_current, sems)
    copies += copies_of([pl.ds(0, rows)], previous, out_previous, whole_sem)
    done[...] = jnp.zeros(done.shape, F32)
    for copy in copies:
        copy.wait()


def sum_kernel(rim, cols, parts, current, _, out, out_current, sems):
    rows, all_cols = current.shape
    columns = pl.ds(all_cols - cols, cols)
    rims = [(pl.ds(0, rim), columns), (pl.ds(rows - rim, rim), columns)]
    copies = copies_of(rims, current, out_current, sems)
    lanes = parts.shape[2]
    total = jnp.sum(parts[...], axis=0)
    each = out.shape[1] // lanes
    for term in range(out.shape[0]):
        for j in range(each):
            out[term : term + 1, j * lanes : (j + 1) * lanes] = total[term * each + j][None]
    for copy in copies:
        copy.wait()


def in_hbm(x):
    return pltpu.with_memory_space_constraint(x, pltpu.HBM)


def local(hamiltonian_blocks, block_columns, probe, previous, current, orbital_weight):
    rows_blk, slots, width, _ = hamiltonian_blocks.shape
    rows, all_cols = current.shape
    cols = all_cols // CHUNKS
    rim = BAND * width
    slabs = lax.axis_size("slab")
    total_blocks = rows_blk * slabs
    odd = lax.axis_index("slab")[None] & 1
    pairs_of = [[(i, i ^ 1) for i in range(slabs)]]
    pairs_of.append([((i + 1) % slabs, (k + 1) % slabs) for i, k in pairs_of[0]])
    shape = jax.ShapeDtypeStruct
    edge_shape = shape((rim, cols), BF16)
    full_shape = shape((rows, all_cols), F32)
    part_shape = shape((8, cols), F32)
    flops = 2 * rows * cols * 9 * width

    def exchange(evens, odds):
        ahead = lax.ppermute(odds, "slab", pairs_of[1])
        return lax.ppermute(evens, "slab", pairs_of[0]), ahead

    def edges(token, chunk):
        return pl.pallas_call(
            functools.partial(edge_kernel, chunk * cols, cols, rim),
            out_shape=(edge_shape, edge_shape),
            in_specs=[SMEM, VMEM, HBM],
            out_specs=(VMEM, VMEM),
            scratch_shapes=[pltpu.VMEM((2, rim, cols), F32), pltpu.SemaphoreType.DMA((2,))],
            compiler_params=params(),
            cost_estimate=cost(0, 6 * 2 * rim * cols),
            name="edges",
        )(odd, token, in_hbm(current))

    def middle(token, term, chunk):
        args = [odd, token, banded, weights, *sources[chunk], terms[term]]
        aliases = {}
        if chunk:
            aliases = {len(args): 0}
            args.append(terms[term + 2])
        outs = (full_shape, shape((rows - 2 * rim, cols), BF16), part_shape)
        if term == TERMS - 1:
            outs = (full_shape, part_shape)
        return pl.pallas_call(
            functools.partial(
                middle_kernel, len(sources[chunk]), chunk * cols, cols, width, rows_blk
            ),
            out_shape=outs,
            in_specs=[SMEM] + [VMEM] * (len(args) - 1),
            out_specs=(VMEM,) * len(outs),
            scratch_shapes=[pltpu.VMEM((rows, cols), BF16)],
            input_output_aliases=aliases,
            compiler_params=params(),
            cost_estimate=cost(flops, 8 * 1024 * 1024),
            name="middle",
        )(*args)

    def rims(token, term, chunk):
        args = [odd, token, banded, weights, *halos[chunk], terms[term + 2], begun[chunk][-1]]
        kind = "inner"
        outs = (full_shape, edge_shape, edge_shape, part_shape)
        if term == TERMS - 1:
            kind = "last"
            outs = (full_shape, part_shape)
            if chunk == CHUNKS - 1:
                kind = "final"
                args += sums
                outs = (full_shape, shape((slabs, TERMS * all_cols // 128, 128), F32))
        return pl.pallas_call(
            functools.partial(rim_kernel, kind, chunk * cols, cols, width, rows_blk),
            out_shape=outs,
            in_specs=[SMEM] + [VMEM] * (len(args) - 1),
            out_specs=(VMEM,) * len(outs),
            input_output_aliases={6: 0},
            compiler_params=params(),
            cost_estimate=cost(flops // 5, 2 * 1024 * 1024),
            name="rims",
        )(*args)

    first_row = lax.axis_index("slab") * rows_blk
    own_row = first_row + jnp.arange(rows_blk, dtype=jnp.int32)[:, None]
    places = (block_columns - own_row + BAND + total_blocks) % total_blocks
    pairs = rows_blk // 2

    halos = [None] * CHUNKS
    opening = edges(jnp.zeros((8, 128), F32), 0)
    halos[0] = exchange(*opening)
    banded = pl.pallas_call(
        band_kernel,
        out_shape=shape((pairs, 2 * width, (2 * BAND + 2) * width), BF16),
        in_specs=[VMEM, SMEM, HBM],
        out_specs=VMEM,
        scratch_shapes=[
            pltpu.VMEM(hamiltonian_blocks.shape, BF16),
            pltpu.SemaphoreType.DMA((pairs,)),
        ],
        compiler_params=params(),
        cost_estimate=cost(0, 12 * 1024 * 1024),
        name="band",
    )(opening[0], places, in_hbm(hamiltonian_blocks))
    token = banded
    for chunk in range(1, CHUNKS):
        opening = edges(token, chunk)
        halos[chunk] = exchange(*opening)
        token = opening[0]
    weights = pl.pallas_call(
        functools.partial(weight_kernel, 1.0 / (total_blocks * width)),
        out_shape=full_shape,
        in_specs=[VMEM] * 3,
        out_specs=VMEM,
        compiler_params=params(),
        cost_estimate=cost(0, 4 * 1024 * 1024),
        name="weights",
    )(token, orbital_weight.reshape(rows_blk, width), probe)

    terms = [previous, current] + [None] * TERMS
    sources = [(current,)] * CHUNKS
    begun = [None] * CHUNKS
    sums = []
    order = [(term, chunk) for term in range(TERMS) for chunk in range(CHUNKS)]

    def begin(token, term, chunk):
        terms[term + 2], *begun[chunk] = middle(token, term, chunk)
        return begun[chunk][-1]

    token = begin(weights, *order[0])
    for step, (term, chunk) in enumerate(order):
        terms[term + 2], *sent, token = rims(token, term, chunk)
        if sent:
            halos[chunk] = exchange(*sent)
            sources[chunk] = (sent[0], begun[chunk][0], sent[1])
        sums.append(token)
        if step + 1 < len(order):
            token = begin(token, *order[step + 1])
        if step + 2 == len(order):
            last_previous, last_current, token = pl.pallas_call(
                functools.partial(store_kernel, rim, cols),
                out_shape=(full_shape, full_shape, shape((8, 128), F32)),
                in_specs=[VMEM] * 3,
                out_specs=(HBM, HBM, VMEM),
                scratch_shapes=[pltpu.SemaphoreType.DMA((1,)), pltpu.SemaphoreType.DMA((2,))],
                compiler_params=params(),
                cost_estimate=cost(0, 16 * 1024 * 1024),
                name="store",
            )(token, terms[-2], terms[-1])
    gathered = lax.all_to_all(sums[-1], "slab", 0, 0)
    moments, last_current = pl.pallas_call(
        functools.partial(sum_kernel, rim, cols),
        out_shape=(shape((TERMS, all_cols), F32), full_shape),
        in_specs=[VMEM, VMEM, HBM],
        out_specs=(VMEM, HBM),
        scratch_shapes=[pltpu.SemaphoreType.DMA((2,))],
        input_output_aliases={2: 1},
        compiler_params=params(),
        name="sums",
    )(gathered, terms[-1], last_current)
    return last_previous, last_current, moments


def solution(mesh):
    return jax.shard_map(
        local,
        mesh=mesh,
        in_specs=(
            P("slab", None, None, None),
            P("slab", None),
            P("slab", "col"),
            P("slab", "col"),
            P("slab", "col"),
            P("slab"),
        ),
        out_specs=(P("slab", "col"), P("slab", "col"), P(None, "col")),
        check_vma=False,
    )
```

```python
import functools
import jax
import jax.numpy as jnp
from jax import lax
from jax.experimental import pallas as pl
from jax.experimental.pallas import tpu as pltpu
from jax.sharding import PartitionSpec as P

BAND = 5
TERMS = 3
CHUNKS = 2
F32 = jnp.float32
BF16 = jnp.bfloat16
VMEM = pl.BlockSpec(memory_space=pltpu.VMEM)
SMEM = pl.BlockSpec(memory_space=pltpu.SMEM)
HBM = pl.BlockSpec(memory_space=pltpu.HBM)


def params(**more):
    return pltpu.CompilerParams(vmem_limit_bytes=12 * 1024 * 1024, **more)


def cost(flops, moved):
    return pl.CostEstimate(flops=flops, bytes_accessed=moved, transcendentals=0)


def hand_out(odd, rims, evens, odds):
    for parity in range(2):

        @pl.when(odd[0] == parity)
        def _():
            evens[...] = rims[1 - parity].astype(BF16)
            odds[...] = rims[parity].astype(BF16)


def pick(odd, side, pairs, at):
    evens, odds = pairs[0][at], pairs[1][at]
    taken = (odd[0] == 1) if side == 0 else (odd[0] == 0)
    return jnp.where(taken, evens, odds)


def fetch_rims(current, first, cols, held, sems):
    rim = held.shape[1]
    rows = current.shape[0]
    piece = rim // sems.shape[1]
    copies = [
        pltpu.make_async_copy(
            current.at[pl.ds(start + i * piece, piece), pl.ds(first, cols)],
            held.at[side, pl.ds(i * piece, piece)],
            sems.at[side, i],
        )
        for side, start in enumerate((0, rows - rim))
        for i in range(sems.shape[1])
    ]
    for copy in copies:
        copy.start()
    return copies


def edge_kernel(first, cols, odd, current, evens, odds, held, sems):
    for copy in fetch_rims(current, first, cols, held, sems):
        copy.wait()
    hand_out(odd, held, evens, odds)


def band_kernel(first, cols, odd, _, places, blocks, current, banded, evens, odds, held, sems, rims, rim_sems):
    rows_blk, slots, width, _ = blocks.shape
    copies = fetch_rims(current, first, cols, rims, rim_sems)

    def fetch(pair):
        two = pl.ds(2 * pair, 2)
        return pltpu.make_async_copy(blocks.at[two], held.at[two], sems.at[pair])

    for pair in range(rows_blk // 2):
        fetch(pair).start()
    for copy in copies:
        copy.wait()
    hand_out(odd, rims, evens, odds)

    def one_pair(pair, _):
        banded[pair] = jnp.zeros(banded.shape[1:], BF16)
        fetch(pair).wait()
        for half in range(2):
            row = 2 * pair + half
            for slot in range(slots):
                at = pl.multiple_of((places[row, slot] + half) * width, width)
                banded[pair, pl.ds(half * width, width), pl.ds(at, width)] = held[row, slot]
        return 0

    lax.fori_loop(0, rows_blk // 2, one_pair, 0)


def weight_kernel(scale, _, orbital, probe, weights):
    lanes = orbital.shape[1]
    for block in range(orbital.shape[0]):
        here = pl.ds(block * lanes, lanes)
        column = jnp.broadcast_to(orbital[block : block + 1, :] * scale, (lanes, lanes)).T
        for j in range(probe.shape[1] // lanes):
            there = pl.ds(j * lanes, lanes)
            weights[here, there] = column * probe[here, there].astype(F32)


def fold(x):
    return jnp.sum(x.reshape(-1, 8, x.shape[-1]), axis=0)


def middle_kernel(sources, first, cols, width, rows_blk, odd, _, banded, weights, *refs):
    source, previous = refs[:sources], refs[sources]
    upcoming, *inner, partial, x = refs[sources + 1 + (first > 0) :]
    columns = pl.ds(first, cols)
    rim = BAND * width
    rows = rows_blk * width
    if sources == 1:
        x[...] = source[0][:, columns].astype(BF16)
    else:
        evens, inside, odds = source
        x[rim : rows - rim] = inside[...]
        for parity in range(2):

            @pl.when(odd[0] == parity)
            def _():
                x[0:rim] = (odds, evens)[parity][...]
                x[rows - rim : rows] = (evens, odds)[parity][...]

    total = jnp.zeros((8, cols), F32)
    for pair in range(rows_blk // 2):
        start = 2 * pair - BAND
        low, high = max(start, 0), min(start + 2 * BAND + 2, rows_blk)
        product = jnp.dot(
            banded[pair, :, (low - start) * width : (high - start) * width],
            x[low * width : high * width],
            preferred_element_type=F32,
        )
        here = pl.ds(2 * pair * width, 2 * width)
        result = 2.0 * product - previous[here, columns]
        upcoming[here, columns] = result
        a = max(2 * pair, BAND)
        b = min(2 * pair + 2, rows_blk - BAND)
        if a < b:
            piece = result[(a - 2 * pair) * width : (b - 2 * pair) * width]
            for out in inner:
                out[(a - BAND) * width : (b - BAND) * width] = piece.astype(BF16)
            total = total + fold(piece * weights[a * width : b * width, columns])
    partial[...] = total


def rim_parts(rows_blk):
    parts = []
    for pair in range(rows_blk // 2):
        start = 2 * pair - BAND
        if 2 * pair < BAND:
            parts.append((0, pair, 0, min(2, BAND - 2 * pair), 0, -start, BAND + start))
    for pair in range(rows_blk // 2):
        start = 2 * pair - BAND
        first = max(2 * pair, rows_blk - BAND)
        if first < 2 * pair + 2:
            parts.append((1, pair, first - 2 * pair, 2, rows_blk - start, 2 * BAND + 2, 0))
    return parts


def rim_kernel(kind, first, cols, width, rows_blk, odd, _, banded, weights, odds, evens, begun, partial, *refs):
    earlier = refs[: TERMS * CHUNKS - 1] if kind == "final" else ()
    upcoming, moments = refs[len(earlier) : len(earlier) + 2]
    sent = refs[len(earlier) + 2 :]
    columns = pl.ds(first, cols)
    rim = BAND * width
    rows = rows_blk * width
    total = partial[...]
    for side, pair, a, b, left, right, at in rim_parts(rows_blk):
        product = jnp.dot(
            banded[pair, a * width : b * width, left * width : right * width],
            pick(odd, side, (evens, odds), slice(at * width, (at + right - left) * width)),
            preferred_element_type=F32,
        )
        top = (2 * pair + a) * width
        here = pl.ds(top, (b - a) * width)
        result = begun[here, columns] + 2.0 * product
        upcoming[here, columns] = result
        if sent:
            base = top - (0 if side == 0 else rows - rim)
            sent[2][side, base : base + (b - a) * width] = result.astype(BF16)
        total = total + fold(result * weights[here, columns])
    if sent:
        hand_out(odd, sent[2], *sent[:2])
    if kind == "final":
        lanes = moments.shape[2]
        parts = []
        for one in [*(ref[...] for ref in earlier), total]:
            one = jnp.sum(one, axis=0, keepdims=True)
            parts += [one[:, j * lanes : (j + 1) * lanes] for j in range(cols // lanes)]
        moments[...] = jnp.broadcast_to(jnp.concatenate(parts, axis=0)[None], moments.shape)
    else:
        moments[...] = total


def copies_of(parts, source, target, sems):
    copies = [
        pltpu.make_async_copy(source.at[part], target.at[part], sems.at[i])
        for i, part in enumerate(parts)
    ]
    for copy in copies:
        copy.start()
    return copies


def store_kernel(rim, cols, _, previous, current, out_previous, out_current, done, whole_sem, sems):
    rows, all_cols = current.shape
    held = all_cols - cols
    parts = [
        (pl.ds(0, rows), pl.ds(0, held)),
        (pl.ds(rim, rows - 2 * rim), pl.ds(held, cols)),
    ]
    copies = copies_of(parts, current, out_current, sems)
    copies += copies_of([pl.ds(0, rows)], previous, out_previous, whole_sem)
    done[...] = jnp.zeros(done.shape, F32)
    for copy in copies:
        copy.wait()


def sum_kernel(rim, cols, parts, current, _, out, out_current, sems):
    rows, all_cols = current.shape
    columns = pl.ds(all_cols - cols, cols)
    rims = [(pl.ds(0, rim), columns), (pl.ds(rows - rim, rim), columns)]
    copies = copies_of(rims, current, out_current, sems)
    lanes = parts.shape[2]
    total = jnp.sum(parts[...], axis=0)
    each = out.shape[1] // lanes
    for term in range(out.shape[0]):
        for j in range(each):
            out[term : term + 1, j * lanes : (j + 1) * lanes] = total[term * each + j][None]
    for copy in copies:
        copy.wait()


def in_hbm(x):
    return pltpu.with_memory_space_constraint(x, pltpu.HBM)


def local(hamiltonian_blocks, block_columns, probe, previous, current, orbital_weight):
    rows_blk, slots, width, _ = hamiltonian_blocks.shape
    rows, all_cols = current.shape
    cols = all_cols // CHUNKS
    rim = BAND * width
    slabs = lax.axis_size("slab")
    total_blocks = rows_blk * slabs
    odd = lax.axis_index("slab")[None] & 1
    pairs_of = [[(i, i ^ 1) for i in range(slabs)]]
    pairs_of.append([((i + 1) % slabs, (k + 1) % slabs) for i, k in pairs_of[0]])
    shape = jax.ShapeDtypeStruct
    edge_shape = shape((rim, cols), BF16)
    full_shape = shape((rows, all_cols), F32)
    part_shape = shape((8, cols), F32)
    flops = 2 * rows * cols * 9 * width

    def exchange(evens, odds):
        ahead = lax.ppermute(odds, "slab", pairs_of[1])
        return ahead, lax.ppermute(evens, "slab", pairs_of[0])

    def middle(token, term, chunk):
        args = [odd, token, banded, weights, *sources[chunk], terms[term]]
        aliases = {}
        if chunk:
            aliases = {len(args): 0}
            args.append(terms[term + 2])
        outs = (full_shape, shape((rows - 2 * rim, cols), BF16), part_shape)
        if term == TERMS - 1:
            outs = (full_shape, part_shape)
        return pl.pallas_call(
            functools.partial(
                middle_kernel, len(sources[chunk]), chunk * cols, cols, width, rows_blk
            ),
            out_shape=outs,
            in_specs=[SMEM] + [VMEM] * (len(args) - 1),
            out_specs=(VMEM,) * len(outs),
            scratch_shapes=[pltpu.VMEM((rows, cols), BF16)],
            input_output_aliases=aliases,
            compiler_params=params(),
            cost_estimate=cost(flops, 8 * 1024 * 1024),
            name="middle",
        )(*args)

    def rims(token, term, chunk):
        args = [odd, token, banded, weights, *halos[chunk], terms[term + 2], begun[chunk][-1]]
        kind = "inner"
        outs = (full_shape, part_shape, edge_shape, edge_shape)
        scratch = [pltpu.VMEM((2, rim, cols), BF16)]
        if term == TERMS - 1:
            kind = "last"
            scratch = []
            outs = (full_shape, part_shape)
            if chunk == CHUNKS - 1:
                kind = "final"
                args += sums
                outs = (full_shape, shape((slabs, TERMS * all_cols // 128, 128), F32))
        return pl.pallas_call(
            functools.partial(rim_kernel, kind, chunk * cols, cols, width, rows_blk),
            out_shape=outs,
            in_specs=[SMEM] + [VMEM] * (len(args) - 1),
            out_specs=(VMEM,) * len(outs),
            scratch_shapes=scratch,
            input_output_aliases={6: 0},
            compiler_params=params(),
            cost_estimate=cost(flops // 5, 2 * 1024 * 1024),
            name="rims",
        )(*args)

    first_row = lax.axis_index("slab") * rows_blk
    own_row = first_row + jnp.arange(rows_blk, dtype=jnp.int32)[:, None]
    places = (block_columns - own_row + BAND + total_blocks) % total_blocks
    pairs = rows_blk // 2

    rim_scratch = [pltpu.VMEM((2, rim, cols), F32), pltpu.SemaphoreType.DMA((2, BAND))]
    opening = pl.pallas_call(
        functools.partial(edge_kernel, 0, cols),
        out_shape=(edge_shape, edge_shape),
        in_specs=[SMEM, HBM],
        out_specs=(VMEM, VMEM),
        scratch_shapes=rim_scratch,
        compiler_params=params(),
        cost_estimate=cost(0, 6 * 2 * rim * cols),
        name="edges",
    )(odd, in_hbm(current))
    halos = [exchange(*opening)]
    banded, *opening = pl.pallas_call(
        functools.partial(band_kernel, cols, cols),
        out_shape=(
            shape((pairs, 2 * width, (2 * BAND + 2) * width), BF16),
            edge_shape,
            edge_shape,
        ),
        in_specs=[SMEM, VMEM, SMEM, HBM, HBM],
        out_specs=(VMEM,) * 3,
        scratch_shapes=[
            pltpu.VMEM(hamiltonian_blocks.shape, BF16),
            pltpu.SemaphoreType.DMA((pairs,)),
            *rim_scratch,
        ],
        compiler_params=params(),
        cost_estimate=cost(0, 12 * 1024 * 1024),
        name="band",
    )(odd, opening[1], places, in_hbm(hamiltonian_blocks), in_hbm(current))
    halos.append(exchange(*opening))
    weights = pl.pallas_call(
        functools.partial(weight_kernel, 1.0 / (total_blocks * width)),
        out_shape=full_shape,
        in_specs=[VMEM] * 3,
        out_specs=VMEM,
        compiler_params=params(),
        cost_estimate=cost(0, 4 * 1024 * 1024),
        name="weights",
    )(opening[1], orbital_weight.reshape(rows_blk, width), probe)

    terms = [previous, current] + [None] * TERMS
    sources = [(current,)] * CHUNKS
    begun = [None] * CHUNKS
    sums = []
    order = [(term, chunk) for term in range(TERMS) for chunk in range(CHUNKS)]

    def begin(token, term, chunk):
        terms[term + 2], *begun[chunk] = middle(token, term, chunk)
        return begun[chunk][-1]

    token = begin(weights, *order[0])
    for step, (term, chunk) in enumerate(order):
        terms[term + 2], token, *sent = rims(token, term, chunk)
        if sent:
            halos[chunk] = exchange(*sent)
            sources[chunk] = (sent[0], begun[chunk][0], sent[1])
        sums.append(token)
        if step + 1 < len(order):
            token = begin(token, *order[step + 1])
        if step + 2 == len(order):
            last_previous, last_current, token = pl.pallas_call(
                functools.partial(store_kernel, rim, cols),
                out_shape=(full_shape, full_shape, shape((8, 128), F32)),
                in_specs=[VMEM] * 3,
                out_specs=(HBM, HBM, VMEM),
                scratch_shapes=[pltpu.SemaphoreType.DMA((1,)), pltpu.SemaphoreType.DMA((2,))],
                compiler_params=params(),
                cost_estimate=cost(0, 16 * 1024 * 1024),
                name="store",
            )(token, terms[-2], terms[-1])
    gathered = lax.all_to_all(sums[-1], "slab", 0, 0)
    moments, last_current = pl.pallas_call(
        functools.partial(sum_kernel, rim, cols),
        out_shape=(shape((TERMS, all_cols), F32), full_shape),
        in_specs=[VMEM, VMEM, HBM],
        out_specs=(VMEM, HBM),
        scratch_shapes=[pltpu.SemaphoreType.DMA((2,))],
        input_output_aliases={2: 1},
        compiler_params=params(),
        name="sums",
    )(gathered, terms[-1], last_current)
    return last_previous, last_current, moments


def solution(mesh):
    return jax.shard_map(
        local,
        mesh=mesh,
        in_specs=(
            P("slab", None, None, None),
            P("slab", None),
            P("slab", "col"),
            P("slab", "col"),
            P("slab", "col"),
            P("slab"),
        ),
        out_specs=(P("slab", "col"), P("slab", "col"), P(None, "col")),
        check_vma=False,
    )
```

```python
import functools
import jax
import jax.numpy as jnp
from jax import lax
from jax.experimental import pallas as pl
from jax.experimental.pallas import tpu as pltpu
from jax.sharding import PartitionSpec as P

BAND = 5
TERMS = 3
CHUNKS = 2
F32 = jnp.float32
BF16 = jnp.bfloat16
VMEM = pl.BlockSpec(memory_space=pltpu.VMEM)
SMEM = pl.BlockSpec(memory_space=pltpu.SMEM)
HBM = pl.BlockSpec(memory_space=pltpu.HBM)


def params(**more):
    return pltpu.CompilerParams(vmem_limit_bytes=12 * 1024 * 1024, **more)


def cost(flops, moved):
    return pl.CostEstimate(flops=flops, bytes_accessed=moved, transcendentals=0)


def hand_out(odd, take, evens, odds):
    for parity in range(2):

        @pl.when(odd[0] == parity)
        def _():
            take((odds, evens) if parity == 0 else (evens, odds))


def pick(odd, side, pairs, at):
    evens, odds = pairs[0][at], pairs[1][at]
    taken = (odd[0] == 1) if side == 0 else (odd[0] == 0)
    return jnp.where(taken, evens, odds)


def fetch_rims(current, first, cols, held, sems):
    rim = held.shape[1]
    rows = current.shape[0]
    piece = rim // sems.shape[1]
    copies = [
        pltpu.make_async_copy(
            current.at[pl.ds(start + i * piece, piece), pl.ds(first, cols)],
            held.at[side, pl.ds(i * piece, piece)],
            sems.at[side, i],
        )
        for side, start in enumerate((0, rows - rim))
        for i in range(sems.shape[1])
    ]
    for copy in copies:
        copy.start()

    def take(targets):
        for k, copy in enumerate(copies):
            side, i = divmod(k, sems.shape[1])
            here = slice(i * piece, (i + 1) * piece)
            copy.wait()
            targets[side][here] = held[side, here].astype(BF16)

    return take


def edge_kernel(first, cols, odd, current, evens, odds, held, sems):
    hand_out(odd, fetch_rims(current, first, cols, held, sems), evens, odds)


def band_kernel(first, cols, odd, _, places, blocks, current, banded, evens, odds, held, sems, rims, rim_sems):
    rows_blk, slots, width, _ = blocks.shape
    take = fetch_rims(current, first, cols, rims, rim_sems)

    def fetch(pair):
        two = pl.ds(2 * pair, 2)
        return pltpu.make_async_copy(blocks.at[two], held.at[two], sems.at[pair])

    for pair in range(rows_blk // 2):
        fetch(pair).start()
    hand_out(odd, take, evens, odds)

    def one_pair(pair, _):
        banded[pair] = jnp.zeros(banded.shape[1:], BF16)
        fetch(pair).wait()
        for half in range(2):
            row = 2 * pair + half
            for slot in range(slots):
                at = pl.multiple_of((places[row, slot] + half) * width, width)
                banded[pair, pl.ds(half * width, width), pl.ds(at, width)] = held[row, slot]
        return 0

    lax.fori_loop(0, rows_blk // 2, one_pair, 0)


def weight_kernel(scale, _, orbital, probe, weights):
    lanes = orbital.shape[1]
    for block in range(orbital.shape[0]):
        here = pl.ds(block * lanes, lanes)
        column = jnp.broadcast_to(orbital[block : block + 1, :] * scale, (lanes, lanes)).T
        for j in range(probe.shape[1] // lanes):
            there = pl.ds(j * lanes, lanes)
            weights[here, there] = column * probe[here, there].astype(F32)


def fold(x):
    return jnp.sum(x.reshape(-1, 8, x.shape[-1]), axis=0)


def middle_kernel(sources, first, cols, width, rows_blk, odd, _, banded, weights, *refs):
    source, previous = refs[:sources], refs[sources]
    upcoming, *inner, partial, x = refs[sources + 1 + (first > 0) :]
    columns = pl.ds(first, cols)
    rim = BAND * width
    rows = rows_blk * width
    if sources == 1:
        x[...] = source[0][:, columns].astype(BF16)
    else:
        evens, inside, odds = source
        x[rim : rows - rim] = inside[...]
        for parity in range(2):

            @pl.when(odd[0] == parity)
            def _():
                x[0:rim] = (odds, evens)[parity][...]
                x[rows - rim : rows] = (evens, odds)[parity][...]

    total = jnp.zeros((8, cols), F32)
    for pair in range(rows_blk // 2):
        start = 2 * pair - BAND
        low, high = max(start, 0), min(start + 2 * BAND + 2, rows_blk)
        product = jnp.dot(
            banded[pair, :, (low - start) * width : (high - start) * width],
            x[low * width : high * width],
            preferred_element_type=F32,
        )
        here = pl.ds(2 * pair * width, 2 * width)
        result = 2.0 * product - previous[here, columns]
        upcoming[here, columns] = result
        a = max(2 * pair, BAND)
        b = min(2 * pair + 2, rows_blk - BAND)
        if a < b:
            piece = result[(a - 2 * pair) * width : (b - 2 * pair) * width]
            for out in inner:
                out[(a - BAND) * width : (b - BAND) * width] = piece.astype(BF16)
            total = total + fold(piece * weights[a * width : b * width, columns])
    partial[...] = total


def rim_parts(rows_blk):
    parts = []
    for pair in range(rows_blk // 2):
        start = 2 * pair - BAND
        first = max(2 * pair, rows_blk - BAND)
        if first < 2 * pair + 2:
            parts.append((1, pair, first - 2 * pair, 2, rows_blk - start, 2 * BAND + 2, 0))
    for pair in range(rows_blk // 2):
        start = 2 * pair - BAND
        if 2 * pair < BAND:
            parts.append((0, pair, 0, min(2, BAND - 2 * pair), 0, -start, BAND + start))
    return parts


def rim_sums(first, cols, width, rows_blk, odd, banded, weights, evens, odds, begun, partial, keep):
    columns = pl.ds(first, cols)
    total = partial[...]
    for part, (side, pair, a, b, left, right, at) in enumerate(rim_parts(rows_blk)):
        product = jnp.dot(
            banded[pair, a * width : b * width, left * width : right * width],
            pick(odd, side, (evens, odds), slice(at * width, (at + right - left) * width)),
            preferred_element_type=F32,
        )
        here = pl.ds((2 * pair + a) * width, (b - a) * width)
        result = begun[here, columns] + 2.0 * product
        keep(part, side, here, columns, result)
        total = total + fold(result * weights[here, columns])
    return total


def rim_kernel(first, cols, width, rows_blk, odd, _, banded, weights, odds_in, evens_in, begun, partial, *refs):
    upcoming, moments, evens, odds, rims = refs
    rim = rims.shape[1]
    rows = rows_blk * width

    def keep(part, side, here, columns, result):
        upcoming[here, columns] = result
        base = here.start - (0 if side == 0 else rows - rim)
        rims[side, base : base + here.size] = result.astype(BF16)

    moments[...] = rim_sums(
        first, cols, width, rows_blk, odd, banded, weights, evens_in, odds_in, begun, partial, keep
    )

    def take(targets):
        for side in range(2):
            targets[side][...] = rims[side]

    hand_out(odd, take, evens, odds)


def last_rim_kernel(count, first, cols, width, rows_blk, odd, _, banded, weights, odds_in, evens_in, begun, partial, *refs):
    earlier, (out, moments, *tail, held, sems) = refs[:count], refs[count + 1 :]
    copies = []

    def keep(part, side, here, columns, result):
        if tail and part == len(rim_parts(rows_blk)) - 1:
            tail[0][...] = result
            return
        slot = held.at[part, pl.ds(0, here.size)]
        slot[...] = result
        copies.append(pltpu.make_async_copy(slot, out.at[here, columns], sems.at[part]))
        copies[-1].start()

    total = rim_sums(
        first, cols, width, rows_blk, odd, banded, weights, evens_in, odds_in, begun, partial, keep
    )
    if tail:
        parts = [jnp.sum(one, axis=0, keepdims=True) for one in [*(ref[...] for ref in earlier), total]]
        row = jnp.concatenate(parts, axis=1)
        for slab in range(moments.shape[0]):
            moments[slab] = row
    else:
        moments[...] = total
    for copy in copies:
        copy.wait()


def store_kernel(rim, _, previous, current, out_previous, out_current, sems):
    inside = pl.ds(rim, current.shape[0] - 2 * rim)
    copies = [
        pltpu.make_async_copy(previous, out_previous, sems.at[0]),
        pltpu.make_async_copy(current.at[inside], out_current.at[inside], sems.at[1]),
    ]
    for copy in copies:
        copy.start()
    for copy in copies:
        copy.wait()


def sum_kernel(top, first, parts, tail, _, out, out_current, sem):
    rows, cols = tail.shape
    copy = pltpu.make_async_copy(tail, out_current.at[pl.ds(top, rows), pl.ds(first, cols)], sem)
    copy.start()
    total = jnp.sum(parts[...], axis=0)
    every = out.shape[1]
    for term in range(out.shape[0]):
        out[term : term + 1] = total[:, term * every : (term + 1) * every]
    copy.wait()


def in_hbm(x):
    return pltpu.with_memory_space_constraint(x, pltpu.HBM)


def local(hamiltonian_blocks, block_columns, probe, previous, current, orbital_weight):
    rows_blk, slots, width, _ = hamiltonian_blocks.shape
    rows, all_cols = current.shape
    cols = all_cols // CHUNKS
    rim = BAND * width
    slabs = lax.axis_size("slab")
    total_blocks = rows_blk * slabs
    odd = lax.axis_index("slab")[None] & 1
    pairs_of = [[(i, i ^ 1) for i in range(slabs)]]
    pairs_of.append([((i + 1) % slabs, (k + 1) % slabs) for i, k in pairs_of[0]])
    shape = jax.ShapeDtypeStruct
    edge_shape = shape((rim, cols), BF16)
    full_shape = shape((rows, all_cols), F32)
    part_shape = shape((8, cols), F32)
    flops = 2 * rows * cols * 9 * width

    def exchange(evens, odds):
        ahead = lax.ppermute(odds, "slab", pairs_of[1])
        return ahead, lax.ppermute(evens, "slab", pairs_of[0])

    def middle(token, term, chunk):
        args = [odd, token, banded, weights, *sources[chunk], terms[term]]
        aliases = {}
        if chunk:
            aliases = {len(args): 0}
            args.append(terms[term + 2])
        outs = (full_shape, shape((rows - 2 * rim, cols), BF16), part_shape)
        if term == TERMS - 1:
            outs = (full_shape, part_shape)
        return pl.pallas_call(
            functools.partial(
                middle_kernel, len(sources[chunk]), chunk * cols, cols, width, rows_blk
            ),
            out_shape=outs,
            in_specs=[SMEM] + [VMEM] * (len(args) - 1),
            out_specs=(VMEM,) * len(outs),
            scratch_shapes=[pltpu.VMEM((rows, cols), BF16)],
            input_output_aliases=aliases,
            compiler_params=params(),
            cost_estimate=cost(flops, 8 * 1024 * 1024),
            name="middle",
        )(*args)

    def rims(token, term, chunk):
        args = [odd, token, banded, weights, *halos[chunk], terms[term + 2], begun[chunk][-1]]
        specs = [SMEM] + [VMEM] * (len(args) - 1)
        bound = (chunk * cols, cols, width, rows_blk)
        if term < TERMS - 1:
            kernel = functools.partial(rim_kernel, *bound)
            outs = (full_shape, part_shape, edge_shape, edge_shape)
            out_specs = (VMEM,) * 4
            scratch = [pltpu.VMEM((2, rim, cols), BF16)]
            aliases = {6: 0}
        else:
            final = chunk == CHUNKS - 1
            if final:
                args += sums
                specs += [VMEM] * len(sums)
            kernel = functools.partial(last_rim_kernel, len(sums) if final else 0, *bound)
            aliases = {len(args): 0}
            args.append(outputs[1])
            specs.append(HBM)
            outs = (full_shape, part_shape)
            if final:
                outs = (full_shape, shape((slabs, 1, TERMS * all_cols), F32), shape((tail, cols), F32))
            out_specs = (HBM,) + (VMEM,) * (len(outs) - 1)
            count = len(rim_parts(rows_blk))
            scratch = [pltpu.VMEM((count, 2 * width, cols), F32), pltpu.SemaphoreType.DMA((count,))]
        return pl.pallas_call(
            kernel,
            out_shape=outs,
            in_specs=specs,
            out_specs=out_specs,
            scratch_shapes=scratch,
            input_output_aliases=aliases,
            compiler_params=params(),
            cost_estimate=cost(flops // 5, 2 * 1024 * 1024),
            name="rims",
        )(*args)

    first_row = lax.axis_index("slab") * rows_blk
    own_row = first_row + jnp.arange(rows_blk, dtype=jnp.int32)[:, None]
    places = (block_columns - own_row + BAND + total_blocks) % total_blocks
    pairs = rows_blk // 2

    rim_scratch = [pltpu.VMEM((2, rim, cols), F32), pltpu.SemaphoreType.DMA((2, BAND))]
    opening = pl.pallas_call(
        functools.partial(edge_kernel, 0, cols),
        out_shape=(edge_shape, edge_shape),
        in_specs=[SMEM, HBM],
        out_specs=(VMEM, VMEM),
        scratch_shapes=rim_scratch,
        compiler_params=params(),
        cost_estimate=cost(0, 6 * 2 * rim * cols),
        name="edges",
    )(odd, in_hbm(current))
    halos = [exchange(*opening)]
    banded, *opening = pl.pallas_call(
        functools.partial(band_kernel, cols, cols),
        out_shape=(
            shape((pairs, 2 * width, (2 * BAND + 2) * width), BF16),
            edge_shape,
            edge_shape,
        ),
        in_specs=[SMEM, VMEM, SMEM, HBM, HBM],
        out_specs=(VMEM,) * 3,
        scratch_shapes=[
            pltpu.VMEM(hamiltonian_blocks.shape, BF16),
            pltpu.SemaphoreType.DMA((pairs,)),
            *rim_scratch,
        ],
        compiler_params=params(),
        cost_estimate=cost(0, 12 * 1024 * 1024),
        name="band",
    )(odd, opening[1], places, in_hbm(hamiltonian_blocks), in_hbm(current))
    halos.append(exchange(*opening))
    weights = pl.pallas_call(
        functools.partial(weight_kernel, 1.0 / (total_blocks * width)),
        out_shape=full_shape,
        in_specs=[VMEM] * 3,
        out_specs=VMEM,
        compiler_params=params(),
        cost_estimate=cost(0, 4 * 1024 * 1024),
        name="weights",
    )(opening[1], orbital_weight.reshape(rows_blk, width), probe)

    terms = [previous, current] + [None] * TERMS
    sources = [(current,)] * CHUNKS
    begun = [None] * CHUNKS
    sums = []
    order = [(term, chunk) for term in range(TERMS) for chunk in range(CHUNKS)]
    ahead = len(order) - CHUNKS
    _, pair, low, high, *_ = rim_parts(rows_blk)[-1]
    top, tail = (2 * pair + low) * width, (high - low) * width
    outputs = None

    def begin(token, term, chunk):
        terms[term + 2], *begun[chunk] = middle(token, term, chunk)
        return begun[chunk][-1]

    token = begin(weights, *order[0])
    for step, (term, chunk) in enumerate(order):
        if step < ahead:
            terms[term + 2], token, *sent = rims(token, term, chunk)
            halos[chunk] = exchange(*sent)
            sources[chunk] = (sent[0], begun[chunk][0], sent[1])
        else:
            last_current, token, *ends = rims(token, term, chunk)
            outputs = (outputs[0], last_current)
        sums.append(token)
        if step + 1 < ahead:
            token = begin(token, *order[step + 1])
        elif step + 1 == ahead:
            for item in order[ahead:]:
                token = begin(token, *item)
            outputs = pl.pallas_call(
                functools.partial(store_kernel, rim),
                out_shape=(full_shape, full_shape),
                in_specs=[VMEM] * 3,
                out_specs=(HBM, HBM),
                scratch_shapes=[pltpu.SemaphoreType.DMA((2,))],
                compiler_params=params(),
                cost_estimate=cost(0, 16 * 1024 * 1024),
                name="store",
            )(token, terms[-2], terms[-1])
    gathered = lax.all_to_all(sums[-1], "slab", 0, 0)
    moments, last_current = pl.pallas_call(
        functools.partial(sum_kernel, top, all_cols - cols),
        out_shape=(shape((TERMS, all_cols), F32), full_shape),
        in_specs=[VMEM, VMEM, HBM],
        out_specs=(VMEM, HBM),
        scratch_shapes=[pltpu.SemaphoreType.DMA],
        input_output_aliases={2: 1},
        compiler_params=params(),
        name="sums",
    )(gathered, ends[0], outputs[1])
    return outputs[0], last_current, moments


def solution(mesh):
    return jax.shard_map(
        local,
        mesh=mesh,
        in_specs=(
            P("slab", None, None, None),
            P("slab", None),
            P("slab", "col"),
            P("slab", "col"),
            P("slab", "col"),
            P("slab"),
        ),
        out_specs=(P("slab", "col"), P("slab", "col"), P(None, "col")),
        check_vma=False,
    )
```

```python
import functools
import jax
import jax.numpy as jnp
from jax import lax
from jax.experimental import pallas as pl
from jax.experimental.pallas import tpu as pltpu
from jax.sharding import PartitionSpec as P

BAND = 5
TERMS = 3
CHUNKS = 2
F32 = jnp.float32
BF16 = jnp.bfloat16
VMEM = pl.BlockSpec(memory_space=pltpu.VMEM)
SMEM = pl.BlockSpec(memory_space=pltpu.SMEM)
HBM = pl.BlockSpec(memory_space=pltpu.HBM)


def params(**more):
    return pltpu.CompilerParams(vmem_limit_bytes=12 * 1024 * 1024, **more)


def cost(flops, moved):
    return pl.CostEstimate(flops=flops, bytes_accessed=moved, transcendentals=0)


def hand_out(odd, take, evens, odds):
    for parity in range(2):

        @pl.when(odd[0] == parity)
        def _():
            take((odds, evens) if parity == 0 else (evens, odds))


def pick(odd, side, pairs, at):
    evens, odds = pairs[0][at], pairs[1][at]
    taken = (odd[0] == 1) if side == 0 else (odd[0] == 0)
    return jnp.where(taken, evens, odds)


def fetch_rims(current, first, cols, held, sems):
    rim = held.shape[1]
    rows = current.shape[0]
    piece = rim // sems.shape[1]
    copies = [
        pltpu.make_async_copy(
            current.at[pl.ds(start + i * piece, piece), pl.ds(first, cols)],
            held.at[side, pl.ds(i * piece, piece)],
            sems.at[side, i],
        )
        for side, start in enumerate((0, rows - rim))
        for i in range(sems.shape[1])
    ]
    for copy in copies:
        copy.start()

    def take(targets):
        for k, copy in enumerate(copies):
            side, i = divmod(k, sems.shape[1])
            here = slice(i * piece, (i + 1) * piece)
            copy.wait()
            targets[side][here] = held[side, here].astype(BF16)

    return take


def edge_kernel(first, cols, odd, current, evens, odds, held, sems):
    hand_out(odd, fetch_rims(current, first, cols, held, sems), evens, odds)


def band_kernel(first, cols, odd, _, places, blocks, current, banded, evens, odds, held, sems, rims, rim_sems):
    rows_blk, slots, width, _ = blocks.shape
    take = fetch_rims(current, first, cols, rims, rim_sems)

    def fetch(pair):
        two = pl.ds(2 * pair, 2)
        return pltpu.make_async_copy(blocks.at[two], held.at[two], sems.at[pair])

    for pair in range(rows_blk // 2):
        fetch(pair).start()
    hand_out(odd, take, evens, odds)

    def one_pair(pair, _):
        banded[pair] = jnp.zeros(banded.shape[1:], BF16)
        fetch(pair).wait()
        for half in range(2):
            row = 2 * pair + half
            for slot in range(slots):
                at = pl.multiple_of((places[row, slot] + half) * width, width)
                banded[pair, pl.ds(half * width, width), pl.ds(at, width)] = held[row, slot]
        return 0

    lax.fori_loop(0, rows_blk // 2, one_pair, 0)


def weight_kernel(scale, _, orbital, probe, weights):
    lanes = orbital.shape[1]
    for block in range(orbital.shape[0]):
        here = pl.ds(block * lanes, lanes)
        column = jnp.broadcast_to(orbital[block : block + 1, :] * scale, (lanes, lanes)).T
        for j in range(probe.shape[1] // lanes):
            there = pl.ds(j * lanes, lanes)
            weights[here, there] = column * probe[here, there].astype(F32)


def fold(x):
    return jnp.sum(x.reshape(-1, 8, x.shape[-1]), axis=0)


def middle_kernel(sources, first, cols, width, rows_blk, odd, _, banded, weights, *refs):
    source, previous = refs[:sources], refs[sources]
    results = refs[sources + 1 + (first > 0) :]
    if sources == 1:
        *results, held, sems = results
    upcoming, *inner, partial, x = results
    columns = pl.ds(first, cols)
    rim = BAND * width
    rows = rows_blk * width
    if sources == 1:
        copies = []
        for pair in range(rows_blk // 2):
            two = pl.ds(2 * pair * width, 2 * width)
            copies.append(pltpu.make_async_copy(previous.at[two, columns], held.at[two], sems.at[pair]))
            copies[-1].start()
        x[...] = source[0][:, columns].astype(BF16)
    else:
        evens, inside, odds = source
        x[rim : rows - rim] = inside[...]
        for parity in range(2):

            @pl.when(odd[0] == parity)
            def _():
                x[0:rim] = (odds, evens)[parity][...]
                x[rows - rim : rows] = (evens, odds)[parity][...]

    total = jnp.zeros((8, cols), F32)
    for pair in range(rows_blk // 2):
        start = 2 * pair - BAND
        low, high = max(start, 0), min(start + 2 * BAND + 2, rows_blk)
        product = jnp.dot(
            banded[pair, :, (low - start) * width : (high - start) * width],
            x[low * width : high * width],
            preferred_element_type=F32,
        )
        here = pl.ds(2 * pair * width, 2 * width)
        if sources == 1:
            copies[pair].wait()
            before = held[here]
        else:
            before = previous[here, columns]
        result = 2.0 * product - before
        upcoming[here, columns] = result
        a = max(2 * pair, BAND)
        b = min(2 * pair + 2, rows_blk - BAND)
        if a < b:
            piece = result[(a - 2 * pair) * width : (b - 2 * pair) * width]
            for out in inner:
                out[(a - BAND) * width : (b - BAND) * width] = piece.astype(BF16)
            total = total + fold(piece * weights[a * width : b * width, columns])
    partial[...] = total


def rim_parts(rows_blk):
    parts = []
    for pair in range(rows_blk // 2):
        start = 2 * pair - BAND
        first = max(2 * pair, rows_blk - BAND)
        if first < 2 * pair + 2:
            parts.append((1, pair, first - 2 * pair, 2, rows_blk - start, 2 * BAND + 2, 0))
    for pair in range(rows_blk // 2):
        start = 2 * pair - BAND
        if 2 * pair < BAND:
            parts.append((0, pair, 0, min(2, BAND - 2 * pair), 0, -start, BAND + start))
    return parts


def rim_sums(first, cols, width, rows_blk, odd, banded, weights, evens, odds, begun, partial, keep):
    columns = pl.ds(first, cols)
    total = partial[...]
    for part, (side, pair, a, b, left, right, at) in enumerate(rim_parts(rows_blk)):
        product = jnp.dot(
            banded[pair, a * width : b * width, left * width : right * width],
            pick(odd, side, (evens, odds), slice(at * width, (at + right - left) * width)),
            preferred_element_type=F32,
        )
        here = pl.ds((2 * pair + a) * width, (b - a) * width)
        result = begun[here, columns] + 2.0 * product
        keep(part, side, here, columns, result)
        total = total + fold(result * weights[here, columns])
    return total


def rim_kernel(first, cols, width, rows_blk, odd, _, banded, weights, odds_in, evens_in, begun, partial, *refs):
    upcoming, moments, evens, odds, rims = refs
    rim = rims.shape[1]
    rows = rows_blk * width

    def keep(part, side, here, columns, result):
        upcoming[here, columns] = result
        base = here.start - (0 if side == 0 else rows - rim)
        rims[side, base : base + here.size] = result.astype(BF16)

    moments[...] = rim_sums(
        first, cols, width, rows_blk, odd, banded, weights, evens_in, odds_in, begun, partial, keep
    )

    def take(targets):
        for side in range(2):
            targets[side][...] = rims[side]

    hand_out(odd, take, evens, odds)


def store_rim_kernel(first, cols, width, rows_blk, odd, _, banded, weights, odds_in, evens_in, begun, partial, __, out, moments, held, sems):
    copies = []

    def keep(part, side, here, columns, result):
        slot = held.at[part, pl.ds(0, here.size)]
        slot[...] = result
        copies.append(pltpu.make_async_copy(slot, out.at[here, columns], sems.at[part]))
        copies[-1].start()

    moments[...] = rim_sums(
        first, cols, width, rows_blk, odd, banded, weights, evens_in, odds_in, begun, partial, keep
    )
    for copy in copies:
        copy.wait()


def last_rim_kernel(first, cols, width, rows_blk, odd, _, banded, weights, odds_in, evens_in, begun, partial, *refs):
    *earlier, moments, rims = refs
    rim = rims.shape[1]

    def keep(part, side, here, columns, result):
        base = here.start - (0 if side == 0 else rows_blk * width - rim)
        rims[side, base : base + here.size] = result

    total = rim_sums(
        first, cols, width, rows_blk, odd, banded, weights, evens_in, odds_in, begun, partial, keep
    )
    parts = [jnp.sum(one, axis=0, keepdims=True) for one in [*(ref[...] for ref in earlier), total]]
    row = jnp.concatenate(parts, axis=1)
    for slab in range(moments.shape[0]):
        moments[slab] = row


def store_kernel(rim, _, previous, current, out_previous, out_current, sems):
    inside = pl.ds(rim, current.shape[0] - 2 * rim)
    copies = [
        pltpu.make_async_copy(previous, out_previous, sems.at[0]),
        pltpu.make_async_copy(current.at[inside], out_current.at[inside], sems.at[1]),
    ]
    for copy in copies:
        copy.start()
    for copy in copies:
        copy.wait()


def sum_kernel(first, parts, rims, _, out, out_current, held, sems):
    _, rim, cols = rims.shape
    starts = (0, out_current.shape[0] - rim)
    copies = [
        pltpu.make_async_copy(
            rims.at[side], out_current.at[pl.ds(start, rim), pl.ds(first, cols)], sems.at[side]
        )
        for side, start in enumerate(starts)
    ]
    for copy in copies:
        copy.start()
    total = jnp.sum(parts[...], axis=0)
    every = held.shape[1]
    for term in range(held.shape[0]):
        held[term : term + 1] = total[:, term * every : (term + 1) * every]
    copies.append(pltpu.make_async_copy(held, out, sems.at[2]))
    copies[-1].start()
    for copy in copies:
        copy.wait()


def in_hbm(x):
    return pltpu.with_memory_space_constraint(x, pltpu.HBM)


def local(hamiltonian_blocks, block_columns, probe, previous, current, orbital_weight):
    rows_blk, slots, width, _ = hamiltonian_blocks.shape
    rows, all_cols = current.shape
    cols = all_cols // CHUNKS
    rim = BAND * width
    slabs = lax.axis_size("slab")
    total_blocks = rows_blk * slabs
    odd = lax.axis_index("slab")[None] & 1
    pairs_of = [[(i, i ^ 1) for i in range(slabs)]]
    pairs_of.append([((i + 1) % slabs, (k + 1) % slabs) for i, k in pairs_of[0]])
    shape = jax.ShapeDtypeStruct
    edge_shape = shape((rim, cols), BF16)
    full_shape = shape((rows, all_cols), F32)
    part_shape = shape((8, cols), F32)
    flops = 2 * rows * cols * 9 * width

    def exchange(evens, odds):
        ahead = lax.ppermute(odds, "slab", pairs_of[1])
        return ahead, lax.ppermute(evens, "slab", pairs_of[0])

    def middle(token, term, chunk):
        args = [odd, token, banded, weights, *sources[chunk], terms[term]]
        specs = [SMEM] + [VMEM] * (len(args) - 1)
        scratch = [pltpu.VMEM((rows, cols), BF16)]
        if term == 0:
            args[-1], specs[-1] = in_hbm(previous), HBM
            scratch += [pltpu.VMEM((rows, cols), F32), pltpu.SemaphoreType.DMA((pairs,))]
        aliases = {}
        if chunk:
            aliases = {len(args): 0}
            args.append(terms[term + 2])
            specs.append(VMEM)
        outs = (full_shape, shape((rows - 2 * rim, cols), BF16), part_shape)
        if term == TERMS - 1:
            outs = (full_shape, part_shape)
        return pl.pallas_call(
            functools.partial(
                middle_kernel, len(sources[chunk]), chunk * cols, cols, width, rows_blk
            ),
            out_shape=outs,
            in_specs=specs,
            out_specs=(VMEM,) * len(outs),
            scratch_shapes=scratch,
            input_output_aliases=aliases,
            compiler_params=params(),
            cost_estimate=cost(flops, 8 * 1024 * 1024),
            name="middle",
        )(*args)

    def rims(token, term, chunk):
        args = [odd, token, banded, weights, *halos[chunk], terms[term + 2], begun[chunk][-1]]
        specs = [SMEM] + [VMEM] * (len(args) - 1)
        bound = (chunk * cols, cols, width, rows_blk)
        if term < TERMS - 1:
            kernel = functools.partial(rim_kernel, *bound)
            outs = (full_shape, part_shape, edge_shape, edge_shape)
            out_specs = (VMEM,) * 4
            scratch = [pltpu.VMEM((2, rim, cols), BF16)]
            aliases = {6: 0}
        elif chunk < CHUNKS - 1:
            kernel = functools.partial(store_rim_kernel, *bound)
            aliases = {len(args): 0}
            args.append(outputs[1])
            specs.append(HBM)
            outs = (full_shape, part_shape)
            out_specs = (HBM, VMEM)
            count = len(rim_parts(rows_blk))
            scratch = [pltpu.VMEM((count, 2 * width, cols), F32), pltpu.SemaphoreType.DMA((count,))]
        else:
            kernel = functools.partial(last_rim_kernel, *bound)
            aliases = {}
            args += sums
            specs += [VMEM] * len(sums)
            outs = (shape((slabs, 1, TERMS * all_cols), F32), shape((2, rim, cols), F32))
            out_specs = (VMEM, VMEM)
            scratch = []
        return pl.pallas_call(
            kernel,
            out_shape=outs,
            in_specs=specs,
            out_specs=out_specs,
            scratch_shapes=scratch,
            input_output_aliases=aliases,
            compiler_params=params(),
            cost_estimate=cost(flops // 5, 2 * 1024 * 1024),
            name="rims",
        )(*args)

    first_row = lax.axis_index("slab") * rows_blk
    own_row = first_row + jnp.arange(rows_blk, dtype=jnp.int32)[:, None]
    places = (block_columns - own_row + BAND + total_blocks) % total_blocks
    pairs = rows_blk // 2

    rim_scratch = [pltpu.VMEM((2, rim, cols), F32), pltpu.SemaphoreType.DMA((2, BAND))]
    opening = pl.pallas_call(
        functools.partial(edge_kernel, 0, cols),
        out_shape=(edge_shape, edge_shape),
        in_specs=[SMEM, HBM],
        out_specs=(VMEM, VMEM),
        scratch_shapes=rim_scratch,
        compiler_params=params(),
        cost_estimate=cost(0, 6 * 2 * rim * cols),
        name="edges",
    )(odd, in_hbm(current))
    halos = [exchange(*opening)]
    banded, *opening = pl.pallas_call(
        functools.partial(band_kernel, cols, cols),
        out_shape=(
            shape((pairs, 2 * width, (2 * BAND + 2) * width), BF16),
            edge_shape,
            edge_shape,
        ),
        in_specs=[SMEM, VMEM, SMEM, HBM, HBM],
        out_specs=(VMEM,) * 3,
        scratch_shapes=[
            pltpu.VMEM(hamiltonian_blocks.shape, BF16),
            pltpu.SemaphoreType.DMA((pairs,)),
            *rim_scratch,
        ],
        compiler_params=params(),
        cost_estimate=cost(0, 12 * 1024 * 1024),
        name="band",
    )(odd, opening[1], places, in_hbm(hamiltonian_blocks), in_hbm(current))
    halos.append(exchange(*opening))
    weights = pl.pallas_call(
        functools.partial(weight_kernel, 1.0 / (total_blocks * width)),
        out_shape=full_shape,
        in_specs=[VMEM] * 3,
        out_specs=VMEM,
        compiler_params=params(),
        cost_estimate=cost(0, 4 * 1024 * 1024),
        name="weights",
    )(opening[1], orbital_weight.reshape(rows_blk, width), probe)

    terms = [previous, current] + [None] * TERMS
    sources = [(current,)] * CHUNKS
    begun = [None] * CHUNKS
    sums = []
    order = [(term, chunk) for term in range(TERMS) for chunk in range(CHUNKS)]
    ahead = len(order) - CHUNKS
    outputs = None

    def begin(token, term, chunk):
        terms[term + 2], *begun[chunk] = middle(token, term, chunk)
        return begun[chunk][-1]

    token = begin(weights, *order[0])
    for step, (term, chunk) in enumerate(order):
        if step < ahead:
            terms[term + 2], token, *sent = rims(token, term, chunk)
            halos[chunk] = exchange(*sent)
            sources[chunk] = (sent[0], begun[chunk][0], sent[1])
        elif step + 1 < len(order):
            last_current, token = rims(token, term, chunk)
            outputs = (outputs[0], last_current)
        else:
            scattered, ends = rims(token, term, chunk)
        sums.append(token)
        if step + 1 < ahead:
            token = begin(token, *order[step + 1])
        elif step + 1 == ahead:
            for item in order[ahead:]:
                token = begin(token, *item)
            outputs = pl.pallas_call(
                functools.partial(store_kernel, rim),
                out_shape=(full_shape, full_shape),
                in_specs=[VMEM] * 3,
                out_specs=(HBM, HBM),
                scratch_shapes=[pltpu.SemaphoreType.DMA((2,))],
                compiler_params=params(),
                cost_estimate=cost(0, 16 * 1024 * 1024),
                name="store",
            )(token, terms[-2], terms[-1])
    gathered = lax.all_to_all(scattered, "slab", 0, 0)
    moments_shape = shape((TERMS, all_cols), F32)
    moments, last_current = pl.pallas_call(
        functools.partial(sum_kernel, all_cols - cols),
        out_shape=(moments_shape, full_shape),
        in_specs=[VMEM, VMEM, HBM],
        out_specs=(HBM, HBM),
        scratch_shapes=[pltpu.VMEM(moments_shape.shape, F32), pltpu.SemaphoreType.DMA((3,))],
        input_output_aliases={2: 1},
        compiler_params=params(),
        name="sums",
    )(gathered, ends, outputs[1])
    return outputs[0], last_current, moments


def solution(mesh):
    return jax.shard_map(
        local,
        mesh=mesh,
        in_specs=(
            P("slab", None, None, None),
            P("slab", None),
            P("slab", "col"),
            P("slab", "col"),
            P("slab", "col"),
            P("slab"),
        ),
        out_specs=(P("slab", "col"), P("slab", "col"), P(None, "col")),
        check_vma=False,
    )
```

```python
import functools
import jax
import jax.numpy as jnp
from jax import lax
from jax.experimental import pallas as pl
from jax.experimental.pallas import tpu as pltpu
from jax.sharding import PartitionSpec as P

BAND = 5
TERMS = 3
CHUNKS = 2
F32 = jnp.float32
BF16 = jnp.bfloat16
VMEM = pl.BlockSpec(memory_space=pltpu.VMEM)
SMEM = pl.BlockSpec(memory_space=pltpu.SMEM)
HBM = pl.BlockSpec(memory_space=pltpu.HBM)


def params(**more):
    return pltpu.CompilerParams(vmem_limit_bytes=12 * 1024 * 1024, **more)


def cost(flops, moved):
    return pl.CostEstimate(flops=flops, bytes_accessed=moved, transcendentals=0)


def hand_out(odd, take, evens, odds):
    for parity in range(2):

        @pl.when(odd[0] == parity)
        def _():
            take((odds, evens) if parity == 0 else (evens, odds))


def pick(odd, side, pairs, at):
    evens, odds = pairs[0][at], pairs[1][at]
    taken = (odd[0] == 1) if side == 0 else (odd[0] == 0)
    return jnp.where(taken, evens, odds)


def fetch_rims(current, first, cols, held, sems):
    rim = held.shape[1]
    rows = current.shape[0]
    piece = rim // sems.shape[1]
    copies = [
        pltpu.make_async_copy(
            current.at[pl.ds(start + i * piece, piece), pl.ds(first, cols)],
            held.at[side, pl.ds(i * piece, piece)],
            sems.at[side, i],
        )
        for side, start in enumerate((0, rows - rim))
        for i in range(sems.shape[1])
    ]
    for copy in copies:
        copy.start()

    def take(targets):
        for k, copy in enumerate(copies):
            side, i = divmod(k, sems.shape[1])
            here = slice(i * piece, (i + 1) * piece)
            copy.wait()
            targets[side][here] = held[side, here].astype(BF16)

    return take


def edge_kernel(first, cols, odd, current, evens, odds, held, sems):
    hand_out(odd, fetch_rims(current, first, cols, held, sems), evens, odds)


def band_kernel(first, cols, odd, _, places, blocks, current, banded, evens, odds, held, sems, rims, rim_sems):
    rows_blk, slots, width, _ = blocks.shape
    take = fetch_rims(current, first, cols, rims, rim_sems)

    def fetch(pair):
        two = pl.ds(2 * pair, 2)
        return pltpu.make_async_copy(blocks.at[two], held.at[two], sems.at[pair])

    for pair in range(rows_blk // 2):
        fetch(pair).start()
    hand_out(odd, take, evens, odds)

    def one_pair(pair, _):
        banded[pair] = jnp.zeros(banded.shape[1:], BF16)
        fetch(pair).wait()
        for half in range(2):
            row = 2 * pair + half
            for slot in range(slots):
                at = pl.multiple_of((places[row, slot] + half) * width, width)
                banded[pair, pl.ds(half * width, width), pl.ds(at, width)] = held[row, slot]
        return 0

    lax.fori_loop(0, rows_blk // 2, one_pair, 0)


def weight_kernel(scale, _, orbital, probe, weights):
    lanes = orbital.shape[1]
    for block in range(orbital.shape[0]):
        here = pl.ds(block * lanes, lanes)
        column = jnp.broadcast_to(orbital[block : block + 1, :] * scale, (lanes, lanes)).T
        for j in range(probe.shape[1] // lanes):
            there = pl.ds(j * lanes, lanes)
            weights[here, there] = column * probe[here, there].astype(F32)


def fold(x):
    return jnp.sum(x.reshape(-1, 8, x.shape[-1]), axis=0)


def middle_kernel(sources, first, cols, width, rows_blk, odd, _, banded, weights, *refs):
    source, previous = refs[:sources], refs[sources]
    upcoming, *inner, partial, x = refs[sources + 1 + (first > 0) :]
    columns = pl.ds(first, cols)
    rim = BAND * width
    rows = rows_blk * width
    if sources == 1:
        x[...] = source[0][:, columns].astype(BF16)
    else:
        evens, inside, odds = source
        x[rim : rows - rim] = inside[...]
        for parity in range(2):

            @pl.when(odd[0] == parity)
            def _():
                x[0:rim] = (odds, evens)[parity][...]
                x[rows - rim : rows] = (evens, odds)[parity][...]

    total = jnp.zeros((8, cols), F32)
    for pair in range(rows_blk // 2):
        start = 2 * pair - BAND
        low, high = max(start, 0), min(start + 2 * BAND + 2, rows_blk)
        product = jnp.dot(
            banded[pair, :, (low - start) * width : (high - start) * width],
            x[low * width : high * width],
            preferred_element_type=F32,
        )
        here = pl.ds(2 * pair * width, 2 * width)
        result = 2.0 * product - previous[here, columns]
        upcoming[here, columns] = result
        a = max(2 * pair, BAND)
        b = min(2 * pair + 2, rows_blk - BAND)
        if a < b:
            piece = result[(a - 2 * pair) * width : (b - 2 * pair) * width]
            for out in inner:
                out[(a - BAND) * width : (b - BAND) * width] = piece.astype(BF16)
            total = total + fold(piece * weights[a * width : b * width, columns])
    partial[...] = total


def rim_parts(rows_blk):
    parts = []
    for pair in range(rows_blk // 2):
        start = 2 * pair - BAND
        first = max(2 * pair, rows_blk - BAND)
        if first < 2 * pair + 2:
            parts.append((1, pair, first - 2 * pair, 2, rows_blk - start, 2 * BAND + 2, 0))
    for pair in range(rows_blk // 2):
        start = 2 * pair - BAND
        if 2 * pair < BAND:
            parts.append((0, pair, 0, min(2, BAND - 2 * pair), 0, -start, BAND + start))
    return parts


def rim_sums(first, cols, width, rows_blk, odd, banded, weights, evens, odds, begun, partial, keep):
    columns = pl.ds(first, cols)
    total = partial[...]
    for part, (side, pair, a, b, left, right, at) in enumerate(rim_parts(rows_blk)):
        product = jnp.dot(
            banded[pair, a * width : b * width, left * width : right * width],
            pick(odd, side, (evens, odds), slice(at * width, (at + right - left) * width)),
            preferred_element_type=F32,
        )
        here = pl.ds((2 * pair + a) * width, (b - a) * width)
        result = begun[here, columns] + 2.0 * product
        keep(part, side, here, columns, result)
        total = total + fold(result * weights[here, columns])
    return total


def rim_kernel(first, cols, width, rows_blk, odd, _, banded, weights, odds_in, evens_in, begun, partial, *refs):
    upcoming, moments, evens, odds, rims = refs
    rim = rims.shape[1]
    rows = rows_blk * width

    def keep(part, side, here, columns, result):
        upcoming[here, columns] = result
        base = here.start - (0 if side == 0 else rows - rim)
        rims[side, base : base + here.size] = result.astype(BF16)

    moments[...] = rim_sums(
        first, cols, width, rows_blk, odd, banded, weights, evens_in, odds_in, begun, partial, keep
    )

    def take(targets):
        for side in range(2):
            targets[side][...] = rims[side]

    hand_out(odd, take, evens, odds)


def store_rim_kernel(first, cols, width, rows_blk, odd, _, banded, weights, odds_in, evens_in, begun, partial, __, out, moments, held, sems):
    copies = []

    def keep(part, side, here, columns, result):
        slot = held.at[part, pl.ds(0, here.size)]
        slot[...] = result
        copies.append(pltpu.make_async_copy(slot, out.at[here, columns], sems.at[part]))
        copies[-1].start()

    moments[...] = rim_sums(
        first, cols, width, rows_blk, odd, banded, weights, evens_in, odds_in, begun, partial, keep
    )
    for copy in copies:
        copy.wait()


def last_rim_kernel(first, cols, width, rows_blk, odd, _, banded, weights, odds_in, evens_in, begun, partial, *refs):
    *earlier, moments, rims = refs
    rim = rims.shape[1]

    def keep(part, side, here, columns, result):
        base = here.start - (0 if side == 0 else rows_blk * width - rim)
        rims[side, base : base + here.size] = result

    total = rim_sums(
        first, cols, width, rows_blk, odd, banded, weights, evens_in, odds_in, begun, partial, keep
    )
    parts = [jnp.sum(one, axis=0, keepdims=True) for one in [*(ref[...] for ref in earlier), total]]
    row = jnp.concatenate(parts, axis=1)
    for slab in range(moments.shape[0]):
        moments[slab] = row


def store_kernel(rim, _, previous, current, out_previous, out_current, sems):
    inside = pl.ds(rim, current.shape[0] - 2 * rim)
    copies = [
        pltpu.make_async_copy(previous, out_previous, sems.at[0]),
        pltpu.make_async_copy(current.at[inside], out_current.at[inside], sems.at[1]),
    ]
    for copy in copies:
        copy.start()
    for copy in copies:
        copy.wait()


def sum_kernel(first, parts, rims, _, out, out_current, held, sems):
    _, rim, cols = rims.shape
    starts = (0, out_current.shape[0] - rim)
    copies = [
        pltpu.make_async_copy(
            rims.at[side], out_current.at[pl.ds(start, rim), pl.ds(first, cols)], sems.at[side]
        )
        for side, start in enumerate(starts)
    ]
    for copy in copies:
        copy.start()
    total = jnp.sum(parts[...], axis=0)
    every = held.shape[1]
    for term in range(held.shape[0]):
        held[term : term + 1] = total[:, term * every : (term + 1) * every]
    copies.append(pltpu.make_async_copy(held, out, sems.at[2]))
    copies[-1].start()
    for copy in copies:
        copy.wait()


def in_hbm(x):
    return pltpu.with_memory_space_constraint(x, pltpu.HBM)


def local(hamiltonian_blocks, block_columns, probe, previous, current, orbital_weight):
    rows_blk, slots, width, _ = hamiltonian_blocks.shape
    rows, all_cols = current.shape
    cols = all_cols // CHUNKS
    rim = BAND * width
    slabs = lax.axis_size("slab")
    total_blocks = rows_blk * slabs
    odd = lax.axis_index("slab")[None] & 1
    pairs_of = [[(i, i ^ 1) for i in range(slabs)]]
    pairs_of.append([((i + 1) % slabs, (k + 1) % slabs) for i, k in pairs_of[0]])
    shape = jax.ShapeDtypeStruct
    edge_shape = shape((rim, cols), BF16)
    full_shape = shape((rows, all_cols), F32)
    part_shape = shape((8, cols), F32)
    flops = 2 * rows * cols * 9 * width

    def exchange(evens, odds):
        ahead = lax.ppermute(odds, "slab", pairs_of[1])
        return ahead, lax.ppermute(evens, "slab", pairs_of[0])

    def middle(token, term, chunk):
        args = [odd, token, banded, weights, *sources[chunk], terms[term]]
        aliases = {}
        if chunk:
            aliases = {len(args): 0}
            args.append(terms[term + 2])
        outs = (full_shape, shape((rows - 2 * rim, cols), BF16), part_shape)
        if term == TERMS - 1:
            outs = (full_shape, part_shape)
        return pl.pallas_call(
            functools.partial(
                middle_kernel, len(sources[chunk]), chunk * cols, cols, width, rows_blk
            ),
            out_shape=outs,
            in_specs=[SMEM] + [VMEM] * (len(args) - 1),
            out_specs=(VMEM,) * len(outs),
            scratch_shapes=[pltpu.VMEM((rows, cols), BF16)],
            input_output_aliases=aliases,
            compiler_params=params(),
            cost_estimate=cost(flops, 8 * 1024 * 1024),
            name="middle",
        )(*args)

    def rims(token, term, chunk):
        args = [odd, token, banded, weights, *halos[chunk], terms[term + 2], begun[chunk][-1]]
        specs = [SMEM] + [VMEM] * (len(args) - 1)
        bound = (chunk * cols, cols, width, rows_blk)
        if term < TERMS - 1:
            kernel = functools.partial(rim_kernel, *bound)
            outs = (full_shape, part_shape, edge_shape, edge_shape)
            out_specs = (VMEM,) * 4
            scratch = [pltpu.VMEM((2, rim, cols), BF16)]
            aliases = {6: 0}
        elif chunk < CHUNKS - 1:
            kernel = functools.partial(store_rim_kernel, *bound)
            aliases = {len(args): 0}
            args.append(outputs[1])
            specs.append(HBM)
            outs = (full_shape, part_shape)
            out_specs = (HBM, VMEM)
            count = len(rim_parts(rows_blk))
            scratch = [pltpu.VMEM((count, 2 * width, cols), F32), pltpu.SemaphoreType.DMA((count,))]
        else:
            kernel = functools.partial(last_rim_kernel, *bound)
            aliases = {}
            args += sums
            specs += [VMEM] * len(sums)
            outs = (shape((slabs, 1, TERMS * all_cols), F32), shape((2, rim, cols), F32))
            out_specs = (VMEM, VMEM)
            scratch = []
        return pl.pallas_call(
            kernel,
            out_shape=outs,
            in_specs=specs,
            out_specs=out_specs,
            scratch_shapes=scratch,
            input_output_aliases=aliases,
            compiler_params=params(),
            cost_estimate=cost(flops // 5, 2 * 1024 * 1024),
            name="rims",
        )(*args)

    first_row = lax.axis_index("slab") * rows_blk
    own_row = first_row + jnp.arange(rows_blk, dtype=jnp.int32)[:, None]
    places = (block_columns - own_row + BAND + total_blocks) % total_blocks
    pairs = rows_blk // 2

    rim_scratch = [pltpu.VMEM((2, rim, cols), F32), pltpu.SemaphoreType.DMA((2, BAND))]
    opening = pl.pallas_call(
        functools.partial(edge_kernel, 0, cols),
        out_shape=(edge_shape, edge_shape),
        in_specs=[SMEM, HBM],
        out_specs=(VMEM, VMEM),
        scratch_shapes=rim_scratch,
        compiler_params=params(),
        cost_estimate=cost(0, 6 * 2 * rim * cols),
        name="edges",
    )(odd, in_hbm(current))
    halos = [exchange(*opening)]
    banded, *opening = pl.pallas_call(
        functools.partial(band_kernel, cols, cols),
        out_shape=(
            shape((pairs, 2 * width, (2 * BAND + 2) * width), BF16),
            edge_shape,
            edge_shape,
        ),
        in_specs=[SMEM, VMEM, SMEM, HBM, HBM],
        out_specs=(VMEM,) * 3,
        scratch_shapes=[
            pltpu.VMEM(hamiltonian_blocks.shape, BF16),
            pltpu.SemaphoreType.DMA((pairs,)),
            *rim_scratch,
        ],
        compiler_params=params(),
        cost_estimate=cost(0, 12 * 1024 * 1024),
        name="band",
    )(odd, opening[1], places, in_hbm(hamiltonian_blocks), in_hbm(current))
    halos.append(exchange(*opening))
    weights = pl.pallas_call(
        functools.partial(weight_kernel, 1.0 / (total_blocks * width)),
        out_shape=full_shape,
        in_specs=[VMEM] * 3,
        out_specs=VMEM,
        compiler_params=params(),
        cost_estimate=cost(0, 4 * 1024 * 1024),
        name="weights",
    )(opening[1], orbital_weight.reshape(rows_blk, width), probe)

    terms = [previous, current] + [None] * TERMS
    sources = [(current,)] * CHUNKS
    begun = [None] * CHUNKS
    sums = []
    order = [(term, chunk) for term in range(TERMS) for chunk in range(CHUNKS)]
    ahead = len(order) - CHUNKS
    outputs = None

    def begin(token, term, chunk):
        terms[term + 2], *begun[chunk] = middle(token, term, chunk)
        return begun[chunk][-1]

    token = begin(weights, *order[0])
    for step, (term, chunk) in enumerate(order):
        if step < ahead:
            terms[term + 2], token, *sent = rims(token, term, chunk)
            halos[chunk] = exchange(*sent)
            sources[chunk] = (sent[0], begun[chunk][0], sent[1])
        elif step + 1 < len(order):
            last_current, token = rims(token, term, chunk)
            outputs = (outputs[0], last_current)
        else:
            scattered, ends = rims(token, term, chunk)
        sums.append(token)
        if step + 1 < ahead:
            token = begin(token, *order[step + 1])
        elif step + 1 == ahead:
            for item in order[ahead:]:
                token = begin(token, *item)
            outputs = pl.pallas_call(
                functools.partial(store_kernel, rim),
                out_shape=(full_shape, full_shape),
                in_specs=[VMEM] * 3,
                out_specs=(HBM, HBM),
                scratch_shapes=[pltpu.SemaphoreType.DMA((2,))],
                compiler_params=params(),
                cost_estimate=cost(0, 16 * 1024 * 1024),
                name="store",
            )(token, terms[-2], terms[-1])
    gathered = lax.all_to_all(scattered, "slab", 0, 0)
    moments_shape = shape((TERMS, all_cols), F32)
    moments, last_current = pl.pallas_call(
        functools.partial(sum_kernel, all_cols - cols),
        out_shape=(moments_shape, full_shape),
        in_specs=[VMEM, VMEM, HBM],
        out_specs=(HBM, HBM),
        scratch_shapes=[pltpu.VMEM(moments_shape.shape, F32), pltpu.SemaphoreType.DMA((3,))],
        input_output_aliases={2: 1},
        compiler_params=params(),
        name="sums",
    )(gathered, ends, outputs[1])
    return outputs[0], last_current, moments


def solution(mesh):
    return jax.shard_map(
        local,
        mesh=mesh,
        in_specs=(
            P("slab", None, None, None),
            P("slab", None),
            P("slab", "col"),
            P("slab", "col"),
            P("slab", "col"),
            P("slab"),
        ),
        out_specs=(P("slab", "col"), P("slab", "col"), P(None, "col")),
        check_vma=False,
    )
```

```python
import functools
import jax
import jax.numpy as jnp
from jax import lax
from jax.experimental import pallas as pl
from jax.experimental.pallas import tpu as pltpu
from jax.sharding import PartitionSpec as P

BAND = 5
TERMS = 3
CHUNKS = 2
F32 = jnp.float32
BF16 = jnp.bfloat16
VMEM = pl.BlockSpec(memory_space=pltpu.VMEM)
SMEM = pl.BlockSpec(memory_space=pltpu.SMEM)
HBM = pl.BlockSpec(memory_space=pltpu.HBM)


def params(**more):
    return pltpu.CompilerParams(vmem_limit_bytes=12 * 1024 * 1024, **more)


def cost(flops, moved):
    return pl.CostEstimate(flops=flops, bytes_accessed=moved, transcendentals=0)


def hand_out(odd, take, evens, odds):
    for parity in range(2):

        @pl.when(odd[0] == parity)
        def _():
            take((odds, evens) if parity == 0 else (evens, odds))


def pick(odd, side, pairs, at):
    evens, odds = pairs[0][at], pairs[1][at]
    taken = (odd[0] == 1) if side == 0 else (odd[0] == 0)
    return jnp.where(taken, evens, odds)


def fetch_rims(current, first, cols, held, sems):
    rim = held.shape[1]
    rows = current.shape[0]
    piece = rim // sems.shape[1]
    copies = [
        pltpu.make_async_copy(
            current.at[pl.ds(start + i * piece, piece), pl.ds(first, cols)],
            held.at[side, pl.ds(i * piece, piece)],
            sems.at[side, i],
        )
        for side, start in enumerate((0, rows - rim))
        for i in range(sems.shape[1])
    ]
    for copy in copies:
        copy.start()

    def take(targets):
        for k, copy in enumerate(copies):
            side, i = divmod(k, sems.shape[1])
            here = slice(i * piece, (i + 1) * piece)
            copy.wait()
            targets[side][here] = held[side, here].astype(BF16)

    return take


def edge_kernel(first, cols, odd, current, evens, odds, held, sems):
    hand_out(odd, fetch_rims(current, first, cols, held, sems), evens, odds)


def band_kernel(first, cols, odd, _, places, blocks, current, banded, evens, odds, sems, rims, rim_sems):
    rows_blk, slots, width, _ = blocks.shape
    take = fetch_rims(current, first, cols, rims, rim_sems)

    def one_pair(pair, _):
        banded[pair] = jnp.zeros(banded.shape[1:], BF16)
        for half in range(2):
            row = 2 * pair + half
            for slot in range(slots):
                at = pl.multiple_of((places[row, slot] + half) * width, width)
                target = banded.at[pair, pl.ds(half * width, width), pl.ds(at, width)]
                pltpu.make_async_copy(blocks.at[row, slot], target, sems.at[pair]).start()
        return 0

    lax.fori_loop(0, rows_blk // 2, one_pair, 0)
    hand_out(odd, take, evens, odds)
    for pair in range(rows_blk // 2):
        bytes_of = banded.at[pair, :, pl.ds(0, slots * width)]
        pltpu.make_async_copy(bytes_of, bytes_of, sems.at[pair]).wait()


def weight_kernel(scale, _, orbital, probe, weights):
    lanes = orbital.shape[1]
    for block in range(orbital.shape[0]):
        here = pl.ds(block * lanes, lanes)
        column = jnp.broadcast_to(orbital[block : block + 1, :] * scale, (lanes, lanes)).T
        for j in range(probe.shape[1] // lanes):
            there = pl.ds(j * lanes, lanes)
            weights[here, there] = column * probe[here, there].astype(F32)


def fold(x):
    return jnp.sum(x.reshape(-1, 8, x.shape[-1]), axis=0)


def middle_kernel(sources, first, cols, width, rows_blk, odd, _, banded, weights, *refs):
    source, previous = refs[:sources], refs[sources]
    upcoming, *inner, partial, x = refs[sources + 1 + (first > 0) :]
    columns = pl.ds(first, cols)
    rim = BAND * width
    rows = rows_blk * width
    if sources == 1:
        x[...] = source[0][:, columns].astype(BF16)
    else:
        evens, inside, odds = source
        x[rim : rows - rim] = inside[...]
        for parity in range(2):

            @pl.when(odd[0] == parity)
            def _():
                x[0:rim] = (odds, evens)[parity][...]
                x[rows - rim : rows] = (evens, odds)[parity][...]

    total = jnp.zeros((8, cols), F32)
    for pair in range(rows_blk // 2):
        start = 2 * pair - BAND
        low, high = max(start, 0), min(start + 2 * BAND + 2, rows_blk)
        product = jnp.dot(
            banded[pair, :, (low - start) * width : (high - start) * width],
            x[low * width : high * width],
            preferred_element_type=F32,
        )
        here = pl.ds(2 * pair * width, 2 * width)
        result = 2.0 * product - previous[here, columns]
        upcoming[here, columns] = result
        a = max(2 * pair, BAND)
        b = min(2 * pair + 2, rows_blk - BAND)
        if a < b:
            piece = result[(a - 2 * pair) * width : (b - 2 * pair) * width]
            for out in inner:
                out[(a - BAND) * width : (b - BAND) * width] = piece.astype(BF16)
            total = total + fold(piece * weights[a * width : b * width, columns])
    partial[...] = total


def rim_parts(rows_blk):
    parts = []
    for pair in range(rows_blk // 2):
        start = 2 * pair - BAND
        first = max(2 * pair, rows_blk - BAND)
        if first < 2 * pair + 2:
            parts.append((1, pair, first - 2 * pair, 2, rows_blk - start, 2 * BAND + 2, 0))
    for pair in range(rows_blk // 2):
        start = 2 * pair - BAND
        if 2 * pair < BAND:
            parts.append((0, pair, 0, min(2, BAND - 2 * pair), 0, -start, BAND + start))
    return parts


def rim_sums(first, cols, width, rows_blk, odd, banded, weights, evens, odds, begun, partial, keep):
    columns = pl.ds(first, cols)
    total = partial[...]
    for part, (side, pair, a, b, left, right, at) in enumerate(rim_parts(rows_blk)):
        product = jnp.dot(
            banded[pair, a * width : b * width, left * width : right * width],
            pick(odd, side, (evens, odds), slice(at * width, (at + right - left) * width)),
            preferred_element_type=F32,
        )
        here = pl.ds((2 * pair + a) * width, (b - a) * width)
        result = begun[here, columns] + 2.0 * product
        keep(part, side, here, columns, result)
        total = total + fold(result * weights[here, columns])
    return total


def rim_kernel(first, cols, width, rows_blk, odd, _, banded, weights, odds_in, evens_in, begun, partial, *refs):
    upcoming, moments, evens, odds, rims = refs
    rim = rims.shape[1]
    rows = rows_blk * width

    def keep(part, side, here, columns, result):
        upcoming[here, columns] = result
        base = here.start - (0 if side == 0 else rows - rim)
        rims[side, base : base + here.size] = result.astype(BF16)

    moments[...] = rim_sums(
        first, cols, width, rows_blk, odd, banded, weights, evens_in, odds_in, begun, partial, keep
    )

    def take(targets):
        for side in range(2):
            targets[side][...] = rims[side]

    hand_out(odd, take, evens, odds)


def store_rim_kernel(first, cols, width, rows_blk, odd, _, banded, weights, odds_in, evens_in, begun, partial, __, out, moments, held, sems):
    copies = []

    def keep(part, side, here, columns, result):
        slot = held.at[part, pl.ds(0, here.size)]
        slot[...] = result
        copies.append(pltpu.make_async_copy(slot, out.at[here, columns], sems.at[part]))
        copies[-1].start()

    moments[...] = rim_sums(
        first, cols, width, rows_blk, odd, banded, weights, evens_in, odds_in, begun, partial, keep
    )
    for copy in copies:
        copy.wait()


def last_rim_kernel(first, cols, width, rows_blk, odd, _, banded, weights, odds_in, evens_in, begun, partial, *refs):
    *earlier, moments, rims = refs
    rim = rims.shape[1]

    def keep(part, side, here, columns, result):
        base = here.start - (0 if side == 0 else rows_blk * width - rim)
        rims[side, base : base + here.size] = result

    total = rim_sums(
        first, cols, width, rows_blk, odd, banded, weights, evens_in, odds_in, begun, partial, keep
    )
    parts = [jnp.sum(one, axis=0, keepdims=True) for one in [*(ref[...] for ref in earlier), total]]
    row = jnp.concatenate(parts, axis=1)
    for slab in range(moments.shape[0]):
        moments[slab] = row


def store_kernel(rim, _, previous, current, out_previous, out_current, sems):
    inside = pl.ds(rim, current.shape[0] - 2 * rim)
    copies = [
        pltpu.make_async_copy(previous, out_previous, sems.at[0]),
        pltpu.make_async_copy(current.at[inside], out_current.at[inside], sems.at[1]),
    ]
    for copy in copies:
        copy.start()
    for copy in copies:
        copy.wait()


def sum_kernel(first, parts, rims, _, out, out_current, held, sems):
    _, rim, cols = rims.shape
    starts = (0, out_current.shape[0] - rim)
    copies = [
        pltpu.make_async_copy(
            rims.at[side], out_current.at[pl.ds(start, rim), pl.ds(first, cols)], sems.at[side]
        )
        for side, start in enumerate(starts)
    ]
    for copy in copies:
        copy.start()
    total = jnp.sum(parts[...], axis=0)
    every = held.shape[1]
    for term in range(held.shape[0]):
        held[term : term + 1] = total[:, term * every : (term + 1) * every]
    copies.append(pltpu.make_async_copy(held, out, sems.at[2]))
    copies[-1].start()
    for copy in copies:
        copy.wait()


def in_hbm(x):
    return pltpu.with_memory_space_constraint(x, pltpu.HBM)


def local(hamiltonian_blocks, block_columns, probe, previous, current, orbital_weight):
    rows_blk, slots, width, _ = hamiltonian_blocks.shape
    rows, all_cols = current.shape
    cols = all_cols // CHUNKS
    rim = BAND * width
    slabs = lax.axis_size("slab")
    total_blocks = rows_blk * slabs
    odd = lax.axis_index("slab")[None] & 1
    pairs_of = [[(i, i ^ 1) for i in range(slabs)]]
    pairs_of.append([((i + 1) % slabs, (k + 1) % slabs) for i, k in pairs_of[0]])
    shape = jax.ShapeDtypeStruct
    edge_shape = shape((rim, cols), BF16)
    full_shape = shape((rows, all_cols), F32)
    part_shape = shape((8, cols), F32)
    flops = 2 * rows * cols * 9 * width

    def exchange(evens, odds):
        ahead = lax.ppermute(odds, "slab", pairs_of[1])
        return ahead, lax.ppermute(evens, "slab", pairs_of[0])

    def middle(token, term, chunk):
        args = [odd, token, banded, weights, *sources[chunk], terms[term]]
        aliases = {}
        if chunk:
            aliases = {len(args): 0}
            args.append(terms[term + 2])
        outs = (full_shape, shape((rows - 2 * rim, cols), BF16), part_shape)
        if term == TERMS - 1:
            outs = (full_shape, part_shape)
        return pl.pallas_call(
            functools.partial(
                middle_kernel, len(sources[chunk]), chunk * cols, cols, width, rows_blk
            ),
            out_shape=outs,
            in_specs=[SMEM] + [VMEM] * (len(args) - 1),
            out_specs=(VMEM,) * len(outs),
            scratch_shapes=[pltpu.VMEM((rows, cols), BF16)],
            input_output_aliases=aliases,
            compiler_params=params(),
            cost_estimate=cost(flops, 8 * 1024 * 1024),
            name="middle",
        )(*args)

    def rims(token, term, chunk):
        args = [odd, token, banded, weights, *halos[chunk], terms[term + 2], begun[chunk][-1]]
        specs = [SMEM] + [VMEM] * (len(args) - 1)
        bound = (chunk * cols, cols, width, rows_blk)
        if term < TERMS - 1:
            kernel = functools.partial(rim_kernel, *bound)
            outs = (full_shape, part_shape, edge_shape, edge_shape)
            out_specs = (VMEM,) * 4
            scratch = [pltpu.VMEM((2, rim, cols), BF16)]
            aliases = {6: 0}
        elif chunk < CHUNKS - 1:
            kernel = functools.partial(store_rim_kernel, *bound)
            aliases = {len(args): 0}
            args.append(outputs[1])
            specs.append(HBM)
            outs = (full_shape, part_shape)
            out_specs = (HBM, VMEM)
            count = len(rim_parts(rows_blk))
            scratch = [pltpu.VMEM((count, 2 * width, cols), F32), pltpu.SemaphoreType.DMA((count,))]
        else:
            kernel = functools.partial(last_rim_kernel, *bound)
            aliases = {}
            args += sums
            specs += [VMEM] * len(sums)
            outs = (shape((slabs, 1, TERMS * all_cols), F32), shape((2, rim, cols), F32))
            out_specs = (VMEM, VMEM)
            scratch = []
        return pl.pallas_call(
            kernel,
            out_shape=outs,
            in_specs=specs,
            out_specs=out_specs,
            scratch_shapes=scratch,
            input_output_aliases=aliases,
            compiler_params=params(),
            cost_estimate=cost(flops // 5, 2 * 1024 * 1024),
            name="rims",
        )(*args)

    first_row = lax.axis_index("slab") * rows_blk
    own_row = first_row + jnp.arange(rows_blk, dtype=jnp.int32)[:, None]
    places = (block_columns - own_row + BAND + total_blocks) % total_blocks
    pairs = rows_blk // 2

    rim_scratch = [pltpu.VMEM((2, rim, cols), F32), pltpu.SemaphoreType.DMA((2, BAND))]
    opening = pl.pallas_call(
        functools.partial(edge_kernel, 0, cols),
        out_shape=(edge_shape, edge_shape),
        in_specs=[SMEM, HBM],
        out_specs=(VMEM, VMEM),
        scratch_shapes=rim_scratch,
        compiler_params=params(),
        cost_estimate=cost(0, 6 * 2 * rim * cols),
        name="edges",
    )(odd, in_hbm(current))
    halos = [exchange(*opening)]
    banded, *opening = pl.pallas_call(
        functools.partial(band_kernel, cols, cols),
        out_shape=(
            shape((pairs, 2 * width, (2 * BAND + 2) * width), BF16),
            edge_shape,
            edge_shape,
        ),
        in_specs=[SMEM, VMEM, SMEM, HBM, HBM],
        out_specs=(VMEM,) * 3,
        scratch_shapes=[
            pltpu.SemaphoreType.DMA((pairs,)),
            *rim_scratch,
        ],
        compiler_params=params(),
        cost_estimate=cost(0, 12 * 1024 * 1024),
        name="band",
    )(odd, opening[1], places, in_hbm(hamiltonian_blocks), in_hbm(current))
    halos.append(exchange(*opening))
    weights = pl.pallas_call(
        functools.partial(weight_kernel, 1.0 / (total_blocks * width)),
        out_shape=full_shape,
        in_specs=[VMEM] * 3,
        out_specs=VMEM,
        compiler_params=params(),
        cost_estimate=cost(0, 4 * 1024 * 1024),
        name="weights",
    )(opening[1], orbital_weight.reshape(rows_blk, width), probe)

    terms = [previous, current] + [None] * TERMS
    sources = [(current,)] * CHUNKS
    begun = [None] * CHUNKS
    sums = []
    order = [(term, chunk) for term in range(TERMS) for chunk in range(CHUNKS)]
    ahead = len(order) - CHUNKS
    outputs = None

    def begin(token, term, chunk):
        terms[term + 2], *begun[chunk] = middle(token, term, chunk)
        return begun[chunk][-1]

    token = begin(weights, *order[0])
    for step, (term, chunk) in enumerate(order):
        if step < ahead:
            terms[term + 2], token, *sent = rims(token, term, chunk)
            halos[chunk] = exchange(*sent)
            sources[chunk] = (sent[0], begun[chunk][0], sent[1])
        elif step + 1 < len(order):
            last_current, token = rims(token, term, chunk)
            outputs = (outputs[0], last_current)
        else:
            scattered, ends = rims(token, term, chunk)
        sums.append(token)
        if step + 1 < ahead:
            token = begin(token, *order[step + 1])
        elif step + 1 == ahead:
            for item in order[ahead:]:
                token = begin(token, *item)
            outputs = pl.pallas_call(
                functools.partial(store_kernel, rim),
                out_shape=(full_shape, full_shape),
                in_specs=[VMEM] * 3,
                out_specs=(HBM, HBM),
                scratch_shapes=[pltpu.SemaphoreType.DMA((2,))],
                compiler_params=params(),
                cost_estimate=cost(0, 16 * 1024 * 1024),
                name="store",
            )(token, terms[-2], terms[-1])
    gathered = lax.all_to_all(scattered, "slab", 0, 0)
    moments_shape = shape((TERMS, all_cols), F32)
    moments, last_current = pl.pallas_call(
        functools.partial(sum_kernel, all_cols - cols),
        out_shape=(moments_shape, full_shape),
        in_specs=[VMEM, VMEM, HBM],
        out_specs=(HBM, HBM),
        scratch_shapes=[pltpu.VMEM(moments_shape.shape, F32), pltpu.SemaphoreType.DMA((3,))],
        input_output_aliases={2: 1},
        compiler_params=params(),
        name="sums",
    )(gathered, ends, outputs[1])
    return outputs[0], last_current, moments


def solution(mesh):
    return jax.shard_map(
        local,
        mesh=mesh,
        in_specs=(
            P("slab", None, None, None),
            P("slab", None),
            P("slab", "col"),
            P("slab", "col"),
            P("slab", "col"),
            P("slab"),
        ),
        out_specs=(P("slab", "col"), P("slab", "col"), P(None, "col")),
        check_vma=False,
    )
```

```python
import functools
import jax
import jax.numpy as jnp
from jax import lax
from jax.experimental import pallas as pl
from jax.experimental.pallas import tpu as pltpu
from jax.sharding import PartitionSpec as P

BAND = 5
TERMS = 3
CHUNKS = 2
F32 = jnp.float32
BF16 = jnp.bfloat16
VMEM = pl.BlockSpec(memory_space=pltpu.VMEM)
SMEM = pl.BlockSpec(memory_space=pltpu.SMEM)
HBM = pl.BlockSpec(memory_space=pltpu.HBM)


def params(**more):
    return pltpu.CompilerParams(vmem_limit_bytes=12 * 1024 * 1024, **more)


def cost(flops, moved):
    return pl.CostEstimate(flops=flops, bytes_accessed=moved, transcendentals=0)


def hand_out(odd, take, evens, odds):
    for parity in range(2):

        @pl.when(odd[0] == parity)
        def _():
            take((odds, evens) if parity == 0 else (evens, odds))


def pick(odd, side, pairs, at):
    evens, odds = pairs[0][at], pairs[1][at]
    taken = (odd[0] == 1) if side == 0 else (odd[0] == 0)
    return jnp.where(taken, evens, odds)


def fetch_rims(current, first, cols, held, sems):
    rim = held.shape[1]
    rows = current.shape[0]
    piece = rim // sems.shape[1]
    copies = [
        pltpu.make_async_copy(
            current.at[pl.ds(start + i * piece, piece), pl.ds(first, cols)],
            held.at[side, pl.ds(i * piece, piece)],
            sems.at[side, i],
        )
        for side, start in enumerate((0, rows - rim))
        for i in range(sems.shape[1])
    ]
    for copy in copies:
        copy.start()

    def take(targets):
        for k, copy in enumerate(copies):
            side, i = divmod(k, sems.shape[1])
            here = slice(i * piece, (i + 1) * piece)
            copy.wait()
            targets[side][here] = held[side, here].astype(BF16)

    return take


def edge_kernel(first, cols, odd, current, evens, odds, held, sems):
    hand_out(odd, fetch_rims(current, first, cols, held, sems), evens, odds)


def band_kernel(first, cols, odd, _, places, blocks, current, banded, evens, odds, sems, rims, rim_sems):
    rows_blk, slots, width, _ = blocks.shape
    take = fetch_rims(current, first, cols, rims, rim_sems)

    def one_pair(pair, _):
        banded[pair] = jnp.zeros(banded.shape[1:], BF16)
        for half in range(2):
            row = 2 * pair + half
            for slot in range(slots):
                at = pl.multiple_of((places[row, slot] + half) * width, width)
                target = banded.at[pair, pl.ds(half * width, width), pl.ds(at, width)]
                pltpu.make_async_copy(blocks.at[row, slot], target, sems.at[pair]).start()
        return 0

    lax.fori_loop(0, rows_blk // 2, one_pair, 0)
    hand_out(odd, take, evens, odds)
    for pair in range(rows_blk // 2):
        bytes_of = banded.at[pair, :, pl.ds(0, slots * width)]
        pltpu.make_async_copy(bytes_of, bytes_of, sems.at[pair]).wait()


def weight_kernel(scale, _, orbital, probe, weights):
    lanes = orbital.shape[1]
    for block in range(orbital.shape[0]):
        here = pl.ds(block * lanes, lanes)
        column = jnp.broadcast_to(orbital[block : block + 1, :] * scale, (lanes, lanes)).T
        for j in range(probe.shape[1] // lanes):
            there = pl.ds(j * lanes, lanes)
            weights[here, there] = column * probe[here, there].astype(F32)


def fold(x):
    return jnp.sum(x.reshape(-1, 8, x.shape[-1]), axis=0)


def middle_kernel(sources, first, cols, width, rows_blk, odd, _, banded, weights, *refs):
    source, previous = refs[:sources], refs[sources]
    upcoming, *inner, partial, x = refs[sources + 1 + (first > 0) :]
    columns = pl.ds(first, cols)
    rim = BAND * width
    rows = rows_blk * width
    if sources == 1:
        x[...] = source[0][:, columns].astype(BF16)
    else:
        evens, inside, odds = source
        x[rim : rows - rim] = inside[...]
        for parity in range(2):

            @pl.when(odd[0] == parity)
            def _():
                x[0:rim] = (odds, evens)[parity][...]
                x[rows - rim : rows] = (evens, odds)[parity][...]

    total = jnp.zeros((8, cols), F32)
    for pair in range(rows_blk // 2):
        start = 2 * pair - BAND
        low, high = max(start, 0), min(start + 2 * BAND + 2, rows_blk)
        product = jnp.dot(
            banded[pair, :, (low - start) * width : (high - start) * width],
            x[low * width : high * width],
            preferred_element_type=F32,
        )
        here = pl.ds(2 * pair * width, 2 * width)
        result = 2.0 * product - previous[here, columns]
        upcoming[here, columns] = result
        a = max(2 * pair, BAND)
        b = min(2 * pair + 2, rows_blk - BAND)
        if a < b:
            piece = result[(a - 2 * pair) * width : (b - 2 * pair) * width]
            for out in inner:
                out[(a - BAND) * width : (b - BAND) * width] = piece.astype(BF16)
            total = total + fold(piece * weights[a * width : b * width, columns])
    partial[...] = total


def rim_parts(rows_blk):
    parts = []
    for pair in range(rows_blk // 2):
        start = 2 * pair - BAND
        first = max(2 * pair, rows_blk - BAND)
        if first < 2 * pair + 2:
            parts.append((1, pair, first - 2 * pair, 2, rows_blk - start, 2 * BAND + 2, 0))
    for pair in range(rows_blk // 2):
        start = 2 * pair - BAND
        if 2 * pair < BAND:
            parts.append((0, pair, 0, min(2, BAND - 2 * pair), 0, -start, BAND + start))
    return parts


def rim_sums(first, cols, width, rows_blk, odd, banded, weights, evens, odds, begun, partial, keep):
    columns = pl.ds(first, cols)
    total = partial[...]
    for part, (side, pair, a, b, left, right, at) in enumerate(rim_parts(rows_blk)):
        product = jnp.dot(
            banded[pair, a * width : b * width, left * width : right * width],
            pick(odd, side, (evens, odds), slice(at * width, (at + right - left) * width)),
            preferred_element_type=F32,
        )
        here = pl.ds((2 * pair + a) * width, (b - a) * width)
        result = begun[here, columns] + 2.0 * product
        keep(part, side, here, columns, result)
        total = total + fold(result * weights[here, columns])
    return total


def rim_kernel(first, cols, width, rows_blk, odd, _, banded, weights, evens_in, odds_in, begun, partial, *refs):
    upcoming, moments, evens, odds, rims = refs
    rim = rims.shape[1]
    rows = rows_blk * width

    def keep(part, side, here, columns, result):
        upcoming[here, columns] = result
        base = here.start - (0 if side == 0 else rows - rim)
        rims[side, base : base + here.size] = result.astype(BF16)

    moments[...] = rim_sums(
        first, cols, width, rows_blk, odd, banded, weights, evens_in, odds_in, begun, partial, keep
    )

    def take(targets):
        for side in range(2):
            targets[side][...] = rims[side]

    hand_out(odd, take, evens, odds)


def store_rim_kernel(first, cols, width, rows_blk, odd, _, banded, weights, evens_in, odds_in, begun, partial, __, out, moments, held, sems):
    copies = []

    def keep(part, side, here, columns, result):
        slot = held.at[part, pl.ds(0, here.size)]
        slot[...] = result
        copies.append(pltpu.make_async_copy(slot, out.at[here, columns], sems.at[part]))
        copies[-1].start()

    moments[...] = rim_sums(
        first, cols, width, rows_blk, odd, banded, weights, evens_in, odds_in, begun, partial, keep
    )
    for copy in copies:
        copy.wait()


def last_rim_kernel(first, cols, width, rows_blk, odd, _, banded, weights, evens_in, odds_in, begun, partial, *refs):
    *earlier, moments, rims = refs
    rim = rims.shape[1]

    def keep(part, side, here, columns, result):
        base = here.start - (0 if side == 0 else rows_blk * width - rim)
        rims[side, base : base + here.size] = result

    total = rim_sums(
        first, cols, width, rows_blk, odd, banded, weights, evens_in, odds_in, begun, partial, keep
    )
    parts = [jnp.sum(one, axis=0, keepdims=True) for one in [*(ref[...] for ref in earlier), total]]
    row = jnp.concatenate(parts, axis=1)
    for slab in range(moments.shape[0]):
        moments[slab] = row


def store_kernel(rim, _, previous, current, out_previous, out_current, sems):
    inside = pl.ds(rim, current.shape[0] - 2 * rim)
    copies = [
        pltpu.make_async_copy(previous, out_previous, sems.at[0]),
        pltpu.make_async_copy(current.at[inside], out_current.at[inside], sems.at[1]),
    ]
    for copy in copies:
        copy.start()
    for copy in copies:
        copy.wait()


def sum_kernel(first, parts, rims, _, out, out_current, held, sems):
    _, rim, cols = rims.shape
    starts = (0, out_current.shape[0] - rim)
    copies = [
        pltpu.make_async_copy(
            rims.at[side], out_current.at[pl.ds(start, rim), pl.ds(first, cols)], sems.at[side]
        )
        for side, start in enumerate(starts)
    ]
    for copy in copies:
        copy.start()
    total = jnp.sum(parts[...], axis=0)
    every = held.shape[1]
    for term in range(held.shape[0]):
        held[term : term + 1] = total[:, term * every : (term + 1) * every]
    copies.append(pltpu.make_async_copy(held, out, sems.at[2]))
    copies[-1].start()
    for copy in copies:
        copy.wait()


def in_hbm(x):
    return pltpu.with_memory_space_constraint(x, pltpu.HBM)


def local(hamiltonian_blocks, block_columns, probe, previous, current, orbital_weight):
    rows_blk, slots, width, _ = hamiltonian_blocks.shape
    rows, all_cols = current.shape
    cols = all_cols // CHUNKS
    rim = BAND * width
    slabs = lax.axis_size("slab")
    total_blocks = rows_blk * slabs
    odd = lax.axis_index("slab")[None] & 1
    pairs_of = [[(i, i ^ 1) for i in range(slabs)]]
    pairs_of.append([((i + 1) % slabs, (k + 1) % slabs) for i, k in pairs_of[0]])
    shape = jax.ShapeDtypeStruct
    edge_shape = shape((rim, cols), BF16)
    full_shape = shape((rows, all_cols), F32)
    part_shape = shape((8, cols), F32)
    flops = 2 * rows * cols * 9 * width

    def exchange(evens, odds):
        return lax.ppermute(evens, "slab", pairs_of[0]), lax.ppermute(odds, "slab", pairs_of[1])

    def middle(token, term, chunk):
        args = [odd, token, banded, weights, *sources[chunk], terms[term]]
        aliases = {}
        if chunk:
            aliases = {len(args): 0}
            args.append(terms[term + 2])
        outs = (full_shape, shape((rows - 2 * rim, cols), BF16), part_shape)
        if term == TERMS - 1:
            outs = (full_shape, part_shape)
        return pl.pallas_call(
            functools.partial(
                middle_kernel, len(sources[chunk]), chunk * cols, cols, width, rows_blk
            ),
            out_shape=outs,
            in_specs=[SMEM] + [VMEM] * (len(args) - 1),
            out_specs=(VMEM,) * len(outs),
            scratch_shapes=[pltpu.VMEM((rows, cols), BF16)],
            input_output_aliases=aliases,
            compiler_params=params(),
            cost_estimate=cost(flops, 8 * 1024 * 1024),
            name="middle",
        )(*args)

    def rims(token, term, chunk):
        args = [odd, token, banded, weights, *halos[chunk], terms[term + 2], begun[chunk][-1]]
        specs = [SMEM] + [VMEM] * (len(args) - 1)
        bound = (chunk * cols, cols, width, rows_blk)
        if term < TERMS - 1:
            kernel = functools.partial(rim_kernel, *bound)
            outs = (full_shape, part_shape, edge_shape, edge_shape)
            out_specs = (VMEM,) * 4
            scratch = [pltpu.VMEM((2, rim, cols), BF16)]
            aliases = {6: 0}
        elif chunk < CHUNKS - 1:
            kernel = functools.partial(store_rim_kernel, *bound)
            aliases = {len(args): 0}
            args.append(outputs[1])
            specs.append(HBM)
            outs = (full_shape, part_shape)
            out_specs = (HBM, VMEM)
            count = len(rim_parts(rows_blk))
            scratch = [pltpu.VMEM((count, 2 * width, cols), F32), pltpu.SemaphoreType.DMA((count,))]
        else:
            kernel = functools.partial(last_rim_kernel, *bound)
            aliases = {}
            args += sums
            specs += [VMEM] * len(sums)
            outs = (shape((slabs, 1, TERMS * all_cols), F32), shape((2, rim, cols), F32))
            out_specs = (VMEM, VMEM)
            scratch = []
        return pl.pallas_call(
            kernel,
            out_shape=outs,
            in_specs=specs,
            out_specs=out_specs,
            scratch_shapes=scratch,
            input_output_aliases=aliases,
            compiler_params=params(),
            cost_estimate=cost(flops // 5, 2 * 1024 * 1024),
            name="rims",
        )(*args)

    first_row = lax.axis_index("slab") * rows_blk
    own_row = first_row + jnp.arange(rows_blk, dtype=jnp.int32)[:, None]
    places = (block_columns - own_row + BAND + total_blocks) % total_blocks
    pairs = rows_blk // 2

    rim_scratch = [pltpu.VMEM((2, rim, cols), F32), pltpu.SemaphoreType.DMA((2, BAND))]
    opening = pl.pallas_call(
        functools.partial(edge_kernel, 0, cols),
        out_shape=(edge_shape, edge_shape),
        in_specs=[SMEM, HBM],
        out_specs=(VMEM, VMEM),
        scratch_shapes=rim_scratch,
        compiler_params=params(),
        cost_estimate=cost(0, 6 * 2 * rim * cols),
        name="edges",
    )(odd, in_hbm(current))
    halos = [exchange(*opening)]
    banded, *opening = pl.pallas_call(
        functools.partial(band_kernel, cols, cols),
        out_shape=(
            shape((pairs, 2 * width, (2 * BAND + 2) * width), BF16),
            edge_shape,
            edge_shape,
        ),
        in_specs=[SMEM, VMEM, SMEM, HBM, HBM],
        out_specs=(VMEM,) * 3,
        scratch_shapes=[
            pltpu.SemaphoreType.DMA((pairs,)),
            *rim_scratch,
        ],
        compiler_params=params(),
        cost_estimate=cost(0, 12 * 1024 * 1024),
        name="band",
    )(odd, opening[1], places, in_hbm(hamiltonian_blocks), in_hbm(current))
    halos.append(exchange(*opening))
    weights = pl.pallas_call(
        functools.partial(weight_kernel, 1.0 / (total_blocks * width)),
        out_shape=full_shape,
        in_specs=[VMEM] * 3,
        out_specs=VMEM,
        compiler_params=params(),
        cost_estimate=cost(0, 4 * 1024 * 1024),
        name="weights",
    )(opening[1], orbital_weight.reshape(rows_blk, width), probe)

    terms = [previous, current] + [None] * TERMS
    sources = [(current,)] * CHUNKS
    begun = [None] * CHUNKS
    sums = []
    order = [(term, chunk) for term in range(TERMS) for chunk in range(CHUNKS)]
    ahead = len(order) - CHUNKS
    outputs = None

    def begin(token, term, chunk):
        terms[term + 2], *begun[chunk] = middle(token, term, chunk)
        return begun[chunk][-1]

    token = begin(weights, *order[0])
    for step, (term, chunk) in enumerate(order):
        if step < ahead:
            terms[term + 2], token, *sent = rims(token, term, chunk)
            halos[chunk] = exchange(*sent)
            sources[chunk] = (sent[0], begun[chunk][0], sent[1])
        elif step + 1 < len(order):
            last_current, token = rims(token, term, chunk)
            outputs = (outputs[0], last_current)
        else:
            scattered, ends = rims(token, term, chunk)
        sums.append(token)
        if step + 1 < ahead:
            token = begin(token, *order[step + 1])
        elif step + 1 == ahead:
            for item in order[ahead:]:
                token = begin(token, *item)
            outputs = pl.pallas_call(
                functools.partial(store_kernel, rim),
                out_shape=(full_shape, full_shape),
                in_specs=[VMEM] * 3,
                out_specs=(HBM, HBM),
                scratch_shapes=[pltpu.SemaphoreType.DMA((2,))],
                compiler_params=params(),
                cost_estimate=cost(0, 16 * 1024 * 1024),
                name="store",
            )(token, terms[-2], terms[-1])
    gathered = lax.all_to_all(scattered, "slab", 0, 0)
    moments_shape = shape((TERMS, all_cols), F32)
    moments, last_current = pl.pallas_call(
        functools.partial(sum_kernel, all_cols - cols),
        out_shape=(moments_shape, full_shape),
        in_specs=[VMEM, VMEM, HBM],
        out_specs=(HBM, HBM),
        scratch_shapes=[pltpu.VMEM(moments_shape.shape, F32), pltpu.SemaphoreType.DMA((3,))],
        input_output_aliases={2: 1},
        compiler_params=params(),
        name="sums",
    )(gathered, ends, outputs[1])
    return outputs[0], last_current, moments


def solution(mesh):
    return jax.shard_map(
        local,
        mesh=mesh,
        in_specs=(
            P("slab", None, None, None),
            P("slab", None),
            P("slab", "col"),
            P("slab", "col"),
            P("slab", "col"),
            P("slab"),
        ),
        out_specs=(P("slab", "col"), P("slab", "col"), P(None, "col")),
        check_vma=False,
    )
```

```python
import functools
import jax
import jax.numpy as jnp
from jax import lax
from jax.experimental import pallas as pl
from jax.experimental.pallas import tpu as pltpu
from jax.sharding import PartitionSpec as P

BAND = 5
TERMS = 3
CHUNKS = 2
F32 = jnp.float32
BF16 = jnp.bfloat16
VMEM = pl.BlockSpec(memory_space=pltpu.VMEM)
SMEM = pl.BlockSpec(memory_space=pltpu.SMEM)
HBM = pl.BlockSpec(memory_space=pltpu.HBM)


def params(**more):
    return pltpu.CompilerParams(vmem_limit_bytes=12 * 1024 * 1024, **more)


def cost(flops, moved):
    return pl.CostEstimate(flops=flops, bytes_accessed=moved, transcendentals=0)


def hand_out(odd, take, evens, odds):
    for parity in range(2):

        @pl.when(odd[0] == parity)
        def _():
            take((odds, evens) if parity == 0 else (evens, odds))


def pick(odd, side, pairs, at):
    evens, odds = pairs[0][at], pairs[1][at]
    taken = (odd[0] == 1) if side == 0 else (odd[0] == 0)
    return jnp.where(taken, evens, odds)


def fetch_rims(current, first, cols, held, sems):
    rim = held.shape[1]
    rows = current.shape[0]
    piece = rim // sems.shape[1]
    copies = [
        pltpu.make_async_copy(
            current.at[pl.ds(start + i * piece, piece), pl.ds(first, cols)],
            held.at[side, pl.ds(i * piece, piece)],
            sems.at[side, i],
        )
        for side, start in enumerate((0, rows - rim))
        for i in range(sems.shape[1])
    ]
    for copy in copies:
        copy.start()

    def take(targets):
        for k, copy in enumerate(copies):
            side, i = divmod(k, sems.shape[1])
            here = slice(i * piece, (i + 1) * piece)
            copy.wait()
            targets[side][here] = held[side, here].astype(BF16)

    return take


def place_blocks(total, slab, columns, blocks, banded, held, sem, sems):
    rows_blk, slots, width, _ = blocks.shape
    load = pltpu.make_async_copy(columns, held, sem)
    load.start()
    load.wait()

    def place(row, slot):
        at = held[row, slot] - (slab[0] * rows_blk + row) + BAND
        at = jnp.where(at < 0, at + total, at)
        return jnp.where(at >= total, at - total, at)

    def one_pair(pair, _):
        banded[pair] = jnp.zeros(banded.shape[1:], BF16)
        for half in range(2):
            row = 2 * pair + half
            for slot in range(slots):
                at = pl.multiple_of((place(row, slot) + half) * width, width)
                target = banded.at[pair, pl.ds(half * width, width), pl.ds(at, width)]
                pltpu.make_async_copy(blocks.at[row, slot], target, sems.at[pair]).start()
        return 0

    lax.fori_loop(0, rows_blk // 2, one_pair, 0)
    for pair in range(rows_blk // 2):
        bytes_of = banded.at[pair, :, pl.ds(0, slots * width)]
        pltpu.make_async_copy(bytes_of, bytes_of, sems.at[pair]).wait()


def edge_kernel(first, cols, total, slab, core, columns, blocks, current, banded, evens, odds, held, rim_sems, *rest):
    hand_out([slab[0] & 1], fetch_rims(current, first, cols, held, rim_sems), evens, odds)

    @pl.when(core[0] == 1)
    def _():
        place_blocks(total, slab, columns, blocks, banded, *rest)


def band_kernel(first, cols, total, slab, core, _, columns, blocks, current, begun, banded, evens, odds, held, rim_sems, *rest):
    take = fetch_rims(current, first, cols, held, rim_sems)

    @pl.when(core[0] == 0)
    def _():
        place_blocks(total, slab, columns, blocks, banded, *rest)

    hand_out([slab[0] & 1], take, evens, odds)


def weight_kernel(scale, _, orbital, probe, weights):
    lanes = orbital.shape[1]
    for block in range(orbital.shape[0]):
        here = pl.ds(block * lanes, lanes)
        column = jnp.broadcast_to(orbital[block : block + 1, :] * scale, (lanes, lanes)).T
        for j in range(probe.shape[1] // lanes):
            there = pl.ds(j * lanes, lanes)
            weights[here, there] = column * probe[here, there].astype(F32)


def fold(x):
    return jnp.sum(x.reshape(-1, 8, x.shape[-1]), axis=0)


def middle_kernel(sources, first, cols, width, rows_blk, odd, _, banded, weights, *refs):
    source, previous = refs[:sources], refs[sources]
    upcoming, *inner, partial, x = refs[sources + 1 + (first > 0) :]
    columns = pl.ds(first, cols)
    rim = BAND * width
    rows = rows_blk * width
    if sources == 1:
        x[...] = source[0][:, columns].astype(BF16)
    else:
        evens, inside, odds = source
        x[rim : rows - rim] = inside[...]
        for parity in range(2):

            @pl.when(odd[0] == parity)
            def _():
                x[0:rim] = (odds, evens)[parity][...]
                x[rows - rim : rows] = (evens, odds)[parity][...]

    total = jnp.zeros((8, cols), F32)
    for pair in range(rows_blk // 2):
        start = 2 * pair - BAND
        low, high = max(start, 0), min(start + 2 * BAND + 2, rows_blk)
        product = jnp.dot(
            banded[pair, :, (low - start) * width : (high - start) * width],
            x[low * width : high * width],
            preferred_element_type=F32,
        )
        here = pl.ds(2 * pair * width, 2 * width)
        result = 2.0 * product - previous[here, columns]
        upcoming[here, columns] = result
        a = max(2 * pair, BAND)
        b = min(2 * pair + 2, rows_blk - BAND)
        if a < b:
            piece = result[(a - 2 * pair) * width : (b - 2 * pair) * width]
            for out in inner:
                out[(a - BAND) * width : (b - BAND) * width] = piece.astype(BF16)
            total = total + fold(piece * weights[a * width : b * width, columns])
    partial[...] = total


def rim_parts(rows_blk):
    parts = []
    for pair in range(rows_blk // 2):
        start = 2 * pair - BAND
        first = max(2 * pair, rows_blk - BAND)
        if first < 2 * pair + 2:
            parts.append((1, pair, first - 2 * pair, 2, rows_blk - start, 2 * BAND + 2, 0))
    for pair in range(rows_blk // 2):
        start = 2 * pair - BAND
        if 2 * pair < BAND:
            parts.append((0, pair, 0, min(2, BAND - 2 * pair), 0, -start, BAND + start))
    return parts


def rim_sums(first, cols, width, rows_blk, odd, banded, weights, evens, odds, begun, partial, keep):
    columns = pl.ds(first, cols)
    total = partial[...]
    for part, (side, pair, a, b, left, right, at) in enumerate(rim_parts(rows_blk)):
        product = jnp.dot(
            banded[pair, a * width : b * width, left * width : right * width],
            pick(odd, side, (evens, odds), slice(at * width, (at + right - left) * width)),
            preferred_element_type=F32,
        )
        here = pl.ds((2 * pair + a) * width, (b - a) * width)
        result = begun[here, columns] + 2.0 * product
        keep(part, side, here, columns, result)
        total = total + fold(result * weights[here, columns])
    return total


def rim_kernel(first, cols, width, rows_blk, odd, _, banded, weights, evens_in, odds_in, begun, partial, *refs):
    upcoming, moments, evens, odds, rims = refs
    rim = rims.shape[1]
    rows = rows_blk * width

    def keep(part, side, here, columns, result):
        upcoming[here, columns] = result
        base = here.start - (0 if side == 0 else rows - rim)
        rims[side, base : base + here.size] = result.astype(BF16)

    moments[...] = rim_sums(
        first, cols, width, rows_blk, odd, banded, weights, evens_in, odds_in, begun, partial, keep
    )

    def take(targets):
        for side in range(2):
            targets[side][...] = rims[side]

    hand_out(odd, take, evens, odds)


def store_rim_kernel(first, cols, width, rows_blk, odd, _, banded, weights, evens_in, odds_in, begun, partial, __, out, moments, held, sems):
    copies = []

    def keep(part, side, here, columns, result):
        slot = held.at[part, pl.ds(0, here.size)]
        slot[...] = result
        copies.append(pltpu.make_async_copy(slot, out.at[here, columns], sems.at[part]))
        copies[-1].start()

    moments[...] = rim_sums(
        first, cols, width, rows_blk, odd, banded, weights, evens_in, odds_in, begun, partial, keep
    )
    for copy in copies:
        copy.wait()


def last_rim_kernel(first, cols, width, rows_blk, odd, _, banded, weights, evens_in, odds_in, begun, partial, *refs):
    *earlier, moments, rims = refs
    rim = rims.shape[1]

    def keep(part, side, here, columns, result):
        base = here.start - (0 if side == 0 else rows_blk * width - rim)
        rims[side, base : base + here.size] = result

    total = rim_sums(
        first, cols, width, rows_blk, odd, banded, weights, evens_in, odds_in, begun, partial, keep
    )
    parts = [jnp.sum(one, axis=0, keepdims=True) for one in [*(ref[...] for ref in earlier), total]]
    row = jnp.concatenate(parts, axis=1)
    for slab in range(moments.shape[0]):
        moments[slab] = row


def store_kernel(rim, _, previous, current, out_previous, out_current, sems):
    inside = pl.ds(rim, current.shape[0] - 2 * rim)
    copies = [
        pltpu.make_async_copy(previous, out_previous, sems.at[0]),
        pltpu.make_async_copy(current.at[inside], out_current.at[inside], sems.at[1]),
    ]
    for copy in copies:
        copy.start()
    for copy in copies:
        copy.wait()


def sum_kernel(first, parts, rims, _, out, out_current, held, sems):
    _, rim, cols = rims.shape
    starts = (0, out_current.shape[0] - rim)
    copies = [
        pltpu.make_async_copy(
            rims.at[side], out_current.at[pl.ds(start, rim), pl.ds(first, cols)], sems.at[side]
        )
        for side, start in enumerate(starts)
    ]
    for copy in copies:
        copy.start()
    total = jnp.sum(parts[...], axis=0)
    every = held.shape[1]
    for term in range(held.shape[0]):
        held[term : term + 1] = total[:, term * every : (term + 1) * every]
    copies.append(pltpu.make_async_copy(held, out, sems.at[2]))
    copies[-1].start()
    for copy in copies:
        copy.wait()


def in_hbm(x):
    return pltpu.with_memory_space_constraint(x, pltpu.HBM)


def local(hamiltonian_blocks, block_columns, probe, previous, current, orbital_weight):
    rows_blk, slots, width, _ = hamiltonian_blocks.shape
    rows, all_cols = current.shape
    cols = all_cols // CHUNKS
    rim = BAND * width
    slabs = lax.axis_size("slab")
    total_blocks = rows_blk * slabs
    slab = lax.axis_index("slab")[None]
    odd = slab & 1
    pairs_of = [[(i, i ^ 1) for i in range(slabs)]]
    pairs_of.append([((i + 1) % slabs, (k + 1) % slabs) for i, k in pairs_of[0]])
    shape = jax.ShapeDtypeStruct
    edge_shape = shape((rim, cols), BF16)
    full_shape = shape((rows, all_cols), F32)
    part_shape = shape((8, cols), F32)
    flops = 2 * rows * cols * 9 * width

    def exchange(evens, odds):
        return lax.ppermute(evens, "slab", pairs_of[0]), lax.ppermute(odds, "slab", pairs_of[1])

    def middle(token, term, chunk):
        args = [odd, token, banded, weights, *sources[chunk], terms[term]]
        aliases = {}
        if chunk:
            aliases = {len(args): 0}
            args.append(terms[term + 2])
        outs = (full_shape, shape((rows - 2 * rim, cols), BF16), part_shape)
        if term == TERMS - 1:
            outs = (full_shape, part_shape)
        return pl.pallas_call(
            functools.partial(
                middle_kernel, len(sources[chunk]), chunk * cols, cols, width, rows_blk
            ),
            out_shape=outs,
            in_specs=[SMEM] + [VMEM] * (len(args) - 1),
            out_specs=(VMEM,) * len(outs),
            scratch_shapes=[pltpu.VMEM((rows, cols), BF16)],
            input_output_aliases=aliases,
            compiler_params=params(),
            cost_estimate=cost(flops, 8 * 1024 * 1024),
            name="middle",
        )(*args)

    def rims(token, term, chunk):
        args = [odd, token, banded, weights, *halos[chunk], terms[term + 2], begun[chunk][-1]]
        specs = [SMEM] + [VMEM] * (len(args) - 1)
        bound = (chunk * cols, cols, width, rows_blk)
        if term < TERMS - 1:
            kernel = functools.partial(rim_kernel, *bound)
            outs = (full_shape, part_shape, edge_shape, edge_shape)
            out_specs = (VMEM,) * 4
            scratch = [pltpu.VMEM((2, rim, cols), BF16)]
            aliases = {6: 0}
        elif chunk < CHUNKS - 1:
            kernel = functools.partial(store_rim_kernel, *bound)
            aliases = {len(args): 0}
            args.append(outputs[1])
            specs.append(HBM)
            outs = (full_shape, part_shape)
            out_specs = (HBM, VMEM)
            count = len(rim_parts(rows_blk))
            scratch = [pltpu.VMEM((count, 2 * width, cols), F32), pltpu.SemaphoreType.DMA((count,))]
        else:
            kernel = functools.partial(last_rim_kernel, *bound)
            aliases = {}
            args += sums
            specs += [VMEM] * len(sums)
            outs = (shape((slabs, 1, TERMS * all_cols), F32), shape((2, rim, cols), F32))
            out_specs = (VMEM, VMEM)
            scratch = []
        return pl.pallas_call(
            kernel,
            out_shape=outs,
            in_specs=specs,
            out_specs=out_specs,
            scratch_shapes=scratch,
            input_output_aliases=aliases,
            compiler_params=params(),
            cost_estimate=cost(flops // 5, 2 * 1024 * 1024),
            name="rims",
        )(*args)

    pairs = rows_blk // 2

    core = lax.axis_index("col")[None] & 1
    band_shape = shape((pairs, 2 * width, (2 * BAND + 2) * width), BF16)
    opening_scratch = [
        pltpu.VMEM((2, rim, cols), F32),
        pltpu.SemaphoreType.DMA((2, BAND)),
        pltpu.SMEM(block_columns.shape, jnp.int32),
        pltpu.SemaphoreType.DMA,
        pltpu.SemaphoreType.DMA((pairs,)),
    ]
    in_main = (in_hbm(block_columns), in_hbm(hamiltonian_blocks), in_hbm(current))
    banded, *opening = pl.pallas_call(
        functools.partial(edge_kernel, 0, cols, total_blocks),
        out_shape=(band_shape, edge_shape, edge_shape),
        in_specs=[SMEM, SMEM, HBM, HBM, HBM],
        out_specs=(VMEM,) * 3,
        scratch_shapes=opening_scratch,
        compiler_params=params(),
        cost_estimate=cost(0, 6 * 2 * rim * cols),
        name="edges",
    )(slab, core, *in_main)
    halos = [exchange(*opening)]
    banded, *opening = pl.pallas_call(
        functools.partial(band_kernel, cols, cols, total_blocks),
        out_shape=(band_shape, edge_shape, edge_shape),
        in_specs=[SMEM, SMEM, VMEM, HBM, HBM, HBM, VMEM],
        out_specs=(VMEM,) * 3,
        scratch_shapes=opening_scratch,
        input_output_aliases={6: 0},
        compiler_params=params(),
        cost_estimate=cost(0, 12 * 1024 * 1024),
        name="band",
    )(slab, core, opening[1], *in_main, banded)
    halos.append(exchange(*opening))
    weights = pl.pallas_call(
        functools.partial(weight_kernel, 1.0 / (total_blocks * width)),
        out_shape=full_shape,
        in_specs=[VMEM] * 3,
        out_specs=VMEM,
        compiler_params=params(),
        cost_estimate=cost(0, 4 * 1024 * 1024),
        name="weights",
    )(opening[1], orbital_weight.reshape(rows_blk, width), probe)

    terms = [previous, current] + [None] * TERMS
    sources = [(current,)] * CHUNKS
    begun = [None] * CHUNKS
    sums = []
    order = [(term, chunk) for term in range(TERMS) for chunk in range(CHUNKS)]
    ahead = len(order) - CHUNKS
    outputs = None

    def begin(token, term, chunk):
        terms[term + 2], *begun[chunk] = middle(token, term, chunk)
        return begun[chunk][-1]

    token = begin(weights, *order[0])
    for step, (term, chunk) in enumerate(order):
        if step < ahead:
            terms[term + 2], token, *sent = rims(token, term, chunk)
            halos[chunk] = exchange(*sent)
            sources[chunk] = (sent[0], begun[chunk][0], sent[1])
        elif step + 1 < len(order):
            last_current, token = rims(token, term, chunk)
            outputs = (outputs[0], last_current)
        else:
            scattered, ends = rims(token, term, chunk)
        sums.append(token)
        if step + 1 < ahead:
            token = begin(token, *order[step + 1])
        elif step + 1 == ahead:
            for item in order[ahead:]:
                token = begin(token, *item)
            outputs = pl.pallas_call(
                functools.partial(store_kernel, rim),
                out_shape=(full_shape, full_shape),
                in_specs=[VMEM] * 3,
                out_specs=(HBM, HBM),
                scratch_shapes=[pltpu.SemaphoreType.DMA((2,))],
                compiler_params=params(),
                cost_estimate=cost(0, 16 * 1024 * 1024),
                name="store",
            )(token, terms[-2], terms[-1])
    gathered = lax.all_to_all(scattered, "slab", 0, 0)
    moments_shape = shape((TERMS, all_cols), F32)
    moments, last_current = pl.pallas_call(
        functools.partial(sum_kernel, all_cols - cols),
        out_shape=(moments_shape, full_shape),
        in_specs=[VMEM, VMEM, HBM],
        out_specs=(HBM, HBM),
        scratch_shapes=[pltpu.VMEM(moments_shape.shape, F32), pltpu.SemaphoreType.DMA((3,))],
        input_output_aliases={2: 1},
        compiler_params=params(),
        name="sums",
    )(gathered, ends, outputs[1])
    return outputs[0], last_current, moments


def solution(mesh):
    return jax.shard_map(
        local,
        mesh=mesh,
        in_specs=(
            P("slab", None, None, None),
            P("slab", None),
            P("slab", "col"),
            P("slab", "col"),
            P("slab", "col"),
            P("slab"),
        ),
        out_specs=(P("slab", "col"), P("slab", "col"), P(None, "col")),
        check_vma=False,
    )
```

```python
import functools
import jax
import jax.numpy as jnp
from jax import lax
from jax.experimental import pallas as pl
from jax.experimental.pallas import tpu as pltpu
from jax.sharding import PartitionSpec as P

BAND = 5
TERMS = 3
CHUNKS = 2
F32 = jnp.float32
BF16 = jnp.bfloat16
VMEM = pl.BlockSpec(memory_space=pltpu.VMEM)
SMEM = pl.BlockSpec(memory_space=pltpu.SMEM)
HBM = pl.BlockSpec(memory_space=pltpu.HBM)


def params(**more):
    return pltpu.CompilerParams(vmem_limit_bytes=12 * 1024 * 1024, **more)


def cost(flops, moved):
    return pl.CostEstimate(flops=flops, bytes_accessed=moved, transcendentals=0)


def hand_out(odd, take, evens, odds):
    for parity in range(2):

        @pl.when(odd[0] == parity)
        def _():
            take((odds, evens) if parity == 0 else (evens, odds))


def pick(odd, side, pairs, at):
    evens, odds = pairs[0][at], pairs[1][at]
    taken = (odd[0] == 1) if side == 0 else (odd[0] == 0)
    return jnp.where(taken, evens, odds)


def fetch_rims(current, first, cols, held, sems):
    rim = held.shape[1]
    rows = current.shape[0]
    piece = rim // sems.shape[1]
    copies = [
        pltpu.make_async_copy(
            current.at[pl.ds(start + i * piece, piece), pl.ds(first, cols)],
            held.at[side, pl.ds(i * piece, piece)],
            sems.at[side, i],
        )
        for side, start in enumerate((0, rows - rim))
        for i in range(sems.shape[1])
    ]
    for copy in copies:
        copy.start()

    def take(targets):
        for k, copy in enumerate(copies):
            side, i = divmod(k, sems.shape[1])
            here = slice(i * piece, (i + 1) * piece)
            copy.wait()
            targets[side][here] = held[side, here].astype(BF16)

    return take


def edge_kernel(which, cols, odd, _, current, out, held, sems):
    rim = held.shape[0]
    piece = rim // sems.shape[0]
    side = odd[0] if which else 1 - odd[0]
    copies = []
    for i in range(sems.shape[0]):
        start = pl.multiple_of(side * (current.shape[0] - rim) + i * piece, piece)
        here = pl.ds(i * piece, piece)
        copies.append(
            pltpu.make_async_copy(current.at[pl.ds(start, piece), pl.ds(0, cols)], held.at[here], sems.at[i])
        )
        copies[-1].start()
    for i, copy in enumerate(copies):
        copy.wait()
        here = pl.ds(i * piece, piece)
        out[here] = held[here].astype(BF16)


def band_kernel(first, cols, odd, _, places, blocks, current, banded, evens, odds, sems, rims, rim_sems):
    rows_blk, slots, width, _ = blocks.shape
    take = fetch_rims(current, first, cols, rims, rim_sems)

    def one_pair(pair, _):
        banded[pair] = jnp.zeros(banded.shape[1:], BF16)
        for half in range(2):
            row = 2 * pair + half
            for slot in range(slots):
                at = pl.multiple_of((places[row, slot] + half) * width, width)
                target = banded.at[pair, pl.ds(half * width, width), pl.ds(at, width)]
                pltpu.make_async_copy(blocks.at[row, slot], target, sems.at[pair]).start()
        return 0

    lax.fori_loop(0, rows_blk // 2, one_pair, 0)
    hand_out(odd, take, evens, odds)
    for pair in range(rows_blk // 2):
        bytes_of = banded.at[pair, :, pl.ds(0, slots * width)]
        pltpu.make_async_copy(bytes_of, bytes_of, sems.at[pair]).wait()


def weight_kernel(scale, _, orbital, probe, weights):
    lanes = orbital.shape[1]
    for block in range(orbital.shape[0]):
        here = pl.ds(block * lanes, lanes)
        column = jnp.broadcast_to(orbital[block : block + 1, :] * scale, (lanes, lanes)).T
        for j in range(probe.shape[1] // lanes):
            there = pl.ds(j * lanes, lanes)
            weights[here, there] = column * probe[here, there].astype(F32)


def fold(x):
    return jnp.sum(x.reshape(-1, 8, x.shape[-1]), axis=0)


def middle_kernel(sources, first, cols, width, rows_blk, odd, _, banded, weights, *refs):
    source, previous = refs[:sources], refs[sources]
    upcoming, *inner, partial, x = refs[sources + 1 + (first > 0) :]
    columns = pl.ds(first, cols)
    rim = BAND * width
    rows = rows_blk * width
    if sources == 1:
        x[...] = source[0][:, columns].astype(BF16)
    else:
        evens, inside, odds = source
        x[rim : rows - rim] = inside[...]
        for parity in range(2):

            @pl.when(odd[0] == parity)
            def _():
                x[0:rim] = (odds, evens)[parity][...]
                x[rows - rim : rows] = (evens, odds)[parity][...]

    total = jnp.zeros((8, cols), F32)
    for pair in range(rows_blk // 2):
        start = 2 * pair - BAND
        low, high = max(start, 0), min(start + 2 * BAND + 2, rows_blk)
        product = jnp.dot(
            banded[pair, :, (low - start) * width : (high - start) * width],
            x[low * width : high * width],
            preferred_element_type=F32,
        )
        here = pl.ds(2 * pair * width, 2 * width)
        result = 2.0 * product - previous[here, columns]
        upcoming[here, columns] = result
        a = max(2 * pair, BAND)
        b = min(2 * pair + 2, rows_blk - BAND)
        if a < b:
            piece = result[(a - 2 * pair) * width : (b - 2 * pair) * width]
            for out in inner:
                out[(a - BAND) * width : (b - BAND) * width] = piece.astype(BF16)
            total = total + fold(piece * weights[a * width : b * width, columns])
    partial[...] = total


def rim_parts(rows_blk):
    parts = []
    for pair in range(rows_blk // 2):
        start = 2 * pair - BAND
        first = max(2 * pair, rows_blk - BAND)
        if first < 2 * pair + 2:
            parts.append((1, pair, first - 2 * pair, 2, rows_blk - start, 2 * BAND + 2, 0))
    for pair in range(rows_blk // 2):
        start = 2 * pair - BAND
        if 2 * pair < BAND:
            parts.append((0, pair, 0, min(2, BAND - 2 * pair), 0, -start, BAND + start))
    return parts


def rim_sums(first, cols, width, rows_blk, odd, banded, weights, evens, odds, begun, partial, keep, only=None):
    columns = pl.ds(first, cols)
    total = partial[...]
    for part, (side, pair, a, b, left, right, at) in enumerate(rim_parts(rows_blk)):
        if only not in (None, side):
            continue
        halo = slice(at * width, (at + right - left) * width)
        product = jnp.dot(
            banded[pair, a * width : b * width, left * width : right * width],
            evens[halo] if only is not None else pick(odd, side, (evens, odds), halo),
            preferred_element_type=F32,
        )
        here = pl.ds((2 * pair + a) * width, (b - a) * width)
        result = begun[here, columns] + 2.0 * product
        keep(part, side, here, columns, result)
        total = total + fold(result * weights[here, columns])
    return total


def rim_kernel(first, cols, width, rows_blk, odd, _, banded, weights, evens_in, odds_in, begun, partial, *refs):
    upcoming, moments, evens, odds, rims = refs
    rim = rims.shape[1]
    rows = rows_blk * width

    def keep(part, side, here, columns, result):
        upcoming[here, columns] = result
        base = here.start - (0 if side == 0 else rows - rim)
        rims[side, base : base + here.size] = result.astype(BF16)

    moments[...] = rim_sums(
        first, cols, width, rows_blk, odd, banded, weights, evens_in, odds_in, begun, partial, keep
    )

    def take(targets):
        for side in range(2):
            targets[side][...] = rims[side]

    hand_out(odd, take, evens, odds)


def store_rim_kernel(first, cols, width, rows_blk, odd, _, banded, weights, evens_in, odds_in, begun, partial, __, out, moments, held, sems):
    copies = []

    def keep(part, side, here, columns, result):
        slot = held.at[part, pl.ds(0, here.size)]
        slot[...] = result
        copies.append(pltpu.make_async_copy(slot, out.at[here, columns], sems.at[part]))
        copies[-1].start()

    moments[...] = rim_sums(
        first, cols, width, rows_blk, odd, banded, weights, evens_in, odds_in, begun, partial, keep
    )
    for copy in copies:
        copy.wait()


def last_side(which, bound, odd, banded, weights, halo, begun, partial, moments, held, done=None):
    for parity in range(2):
        side = parity if which else 1 - parity
        top = 0 if side == 0 else begun.shape[0] - held.shape[0]

        def keep(part, side, here, columns, result, top=top):
            held[here.start - top : here.start - top + here.size] = result

        @pl.when(odd[0] == parity)
        def _():
            moments[...] = rim_sums(
                *bound, odd, banded, weights, halo, None, begun, partial, keep, only=side
            )
            if done is not None:
                done(top)


def even_rim_kernel(first, cols, width, rows_blk, odd, _, banded, weights, halo, begun, partial, __, out, moments, held, sem):
    def done(top):
        copy = pltpu.make_async_copy(held, out.at[pl.ds(top, held.shape[0]), pl.ds(first, cols)], sem)
        copy.start()
        copy.wait()

    bound = (first, cols, width, rows_blk)
    last_side(0, bound, odd, banded, weights, halo, begun, partial, moments, held, done)


def odd_rim_kernel(first, cols, width, rows_blk, odd, _, banded, weights, halo, begun, partial, *refs):
    *earlier, moments, held, total = refs
    bound = (first, cols, width, rows_blk)
    last_side(1, bound, odd, banded, weights, halo, begun, partial, total, held)
    parts = [jnp.sum(one[...], axis=0, keepdims=True) for one in [*earlier, total]]
    row = jnp.concatenate(parts, axis=1)
    for slab in range(moments.shape[0]):
        moments[slab] = row


def store_kernel(rim, _, previous, current, out_previous, out_current, sems):
    inside = pl.ds(rim, current.shape[0] - 2 * rim)
    copies = [
        pltpu.make_async_copy(previous, out_previous, sems.at[0]),
        pltpu.make_async_copy(current.at[inside], out_current.at[inside], sems.at[1]),
    ]
    for copy in copies:
        copy.start()
    for copy in copies:
        copy.wait()


def sum_kernel(first, odd, parts, rims, _, out, out_current, held, sems):
    rim, cols = rims.shape
    top = pl.multiple_of(odd[0] * (out_current.shape[0] - rim), rim // BAND)
    copies = [
        pltpu.make_async_copy(rims, out_current.at[pl.ds(top, rim), pl.ds(first, cols)], sems.at[0])
    ]
    copies[0].start()
    total = jnp.sum(parts[...], axis=0)
    every = held.shape[1]
    for term in range(held.shape[0]):
        held[term : term + 1] = total[:, term * every : (term + 1) * every]
    copies.append(pltpu.make_async_copy(held, out, sems.at[1]))
    copies[-1].start()
    for copy in copies:
        copy.wait()


def in_hbm(x):
    return pltpu.with_memory_space_constraint(x, pltpu.HBM)


def local(hamiltonian_blocks, block_columns, probe, previous, current, orbital_weight):
    rows_blk, slots, width, _ = hamiltonian_blocks.shape
    rows, all_cols = current.shape
    cols = all_cols // CHUNKS
    rim = BAND * width
    slabs = lax.axis_size("slab")
    total_blocks = rows_blk * slabs
    odd = lax.axis_index("slab")[None] & 1
    pairs_of = [[(i, i ^ 1) for i in range(slabs)]]
    pairs_of.append([((i + 1) % slabs, (k + 1) % slabs) for i, k in pairs_of[0]])
    shape = jax.ShapeDtypeStruct
    edge_shape = shape((rim, cols), BF16)
    full_shape = shape((rows, all_cols), F32)
    part_shape = shape((8, cols), F32)
    flops = 2 * rows * cols * 9 * width

    def exchange(evens, odds):
        return lax.ppermute(evens, "slab", pairs_of[0]), lax.ppermute(odds, "slab", pairs_of[1])

    def middle(token, term, chunk):
        args = [odd, token, banded, weights, *sources[chunk], terms[term]]
        aliases = {}
        if chunk:
            aliases = {len(args): 0}
            args.append(terms[term + 2])
        outs = (full_shape, shape((rows - 2 * rim, cols), BF16), part_shape)
        if term == TERMS - 1:
            outs = (full_shape, part_shape)
        return pl.pallas_call(
            functools.partial(
                middle_kernel, len(sources[chunk]), chunk * cols, cols, width, rows_blk
            ),
            out_shape=outs,
            in_specs=[SMEM] + [VMEM] * (len(args) - 1),
            out_specs=(VMEM,) * len(outs),
            scratch_shapes=[pltpu.VMEM((rows, cols), BF16)],
            input_output_aliases=aliases,
            compiler_params=params(),
            cost_estimate=cost(flops, 8 * 1024 * 1024),
            name="middle",
        )(*args)

    def rims(token, term, chunk):
        args = [odd, token, banded, weights, *halos[chunk], terms[term + 2], begun[chunk][-1]]
        specs = [SMEM] + [VMEM] * (len(args) - 1)
        bound = (chunk * cols, cols, width, rows_blk)
        if term < TERMS - 1:
            kernel = functools.partial(rim_kernel, *bound)
            outs = (full_shape, part_shape, edge_shape, edge_shape)
            out_specs = (VMEM,) * 4
            scratch = [pltpu.VMEM((2, rim, cols), BF16)]
            aliases = {6: 0}
        else:
            kernel = functools.partial(store_rim_kernel, *bound)
            aliases = {len(args): 0}
            args.append(outputs[1])
            specs.append(HBM)
            outs = (full_shape, part_shape)
            out_specs = (HBM, VMEM)
            count = len(rim_parts(rows_blk))
            scratch = [pltpu.VMEM((count, 2 * width, cols), F32), pltpu.SemaphoreType.DMA((count,))]
        return pl.pallas_call(
            kernel,
            out_shape=outs,
            in_specs=specs,
            out_specs=out_specs,
            scratch_shapes=scratch,
            input_output_aliases=aliases,
            compiler_params=params(),
            cost_estimate=cost(flops // 5, 2 * 1024 * 1024),
            name="rims",
        )(*args)

    first_row = lax.axis_index("slab") * rows_blk
    own_row = first_row + jnp.arange(rows_blk, dtype=jnp.int32)[:, None]
    places = (block_columns - own_row + BAND + total_blocks) % total_blocks
    pairs = rows_blk // 2

    rim_scratch = [pltpu.VMEM((2, rim, cols), F32), pltpu.SemaphoreType.DMA((2, BAND))]

    def edge(token, which):
        return pl.pallas_call(
            functools.partial(edge_kernel, which, cols),
            out_shape=edge_shape,
            in_specs=[SMEM, VMEM, HBM],
            out_specs=VMEM,
            scratch_shapes=[pltpu.VMEM((rim, cols), F32), pltpu.SemaphoreType.DMA((BAND,))],
            compiler_params=params(),
            cost_estimate=cost(0, 6 * rim * cols),
            name="edge",
        )(odd, token, in_hbm(current))

    odds = edge(jnp.zeros((8, 128), F32), 1)
    from_odds = lax.ppermute(odds, "slab", pairs_of[1])
    evens = edge(odds, 0)
    halos = [(lax.ppermute(evens, "slab", pairs_of[0]), from_odds)]
    opening = (odds, evens)
    banded, *opening = pl.pallas_call(
        functools.partial(band_kernel, cols, cols),
        out_shape=(
            shape((pairs, 2 * width, (2 * BAND + 2) * width), BF16),
            edge_shape,
            edge_shape,
        ),
        in_specs=[SMEM, VMEM, SMEM, HBM, HBM],
        out_specs=(VMEM,) * 3,
        scratch_shapes=[
            pltpu.SemaphoreType.DMA((pairs,)),
            *rim_scratch,
        ],
        compiler_params=params(),
        cost_estimate=cost(0, 12 * 1024 * 1024),
        name="band",
    )(odd, opening[1], places, in_hbm(hamiltonian_blocks), in_hbm(current))
    halos.append(exchange(*opening))
    weights = pl.pallas_call(
        functools.partial(weight_kernel, 1.0 / (total_blocks * width)),
        out_shape=full_shape,
        in_specs=[VMEM] * 3,
        out_specs=VMEM,
        compiler_params=params(),
        cost_estimate=cost(0, 4 * 1024 * 1024),
        name="weights",
    )(opening[1], orbital_weight.reshape(rows_blk, width), probe)

    terms = [previous, current] + [None] * TERMS
    sources = [(current,)] * CHUNKS
    begun = [None] * CHUNKS
    sums = []
    order = [(term, chunk) for term in range(TERMS) for chunk in range(CHUNKS)]
    ahead = len(order) - CHUNKS
    outputs = None

    def begin(token, term, chunk):
        terms[term + 2], *begun[chunk] = middle(token, term, chunk)
        return begun[chunk][-1]

    token = begin(weights, *order[0])
    for step, (term, chunk) in enumerate(order):
        if step < ahead:
            terms[term + 2], token, *sent = rims(token, term, chunk)
            halos[chunk] = exchange(*sent)
            sources[chunk] = (sent[0], begun[chunk][0], sent[1])
        elif step + 1 < len(order):
            last_current, token = rims(token, term, chunk)
            outputs = (outputs[0], last_current)
        else:
            break
        sums.append(token)
        if step + 1 < ahead:
            token = begin(token, *order[step + 1])
        elif step + 1 == ahead:
            for item in order[ahead:]:
                token = begin(token, *item)
            outputs = pl.pallas_call(
                functools.partial(store_kernel, rim),
                out_shape=(full_shape, full_shape),
                in_specs=[VMEM] * 3,
                out_specs=(HBM, HBM),
                scratch_shapes=[pltpu.SemaphoreType.DMA((2,))],
                compiler_params=params(),
                cost_estimate=cost(0, 16 * 1024 * 1024),
                name="store",
            )(token, terms[-2], terms[-1])
    bound = (chunk * cols, cols, width, rows_blk)
    args = [odd, token, banded, weights, halos[chunk][0], terms[-1], begun[chunk][-1], outputs[1]]
    last_current, token = pl.pallas_call(
        functools.partial(even_rim_kernel, *bound),
        out_shape=(full_shape, part_shape),
        in_specs=[SMEM] + [VMEM] * 6 + [HBM],
        out_specs=(HBM, VMEM),
        scratch_shapes=[pltpu.VMEM((rim, cols), F32), pltpu.SemaphoreType.DMA],
        input_output_aliases={7: 0},
        compiler_params=params(),
        cost_estimate=cost(flops // 10, 1024 * 1024),
        name="even_rims",
    )(*args)
    args = [odd, token, banded, weights, halos[chunk][1], terms[-1], token, *sums]
    scattered, ends = pl.pallas_call(
        functools.partial(odd_rim_kernel, *bound),
        out_shape=(shape((slabs, 1, TERMS * all_cols), F32), shape((rim, cols), F32)),
        in_specs=[SMEM] + [VMEM] * (len(args) - 1),
        out_specs=(VMEM, VMEM),
        scratch_shapes=[pltpu.VMEM(part_shape.shape, F32)],
        compiler_params=params(),
        cost_estimate=cost(flops // 10, 1024 * 1024),
        name="odd_rims",
    )(*args)
    gathered = lax.all_to_all(scattered, "slab", 0, 0)
    moments_shape = shape((TERMS, all_cols), F32)
    moments, last_current = pl.pallas_call(
        functools.partial(sum_kernel, all_cols - cols),
        out_shape=(moments_shape, full_shape),
        in_specs=[SMEM, VMEM, VMEM, HBM],
        out_specs=(HBM, HBM),
        scratch_shapes=[pltpu.VMEM(moments_shape.shape, F32), pltpu.SemaphoreType.DMA((2,))],
        input_output_aliases={3: 1},
        compiler_params=params(),
        name="sums",
    )(odd, gathered, ends, last_current)
    return outputs[0], last_current, moments


def solution(mesh):
    return jax.shard_map(
        local,
        mesh=mesh,
        in_specs=(
            P("slab", None, None, None),
            P("slab", None),
            P("slab", "col"),
            P("slab", "col"),
            P("slab", "col"),
            P("slab"),
        ),
        out_specs=(P("slab", "col"), P("slab", "col"), P(None, "col")),
        check_vma=False,
    )
```

```python
import functools
import jax
import jax.numpy as jnp
from jax import lax
from jax.experimental import pallas as pl
from jax.experimental.pallas import tpu as pltpu
from jax.sharding import PartitionSpec as P

BAND = 5
TERMS = 3
CHUNKS = 2
F32 = jnp.float32
BF16 = jnp.bfloat16
VMEM = pl.BlockSpec(memory_space=pltpu.VMEM)
SMEM = pl.BlockSpec(memory_space=pltpu.SMEM)
HBM = pl.BlockSpec(memory_space=pltpu.HBM)


def params(**more):
    return pltpu.CompilerParams(vmem_limit_bytes=12 * 1024 * 1024, **more)


def cost(flops, moved):
    return pl.CostEstimate(flops=flops, bytes_accessed=moved, transcendentals=0)


def hand_out(odd, take, evens, odds):
    for parity in range(2):

        @pl.when(odd[0] == parity)
        def _():
            take((odds, evens) if parity == 0 else (evens, odds))


def pick(odd, side, pairs, at):
    evens, odds = pairs[0][at], pairs[1][at]
    taken = (odd[0] == 1) if side == 0 else (odd[0] == 0)
    return jnp.where(taken, evens, odds)


def fetch_rims(current, first, cols, held, sems):
    rim = held.shape[1]
    rows = current.shape[0]
    piece = rim // sems.shape[1]
    copies = [
        pltpu.make_async_copy(
            current.at[pl.ds(start + i * piece, piece), pl.ds(first, cols)],
            held.at[side, pl.ds(i * piece, piece)],
            sems.at[side, i],
        )
        for side, start in enumerate((0, rows - rim))
        for i in range(sems.shape[1])
    ]
    for copy in copies:
        copy.start()

    def take(targets):
        for k, copy in enumerate(copies):
            side, i = divmod(k, sems.shape[1])
            here = slice(i * piece, (i + 1) * piece)
            copy.wait()
            targets[side][here] = held[side, here].astype(BF16)

    return take


def edge_kernel(first, cols, odd, current, evens, odds, held, sems):
    hand_out(odd, fetch_rims(current, first, cols, held, sems), evens, odds)


def band_kernel(first, cols, odd, _, places, blocks, current, banded, evens, odds, sems, rims, rim_sems):
    rows_blk, slots, width, _ = blocks.shape
    take = fetch_rims(current, first, cols, rims, rim_sems)

    def one_pair(pair, _):
        banded[pair] = jnp.zeros(banded.shape[1:], BF16)
        for half in range(2):
            row = 2 * pair + half
            for slot in range(slots):
                at = pl.multiple_of((places[row, slot] + half) * width, width)
                target = banded.at[pair, pl.ds(half * width, width), pl.ds(at, width)]
                pltpu.make_async_copy(blocks.at[row, slot], target, sems.at[pair]).start()
        return 0

    lax.fori_loop(0, rows_blk // 2, one_pair, 0)
    hand_out(odd, take, evens, odds)
    for pair in range(rows_blk // 2):
        bytes_of = banded.at[pair, :, pl.ds(0, slots * width)]
        pltpu.make_async_copy(bytes_of, bytes_of, sems.at[pair]).wait()


def weight_kernel(scale, _, orbital, probe, weights):
    lanes = orbital.shape[1]
    for block in range(orbital.shape[0]):
        here = pl.ds(block * lanes, lanes)
        column = jnp.broadcast_to(orbital[block : block + 1, :] * scale, (lanes, lanes)).T
        for j in range(probe.shape[1] // lanes):
            there = pl.ds(j * lanes, lanes)
            weights[here, there] = column * probe[here, there].astype(F32)


def fold(x):
    return jnp.sum(x.reshape(-1, 8, x.shape[-1]), axis=0)


def middle_kernel(sources, first, cols, width, rows_blk, odd, _, banded, weights, *refs):
    source, previous = refs[:sources], refs[sources]
    upcoming, *inner, partial, x = refs[sources + 1 + (first > 0) :]
    columns = pl.ds(first, cols)
    rim = BAND * width
    rows = rows_blk * width
    if sources == 1:
        x[...] = source[0][:, columns].astype(BF16)
    else:
        evens, inside, odds = source
        x[rim : rows - rim] = inside[...]
        for parity in range(2):

            @pl.when(odd[0] == parity)
            def _():
                x[0:rim] = (odds, evens)[parity][...]
                x[rows - rim : rows] = (evens, odds)[parity][...]

    total = jnp.zeros((8, cols), F32)
    for pair in range(rows_blk // 2):
        start = 2 * pair - BAND
        low, high = max(start, 0), min(start + 2 * BAND + 2, rows_blk)
        product = jnp.dot(
            banded[pair, :, (low - start) * width : (high - start) * width],
            x[low * width : high * width],
            preferred_element_type=F32,
        )
        here = pl.ds(2 * pair * width, 2 * width)
        result = 2.0 * product - previous[here, columns]
        upcoming[here, columns] = result
        a = max(2 * pair, BAND)
        b = min(2 * pair + 2, rows_blk - BAND)
        if a < b:
            piece = result[(a - 2 * pair) * width : (b - 2 * pair) * width]
            for out in inner:
                out[(a - BAND) * width : (b - BAND) * width] = piece.astype(BF16)
            total = total + fold(piece * weights[a * width : b * width, columns])
    partial[...] = total


def rim_parts(rows_blk):
    parts = []
    for pair in range(rows_blk // 2):
        start = 2 * pair - BAND
        first = max(2 * pair, rows_blk - BAND)
        if first < 2 * pair + 2:
            parts.append((1, pair, first - 2 * pair, 2, rows_blk - start, 2 * BAND + 2, 0))
    for pair in range(rows_blk // 2):
        start = 2 * pair - BAND
        if 2 * pair < BAND:
            parts.append((0, pair, 0, min(2, BAND - 2 * pair), 0, -start, BAND + start))
    return parts


def rim_sums(first, cols, width, rows_blk, odd, banded, weights, evens, odds, begun, partial, keep, only=None):
    columns = pl.ds(first, cols)
    total = partial[...]
    for part, (side, pair, a, b, left, right, at) in enumerate(rim_parts(rows_blk)):
        if only not in (None, side):
            continue
        halo = slice(at * width, (at + right - left) * width)
        product = jnp.dot(
            banded[pair, a * width : b * width, left * width : right * width],
            evens[halo] if only is not None else pick(odd, side, (evens, odds), halo),
            preferred_element_type=F32,
        )
        here = pl.ds((2 * pair + a) * width, (b - a) * width)
        result = begun[here, columns] + 2.0 * product
        keep(part, side, here, columns, result)
        total = total + fold(result * weights[here, columns])
    return total


def rim_kernel(first, cols, width, rows_blk, odd, _, banded, weights, odds_in, evens_in, begun, partial, *refs):
    upcoming, moments, evens, odds, rims = refs
    rim = rims.shape[1]
    rows = rows_blk * width

    def keep(part, side, here, columns, result):
        upcoming[here, columns] = result
        base = here.start - (0 if side == 0 else rows - rim)
        rims[side, base : base + here.size] = result.astype(BF16)

    moments[...] = rim_sums(
        first, cols, width, rows_blk, odd, banded, weights, evens_in, odds_in, begun, partial, keep
    )

    def take(targets):
        for side in range(2):
            targets[side][...] = rims[side]

    hand_out(odd, take, evens, odds)


def store_rim_kernel(first, cols, width, rows_blk, odd, _, banded, weights, evens_in, odds_in, begun, partial, __, out, moments, held, sems):
    copies = []

    def keep(part, side, here, columns, result):
        slot = held.at[part, pl.ds(0, here.size)]
        slot[...] = result
        copies.append(pltpu.make_async_copy(slot, out.at[here, columns], sems.at[part]))
        copies[-1].start()

    moments[...] = rim_sums(
        first, cols, width, rows_blk, odd, banded, weights, evens_in, odds_in, begun, partial, keep
    )
    for copy in copies:
        copy.wait()


def last_side(which, bound, odd, banded, weights, halo, begun, partial, moments, held, done=None):
    for parity in range(2):
        side = parity if which else 1 - parity
        top = 0 if side == 0 else begun.shape[0] - held.shape[0]

        def keep(part, side, here, columns, result, top=top):
            held[here.start - top : here.start - top + here.size] = result

        @pl.when(odd[0] == parity)
        def _():
            moments[...] = rim_sums(
                *bound, odd, banded, weights, halo, None, begun, partial, keep, only=side
            )
            if done is not None:
                done(top)


def even_rim_kernel(first, cols, width, rows_blk, odd, _, banded, weights, halo, begun, partial, __, out, moments, held, sem):
    def done(top):
        copy = pltpu.make_async_copy(held, out.at[pl.ds(top, held.shape[0]), pl.ds(first, cols)], sem)
        copy.start()
        copy.wait()

    bound = (first, cols, width, rows_blk)
    last_side(0, bound, odd, banded, weights, halo, begun, partial, moments, held, done)


def odd_rim_kernel(first, cols, width, rows_blk, odd, _, banded, weights, halo, begun, partial, *refs):
    *earlier, moments, held, total = refs
    bound = (first, cols, width, rows_blk)
    last_side(1, bound, odd, banded, weights, halo, begun, partial, total, held)
    parts = [jnp.sum(one[...], axis=0, keepdims=True) for one in [*earlier, total]]
    row = jnp.concatenate(parts, axis=1)
    for slab in range(moments.shape[0]):
        moments[slab] = row


def store_kernel(rim, _, previous, current, out_previous, out_current, sems):
    inside = pl.ds(rim, current.shape[0] - 2 * rim)
    copies = [
        pltpu.make_async_copy(previous, out_previous, sems.at[0]),
        pltpu.make_async_copy(current.at[inside], out_current.at[inside], sems.at[1]),
    ]
    for copy in copies:
        copy.start()
    for copy in copies:
        copy.wait()


def sum_kernel(first, odd, parts, rims, _, out, out_current, held, sems):
    rim, cols = rims.shape
    top = pl.multiple_of(odd[0] * (out_current.shape[0] - rim), rim // BAND)
    copies = [
        pltpu.make_async_copy(rims, out_current.at[pl.ds(top, rim), pl.ds(first, cols)], sems.at[0])
    ]
    copies[0].start()
    total = jnp.sum(parts[...], axis=0)
    every = held.shape[1]
    for term in range(held.shape[0]):
        held[term : term + 1] = total[:, term * every : (term + 1) * every]
    copies.append(pltpu.make_async_copy(held, out, sems.at[1]))
    copies[-1].start()
    for copy in copies:
        copy.wait()


def in_hbm(x):
    return pltpu.with_memory_space_constraint(x, pltpu.HBM)


def local(hamiltonian_blocks, block_columns, probe, previous, current, orbital_weight):
    rows_blk, slots, width, _ = hamiltonian_blocks.shape
    rows, all_cols = current.shape
    cols = all_cols // CHUNKS
    rim = BAND * width
    slabs = lax.axis_size("slab")
    total_blocks = rows_blk * slabs
    odd = lax.axis_index("slab")[None] & 1
    pairs_of = [[(i, i ^ 1) for i in range(slabs)]]
    pairs_of.append([((i + 1) % slabs, (k + 1) % slabs) for i, k in pairs_of[0]])
    shape = jax.ShapeDtypeStruct
    edge_shape = shape((rim, cols), BF16)
    full_shape = shape((rows, all_cols), F32)
    part_shape = shape((8, cols), F32)
    flops = 2 * rows * cols * 9 * width

    def exchange(evens, odds):
        return lax.ppermute(evens, "slab", pairs_of[0]), lax.ppermute(odds, "slab", pairs_of[1])

    def middle(token, term, chunk):
        args = [odd, token, banded, weights, *sources[chunk], terms[term]]
        aliases = {}
        if chunk:
            aliases = {len(args): 0}
            args.append(terms[term + 2])
        outs = (full_shape, shape((rows - 2 * rim, cols), BF16), part_shape)
        if term == TERMS - 1:
            outs = (full_shape, part_shape)
        return pl.pallas_call(
            functools.partial(
                middle_kernel, len(sources[chunk]), chunk * cols, cols, width, rows_blk
            ),
            out_shape=outs,
            in_specs=[SMEM] + [VMEM] * (len(args) - 1),
            out_specs=(VMEM,) * len(outs),
            scratch_shapes=[pltpu.VMEM((rows, cols), BF16)],
            input_output_aliases=aliases,
            compiler_params=params(),
            cost_estimate=cost(flops, 8 * 1024 * 1024),
            name="middle",
        )(*args)

    def rims(token, term, chunk):
        args = [odd, token, banded, weights, *halos[chunk], terms[term + 2], begun[chunk][-1]]
        specs = [SMEM] + [VMEM] * (len(args) - 1)
        bound = (chunk * cols, cols, width, rows_blk)
        if term < TERMS - 1:
            args[4], args[5] = args[5], args[4]
            kernel = functools.partial(rim_kernel, *bound)
            outs = (full_shape, part_shape, edge_shape, edge_shape)
            out_specs = (VMEM,) * 4
            scratch = [pltpu.VMEM((2, rim, cols), BF16)]
            aliases = {6: 0}
        else:
            kernel = functools.partial(store_rim_kernel, *bound)
            aliases = {len(args): 0}
            args.append(outputs[1])
            specs.append(HBM)
            outs = (full_shape, part_shape)
            out_specs = (HBM, VMEM)
            count = len(rim_parts(rows_blk))
            scratch = [pltpu.VMEM((count, 2 * width, cols), F32), pltpu.SemaphoreType.DMA((count,))]
        return pl.pallas_call(
            kernel,
            out_shape=outs,
            in_specs=specs,
            out_specs=out_specs,
            scratch_shapes=scratch,
            input_output_aliases=aliases,
            compiler_params=params(),
            cost_estimate=cost(flops // 5, 2 * 1024 * 1024),
            name="rims",
        )(*args)

    first_row = lax.axis_index("slab") * rows_blk
    own_row = first_row + jnp.arange(rows_blk, dtype=jnp.int32)[:, None]
    places = (block_columns - own_row + BAND + total_blocks) % total_blocks
    pairs = rows_blk // 2

    rim_scratch = [pltpu.VMEM((2, rim, cols), F32), pltpu.SemaphoreType.DMA((2, BAND))]
    opening = pl.pallas_call(
        functools.partial(edge_kernel, 0, cols),
        out_shape=(edge_shape, edge_shape),
        in_specs=[SMEM, HBM],
        out_specs=(VMEM, VMEM),
        scratch_shapes=rim_scratch,
        compiler_params=params(),
        cost_estimate=cost(0, 6 * 2 * rim * cols),
        name="edges",
    )(odd, in_hbm(current))
    halos = [exchange(*opening)]
    banded, *opening = pl.pallas_call(
        functools.partial(band_kernel, cols, cols),
        out_shape=(
            shape((pairs, 2 * width, (2 * BAND + 2) * width), BF16),
            edge_shape,
            edge_shape,
        ),
        in_specs=[SMEM, VMEM, SMEM, HBM, HBM],
        out_specs=(VMEM,) * 3,
        scratch_shapes=[
            pltpu.SemaphoreType.DMA((pairs,)),
            *rim_scratch,
        ],
        compiler_params=params(),
        cost_estimate=cost(0, 12 * 1024 * 1024),
        name="band",
    )(odd, opening[1], places, in_hbm(hamiltonian_blocks), in_hbm(current))
    halos.append(exchange(*opening))
    weights = pl.pallas_call(
        functools.partial(weight_kernel, 1.0 / (total_blocks * width)),
        out_shape=full_shape,
        in_specs=[VMEM] * 3,
        out_specs=VMEM,
        compiler_params=params(),
        cost_estimate=cost(0, 4 * 1024 * 1024),
        name="weights",
    )(opening[1], orbital_weight.reshape(rows_blk, width), probe)

    terms = [previous, current] + [None] * TERMS
    sources = [(current,)] * CHUNKS
    begun = [None] * CHUNKS
    sums = []
    order = [(term, chunk) for term in range(TERMS) for chunk in range(CHUNKS)]
    ahead = len(order) - CHUNKS
    outputs = None

    def begin(token, term, chunk):
        terms[term + 2], *begun[chunk] = middle(token, term, chunk)
        return begun[chunk][-1]

    token = begin(weights, *order[0])
    for step, (term, chunk) in enumerate(order):
        if step < ahead:
            terms[term + 2], token, *sent = rims(token, term, chunk)
            halos[chunk] = exchange(*sent)
            sources[chunk] = (sent[0], begun[chunk][0], sent[1])
        elif step + 1 < len(order):
            last_current, token = rims(token, term, chunk)
            outputs = (outputs[0], last_current)
        else:
            break
        sums.append(token)
        if step + 1 < ahead:
            token = begin(token, *order[step + 1])
        elif step + 1 == ahead:
            for item in order[ahead:]:
                token = begin(token, *item)
            outputs = pl.pallas_call(
                functools.partial(store_kernel, rim),
                out_shape=(full_shape, full_shape),
                in_specs=[VMEM] * 3,
                out_specs=(HBM, HBM),
                scratch_shapes=[pltpu.SemaphoreType.DMA((2,))],
                compiler_params=params(),
                cost_estimate=cost(0, 16 * 1024 * 1024),
                name="store",
            )(token, terms[-2], terms[-1])
    bound = (chunk * cols, cols, width, rows_blk)
    args = [odd, token, banded, weights, halos[chunk][0], terms[-1], begun[chunk][-1], outputs[1]]
    last_current, token = pl.pallas_call(
        functools.partial(even_rim_kernel, *bound),
        out_shape=(full_shape, part_shape),
        in_specs=[SMEM] + [VMEM] * 6 + [HBM],
        out_specs=(HBM, VMEM),
        scratch_shapes=[pltpu.VMEM((rim, cols), F32), pltpu.SemaphoreType.DMA],
        input_output_aliases={7: 0},
        compiler_params=params(),
        cost_estimate=cost(flops // 10, 1024 * 1024),
        name="even_rims",
    )(*args)
    args = [odd, token, banded, weights, halos[chunk][1], terms[-1], token, *sums]
    scattered, ends = pl.pallas_call(
        functools.partial(odd_rim_kernel, *bound),
        out_shape=(shape((slabs, 1, TERMS * all_cols), F32), shape((rim, cols), F32)),
        in_specs=[SMEM] + [VMEM] * (len(args) - 1),
        out_specs=(VMEM, VMEM),
        scratch_shapes=[pltpu.VMEM(part_shape.shape, F32)],
        compiler_params=params(),
        cost_estimate=cost(flops // 10, 1024 * 1024),
        name="odd_rims",
    )(*args)
    gathered = lax.all_to_all(scattered, "slab", 0, 0)
    moments_shape = shape((TERMS, all_cols), F32)
    moments, last_current = pl.pallas_call(
        functools.partial(sum_kernel, all_cols - cols),
        out_shape=(moments_shape, full_shape),
        in_specs=[SMEM, VMEM, VMEM, HBM],
        out_specs=(HBM, HBM),
        scratch_shapes=[pltpu.VMEM(moments_shape.shape, F32), pltpu.SemaphoreType.DMA((2,))],
        input_output_aliases={3: 1},
        compiler_params=params(),
        name="sums",
    )(odd, gathered, ends, last_current)
    return outputs[0], last_current, moments


def solution(mesh):
    return jax.shard_map(
        local,
        mesh=mesh,
        in_specs=(
            P("slab", None, None, None),
            P("slab", None),
            P("slab", "col"),
            P("slab", "col"),
            P("slab", "col"),
            P("slab"),
        ),
        out_specs=(P("slab", "col"), P("slab", "col"), P(None, "col")),
        check_vma=False,
    )
```

```python
import functools
import jax
import jax.numpy as jnp
from jax import lax
from jax.experimental import pallas as pl
from jax.experimental.pallas import tpu as pltpu
from jax.sharding import PartitionSpec as P

BAND = 5
TERMS = 3
CHUNKS = 2
F32 = jnp.float32
BF16 = jnp.bfloat16
VMEM = pl.BlockSpec(memory_space=pltpu.VMEM)
SMEM = pl.BlockSpec(memory_space=pltpu.SMEM)
HBM = pl.BlockSpec(memory_space=pltpu.HBM)


def params(**more):
    return pltpu.CompilerParams(vmem_limit_bytes=12 * 1024 * 1024, **more)


def cost(flops, moved):
    return pl.CostEstimate(flops=flops, bytes_accessed=moved, transcendentals=0)


def hand_out(odd, take, evens, odds):
    for parity in range(2):

        @pl.when(odd[0] == parity)
        def _():
            take((odds, evens) if parity == 0 else (evens, odds))


def pick(odd, side, pairs, at):
    evens, odds = pairs[0][at], pairs[1][at]
    taken = (odd[0] == 1) if side == 0 else (odd[0] == 0)
    return jnp.where(taken, evens, odds)


def fetch_rims(current, first, cols, held, sems):
    rim = held.shape[1]
    rows = current.shape[0]
    piece = rim // sems.shape[1]
    copies = [
        pltpu.make_async_copy(
            current.at[pl.ds(start + i * piece, piece), pl.ds(first, cols)],
            held.at[side, pl.ds(i * piece, piece)],
            sems.at[side, i],
        )
        for side, start in enumerate((0, rows - rim))
        for i in range(sems.shape[1])
    ]
    for copy in copies:
        copy.start()

    def take(targets):
        for k, copy in enumerate(copies):
            side, i = divmod(k, sems.shape[1])
            here = slice(i * piece, (i + 1) * piece)
            copy.wait()
            targets[side][here] = held[side, here].astype(BF16)

    return take


def edge_kernel(first, cols, odd, current, evens, odds, held, sems):
    hand_out(odd, fetch_rims(current, first, cols, held, sems), evens, odds)


def band_kernel(first, cols, odd, _, places, blocks, current, banded, evens, odds, sems, rims, rim_sems):
    rows_blk, slots, width, _ = blocks.shape
    take = fetch_rims(current, first, cols, rims, rim_sems)

    def one_pair(pair, _):
        banded[pair] = jnp.zeros(banded.shape[1:], BF16)
        for half in range(2):
            row = 2 * pair + half
            for slot in range(slots):
                at = pl.multiple_of((places[row, slot] + half) * width, width)
                target = banded.at[pair, pl.ds(half * width, width), pl.ds(at, width)]
                pltpu.make_async_copy(blocks.at[row, slot], target, sems.at[pair]).start()
        return 0

    lax.fori_loop(0, rows_blk // 2, one_pair, 0)
    hand_out(odd, take, evens, odds)
    for pair in range(rows_blk // 2):
        bytes_of = banded.at[pair, :, pl.ds(0, slots * width)]
        pltpu.make_async_copy(bytes_of, bytes_of, sems.at[pair]).wait()


def weight_kernel(scale, _, orbital, probe, weights):
    lanes = orbital.shape[1]
    for block in range(orbital.shape[0]):
        here = pl.ds(block * lanes, lanes)
        column = jnp.broadcast_to(orbital[block : block + 1, :] * scale, (lanes, lanes)).T
        for j in range(probe.shape[1] // lanes):
            there = pl.ds(j * lanes, lanes)
            weights[here, there] = column * probe[here, there].astype(F32)


def fold(x):
    return jnp.sum(x.reshape(-1, 8, x.shape[-1]), axis=0)


def middle_kernel(sources, first, cols, width, rows_blk, odd, _, banded, weights, *refs):
    source, previous = refs[:sources], refs[sources]
    upcoming, *inner, partial, x = refs[sources + 1 + (first > 0) :]
    columns = pl.ds(first, cols)
    rim = BAND * width
    rows = rows_blk * width
    if sources == 1:
        x[...] = source[0][:, columns].astype(BF16)
    else:
        evens, inside, odds = source
        x[rim : rows - rim] = inside[...]
        for parity in range(2):

            @pl.when(odd[0] == parity)
            def _():
                x[0:rim] = (odds, evens)[parity][...]
                x[rows - rim : rows] = (evens, odds)[parity][...]

    total = jnp.zeros((8, cols), F32)
    for pair in range(rows_blk // 2):
        start = 2 * pair - BAND
        low, high = max(start, 0), min(start + 2 * BAND + 2, rows_blk)
        product = jnp.dot(
            banded[pair, :, (low - start) * width : (high - start) * width],
            x[low * width : high * width],
            preferred_element_type=F32,
        )
        here = pl.ds(2 * pair * width, 2 * width)
        result = 2.0 * product - previous[here, columns]
        upcoming[here, columns] = result
        a = max(2 * pair, BAND)
        b = min(2 * pair + 2, rows_blk - BAND)
        if a < b:
            piece = result[(a - 2 * pair) * width : (b - 2 * pair) * width]
            for out in inner:
                out[(a - BAND) * width : (b - BAND) * width] = piece.astype(BF16)
            total = total + fold(piece * weights[a * width : b * width, columns])
    partial[...] = total


def rim_parts(rows_blk):
    parts = []
    for pair in range(rows_blk // 2):
        start = 2 * pair - BAND
        first = max(2 * pair, rows_blk - BAND)
        if first < 2 * pair + 2:
            parts.append((1, pair, first - 2 * pair, 2, rows_blk - start, 2 * BAND + 2, 0))
    for pair in range(rows_blk // 2):
        start = 2 * pair - BAND
        if 2 * pair < BAND:
            parts.append((0, pair, 0, min(2, BAND - 2 * pair), 0, -start, BAND + start))
    return parts


def rim_sums(first, cols, width, rows_blk, odd, banded, weights, evens, odds, begun, partial, keep, only=None):
    columns = pl.ds(first, cols)
    total = partial[...]
    for part, (side, pair, a, b, left, right, at) in enumerate(rim_parts(rows_blk)):
        if only not in (None, side):
            continue
        halo = slice(at * width, (at + right - left) * width)
        product = jnp.dot(
            banded[pair, a * width : b * width, left * width : right * width],
            evens[halo] if only is not None else pick(odd, side, (evens, odds), halo),
            preferred_element_type=F32,
        )
        here = pl.ds((2 * pair + a) * width, (b - a) * width)
        result = begun[here, columns] + 2.0 * product
        keep(part, side, here, columns, result)
        total = total + fold(result * weights[here, columns])
    return total


def rim_kernel(first, cols, width, rows_blk, odd, _, banded, weights, odds_in, evens_in, begun, partial, *refs):
    upcoming, moments, evens, odds, rims = refs
    rim = rims.shape[1]
    rows = rows_blk * width

    def keep(part, side, here, columns, result):
        upcoming[here, columns] = result
        base = here.start - (0 if side == 0 else rows - rim)
        rims[side, base : base + here.size] = result.astype(BF16)

    moments[...] = rim_sums(
        first, cols, width, rows_blk, odd, banded, weights, evens_in, odds_in, begun, partial, keep
    )

    def take(targets):
        for side in range(2):
            targets[side][...] = rims[side]

    hand_out(odd, take, evens, odds)


def plain_rim_kernel(first, cols, width, rows_blk, odd, _, banded, weights, evens_in, odds_in, begun, partial, moments, rims):
    rim = rims.shape[1]

    def keep(part, side, here, columns, result):
        base = here.start - (0 if side == 0 else rows_blk * width - rim)
        rims[side, base : base + here.size] = result

    moments[...] = rim_sums(
        first, cols, width, rows_blk, odd, banded, weights, evens_in, odds_in, begun, partial, keep
    )


def last_side(which, bound, odd, banded, weights, halo, begun, partial, moments, held, done=None):
    for parity in range(2):
        side = parity if which else 1 - parity
        top = 0 if side == 0 else begun.shape[0] - held.shape[0]

        def keep(part, side, here, columns, result, top=top):
            held[here.start - top : here.start - top + here.size] = result

        @pl.when(odd[0] == parity)
        def _():
            moments[...] = rim_sums(
                *bound, odd, banded, weights, halo, None, begun, partial, keep, only=side
            )
            if done is not None:
                done(top)


def even_rim_kernel(first, cols, width, rows_blk, odd, _, banded, weights, halo, begun, partial, others, __, out, moments, held, sem, sems):
    rim = held.shape[0]
    copies = [
        pltpu.make_async_copy(
            others.at[side], out.at[pl.ds(start, rim), pl.ds(first - cols, cols)], sems.at[side]
        )
        for side, start in enumerate((0, rows_blk * width - rim))
    ]
    for copy in copies:
        copy.start()

    def done(top):
        copy = pltpu.make_async_copy(held, out.at[pl.ds(top, rim), pl.ds(first, cols)], sem)
        copy.start()
        copy.wait()

    bound = (first, cols, width, rows_blk)
    last_side(0, bound, odd, banded, weights, halo, begun, partial, moments, held, done)
    for copy in copies:
        copy.wait()


def odd_rim_kernel(first, cols, width, rows_blk, odd, _, banded, weights, halo, begun, partial, *refs):
    *earlier, moments, held, total = refs
    bound = (first, cols, width, rows_blk)
    last_side(1, bound, odd, banded, weights, halo, begun, partial, total, held)
    parts = [jnp.sum(one[...], axis=0, keepdims=True) for one in [*earlier, total]]
    row = jnp.concatenate(parts, axis=1)
    for slab in range(moments.shape[0]):
        moments[slab] = row


def store_kernel(rim, _, previous, current, out_previous, out_current, sems):
    inside = pl.ds(rim, current.shape[0] - 2 * rim)
    copies = [
        pltpu.make_async_copy(previous, out_previous, sems.at[0]),
        pltpu.make_async_copy(current.at[inside], out_current.at[inside], sems.at[1]),
    ]
    for copy in copies:
        copy.start()
    for copy in copies:
        copy.wait()


def sum_kernel(first, odd, parts, rims, _, out, out_current, held, sems):
    rim, cols = rims.shape
    top = pl.multiple_of(odd[0] * (out_current.shape[0] - rim), rim // BAND)
    copies = [
        pltpu.make_async_copy(rims, out_current.at[pl.ds(top, rim), pl.ds(first, cols)], sems.at[0])
    ]
    copies[0].start()
    total = jnp.sum(parts[...], axis=0)
    every = held.shape[1]
    for term in range(held.shape[0]):
        held[term : term + 1] = total[:, term * every : (term + 1) * every]
    copies.append(pltpu.make_async_copy(held, out, sems.at[1]))
    copies[-1].start()
    for copy in copies:
        copy.wait()


def in_hbm(x):
    return pltpu.with_memory_space_constraint(x, pltpu.HBM)


def local(hamiltonian_blocks, block_columns, probe, previous, current, orbital_weight):
    rows_blk, slots, width, _ = hamiltonian_blocks.shape
    rows, all_cols = current.shape
    cols = all_cols // CHUNKS
    rim = BAND * width
    slabs = lax.axis_size("slab")
    total_blocks = rows_blk * slabs
    odd = lax.axis_index("slab")[None] & 1
    pairs_of = [[(i, i ^ 1) for i in range(slabs)]]
    pairs_of.append([((i + 1) % slabs, (k + 1) % slabs) for i, k in pairs_of[0]])
    shape = jax.ShapeDtypeStruct
    edge_shape = shape((rim, cols), BF16)
    full_shape = shape((rows, all_cols), F32)
    part_shape = shape((8, cols), F32)
    flops = 2 * rows * cols * 9 * width

    def exchange(evens, odds):
        return lax.ppermute(evens, "slab", pairs_of[0]), lax.ppermute(odds, "slab", pairs_of[1])

    def middle(token, term, chunk):
        args = [odd, token, banded, weights, *sources[chunk], terms[term]]
        aliases = {}
        if chunk:
            aliases = {len(args): 0}
            args.append(terms[term + 2])
        outs = (full_shape, shape((rows - 2 * rim, cols), BF16), part_shape)
        if term == TERMS - 1:
            outs = (full_shape, part_shape)
        return pl.pallas_call(
            functools.partial(
                middle_kernel, len(sources[chunk]), chunk * cols, cols, width, rows_blk
            ),
            out_shape=outs,
            in_specs=[SMEM] + [VMEM] * (len(args) - 1),
            out_specs=(VMEM,) * len(outs),
            scratch_shapes=[pltpu.VMEM((rows, cols), BF16)],
            input_output_aliases=aliases,
            compiler_params=params(),
            cost_estimate=cost(flops, 8 * 1024 * 1024),
            name="middle",
        )(*args)

    def rims(token, term, chunk):
        args = [odd, token, banded, weights, *halos[chunk], terms[term + 2], begun[chunk][-1]]
        specs = [SMEM] + [VMEM] * (len(args) - 1)
        bound = (chunk * cols, cols, width, rows_blk)
        if term < TERMS - 1:
            args[4], args[5] = args[5], args[4]
            kernel = functools.partial(rim_kernel, *bound)
            outs = (full_shape, part_shape, edge_shape, edge_shape)
            out_specs = (VMEM,) * 4
            scratch = [pltpu.VMEM((2, rim, cols), BF16)]
            aliases = {6: 0}
        else:
            kernel = functools.partial(plain_rim_kernel, *bound)
            outs = (part_shape, shape((2, rim, cols), F32))
            out_specs = (VMEM, VMEM)
            scratch = []
            aliases = {}
        return pl.pallas_call(
            kernel,
            out_shape=outs,
            in_specs=specs,
            out_specs=out_specs,
            scratch_shapes=scratch,
            input_output_aliases=aliases,
            compiler_params=params(),
            cost_estimate=cost(flops // 5, 2 * 1024 * 1024),
            name="rims",
        )(*args)

    first_row = lax.axis_index("slab") * rows_blk
    own_row = first_row + jnp.arange(rows_blk, dtype=jnp.int32)[:, None]
    places = (block_columns - own_row + BAND + total_blocks) % total_blocks
    pairs = rows_blk // 2

    rim_scratch = [pltpu.VMEM((2, rim, cols), F32), pltpu.SemaphoreType.DMA((2, BAND))]
    opening = pl.pallas_call(
        functools.partial(edge_kernel, 0, cols),
        out_shape=(edge_shape, edge_shape),
        in_specs=[SMEM, HBM],
        out_specs=(VMEM, VMEM),
        scratch_shapes=rim_scratch,
        compiler_params=params(),
        cost_estimate=cost(0, 6 * 2 * rim * cols),
        name="edges",
    )(odd, in_hbm(current))
    halos = [exchange(*opening)]
    banded, *opening = pl.pallas_call(
        functools.partial(band_kernel, cols, cols),
        out_shape=(
            shape((pairs, 2 * width, (2 * BAND + 2) * width), BF16),
            edge_shape,
            edge_shape,
        ),
        in_specs=[SMEM, VMEM, SMEM, HBM, HBM],
        out_specs=(VMEM,) * 3,
        scratch_shapes=[
            pltpu.SemaphoreType.DMA((pairs,)),
            *rim_scratch,
        ],
        compiler_params=params(),
        cost_estimate=cost(0, 12 * 1024 * 1024),
        name="band",
    )(odd, opening[1], places, in_hbm(hamiltonian_blocks), in_hbm(current))
    halos.append(exchange(*opening))
    weights = pl.pallas_call(
        functools.partial(weight_kernel, 1.0 / (total_blocks * width)),
        out_shape=full_shape,
        in_specs=[VMEM] * 3,
        out_specs=VMEM,
        compiler_params=params(),
        cost_estimate=cost(0, 4 * 1024 * 1024),
        name="weights",
    )(opening[1], orbital_weight.reshape(rows_blk, width), probe)

    terms = [previous, current] + [None] * TERMS
    sources = [(current,)] * CHUNKS
    begun = [None] * CHUNKS
    sums = []
    order = [(term, chunk) for term in range(TERMS) for chunk in range(CHUNKS)]
    ahead = len(order) - CHUNKS
    outputs = None

    def begin(token, term, chunk):
        terms[term + 2], *begun[chunk] = middle(token, term, chunk)
        return begun[chunk][-1]

    token = begin(weights, *order[0])
    for step, (term, chunk) in enumerate(order):
        if step < ahead:
            terms[term + 2], token, *sent = rims(token, term, chunk)
            halos[chunk] = exchange(*sent)
            sources[chunk] = (sent[0], begun[chunk][0], sent[1])
        elif step + 1 < len(order):
            token, others = rims(token, term, chunk)
        else:
            break
        sums.append(token)
        if step + 1 < ahead:
            token = begin(token, *order[step + 1])
        elif step + 1 == ahead:
            for item in order[ahead:]:
                token = begin(token, *item)
            outputs = pl.pallas_call(
                functools.partial(store_kernel, rim),
                out_shape=(full_shape, full_shape),
                in_specs=[VMEM] * 3,
                out_specs=(HBM, HBM),
                scratch_shapes=[pltpu.SemaphoreType.DMA((2,))],
                compiler_params=params(),
                cost_estimate=cost(0, 16 * 1024 * 1024),
                name="store",
            )(token, terms[-2], terms[-1])
    bound = (chunk * cols, cols, width, rows_blk)
    args = [odd, token, banded, weights, halos[chunk][0], terms[-1], begun[chunk][-1], others, outputs[1]]
    last_current, token = pl.pallas_call(
        functools.partial(even_rim_kernel, *bound),
        out_shape=(full_shape, part_shape),
        in_specs=[SMEM] + [VMEM] * 7 + [HBM],
        out_specs=(HBM, VMEM),
        scratch_shapes=[
            pltpu.VMEM((rim, cols), F32),
            pltpu.SemaphoreType.DMA,
            pltpu.SemaphoreType.DMA((2,)),
        ],
        input_output_aliases={8: 0},
        compiler_params=params(),
        cost_estimate=cost(flops // 10, 1024 * 1024),
        name="even_rims",
    )(*args)
    args = [odd, token, banded, weights, halos[chunk][1], terms[-1], token, *sums]
    scattered, ends = pl.pallas_call(
        functools.partial(odd_rim_kernel, *bound),
        out_shape=(shape((slabs, 1, TERMS * all_cols), F32), shape((rim, cols), F32)),
        in_specs=[SMEM] + [VMEM] * (len(args) - 1),
        out_specs=(VMEM, VMEM),
        scratch_shapes=[pltpu.VMEM(part_shape.shape, F32)],
        compiler_params=params(),
        cost_estimate=cost(flops // 10, 1024 * 1024),
        name="odd_rims",
    )(*args)
    gathered = lax.all_to_all(scattered, "slab", 0, 0)
    moments_shape = shape((TERMS, all_cols), F32)
    moments, last_current = pl.pallas_call(
        functools.partial(sum_kernel, all_cols - cols),
        out_shape=(moments_shape, full_shape),
        in_specs=[SMEM, VMEM, VMEM, HBM],
        out_specs=(HBM, HBM),
        scratch_shapes=[pltpu.VMEM(moments_shape.shape, F32), pltpu.SemaphoreType.DMA((2,))],
        input_output_aliases={3: 1},
        compiler_params=params(),
        name="sums",
    )(odd, gathered, ends, last_current)
    return outputs[0], last_current, moments


def solution(mesh):
    return jax.shard_map(
        local,
        mesh=mesh,
        in_specs=(
            P("slab", None, None, None),
            P("slab", None),
            P("slab", "col"),
            P("slab", "col"),
            P("slab", "col"),
            P("slab"),
        ),
        out_specs=(P("slab", "col"), P("slab", "col"), P(None, "col")),
        check_vma=False,
    )
```
